32 devices in a mesh: lat: 4 (over z), lon: 2 (over core), ens: 4 (over y, x).
Axes of the slice: x: 2, y: 2, z: 4, core: 2. Of those that a mesh axis runs over, the one named last changes fastest.
Arguments:
- fields: bfloat16 [128, 256, 256], P(('ens', 'lat'), 'lon'), parts along dimension 0, may hold values from -6 to 6
- lon_taps: float32 [32, 4, 9], replicated, may hold values from -2 to 2
- lat_taps: bfloat16 [32, 4, 6], P('lat'), may hold values from -2.5 to 2.5
- cycle_taps: bfloat16 [4, 8, 256], replicated, may hold values from -0.375 to 0.375
- band_start: int32 [32], P('lat'), may hold values from -4 to 30, as said below
- band_width: int32 [32], P('lat'), may hold values from 4 to 6, as said below
- mixing: bfloat16 [4, 256, 256], replicated, may hold values from -0.1875 to 0.1875
Outputs:
- layer_out: bfloat16 [128, 256, 256], P(('ens', 'lat'), 'lon'), parts along dimension 0
The draws below stay inside these ranges and needn't reach their ends.
There are 4 independent parts, one for each index of `ens`. The reference program is written for one: setup_inputs(seed, part) draws one part's arguments, and reference() takes and returns one part's arrays. A program takes and returns all parts, laid end to end along the dimension named above; an argument that names none is the same for every part. Nothing has to cross between parts.
Inputs may be any that keep to these rules, and one draw needn't show every extreme that they name: band_start[i] = i - 4 + s with s in 0 .. 3; s = 0 where i % 8 == 0 and s = 3 where i % 8 == 7. band_width[i] = 6 where i % 8 is 0 or 7.
All inputs are finite; a program needn't handle non-finite values.
Results may differ from the reference program's by a relative error of at most 0.0052.
Values may be sent and summed in bfloat16 or wider, within the bound.
No kernel may reach another device: no remote copies, remote signals or barrier semaphores. Data moves between devices by JAX's collectives and lax.ppermute only.
A program may use at most 64 MiB of HBM per device.

```python
import jax
import jax.numpy as jnp
from jax import lax

CHAN = 256
BASIS = 4
REACH = 4
BAND = 6
HALO = 4
LAT_DEV = 8
POLAR = 4
NLAT = 32
NLON = 256


def draw_band_start(key, part):
    rows_all = jnp.arange(NLAT, dtype=jnp.int32)
    top_shift = 2 * HALO - BAND + 1
    shift = jax.random.randint(jax.random.fold_in(key, 11), (NLAT,), 0, top_shift + 1, dtype=jnp.int32)
    inside = rows_all % LAT_DEV
    shift = jnp.where(inside == 0, 0, jnp.where(inside == LAT_DEV - 1, top_shift, shift))
    return (rows_all - HALO + shift).astype(jnp.int32)


def draw_band_width(key, part):
    rows_all = jnp.arange(NLAT, dtype=jnp.int32)
    widths = jax.random.randint(jax.random.fold_in(key, 23), (NLAT,), BAND - 2, BAND + 1, dtype=jnp.int32)
    inside = rows_all % LAT_DEV
    edge = (inside == 0) | (inside == LAT_DEV - 1)
    return jnp.where(edge, BAND, widths).astype(jnp.int32)


def steps_of(stream_key, shape, pieces, smallest, high):
    factor_of, own = 1.0, jax.random.fold_in(stream_key, 6)
    for dim, blocks in pieces:
        steps = jnp.exp(jax.random.uniform(jax.random.fold_in(own, dim), (blocks,), jnp.float32, smallest / len(pieces), high / len(pieces)))
        factor_of = factor_of * jnp.repeat(steps, shape[dim] // blocks).reshape([-1 if axis == dim else 1 for axis in range(len(shape))])
    return factor_of


def gaussian(rng, shape, scale, bound, split=(), kind=jnp.bfloat16):
    values = jax.random.normal(rng, shape, jnp.float32) * scale
    if len(split) > 0:
        values = steps_of(rng, shape, split, -0.22, 0.18) * values
    return jnp.clip(values, min=-bound, max=bound).astype(kind)


def setup_inputs(seed: int = 0, part: int = 0) -> dict:
    splits = jax.random.split(jax.random.key(seed), 8)
    part_keys = jax.random.split(jax.random.fold_in(splits[7], part), 8)
    fields = gaussian(part_keys[0], (NLAT, NLON, CHAN), 1.0, 6.0, ((0, 4), (1, 2)))
    lon_taps = gaussian(splits[1], (NLAT, BASIS, 2 * REACH + 1), 0.35, 2.0, (), jnp.float32)
    lat_taps = gaussian(splits[2], (NLAT, BASIS, BAND), 0.45, 2.5, ((0, 4),))
    cycle_taps = gaussian(splits[3], (BASIS, 2 * POLAR, NLON), NLON ** -0.5, 0.375)
    band_start = draw_band_start(jax.random.fold_in(splits[7], 71), part)
    band_width = draw_band_width(jax.random.fold_in(splits[7], 71), part)
    mixing = gaussian(splits[6], (BASIS, CHAN, CHAN), (BASIS * CHAN) ** -0.5, 0.1875)
    return {"fields": fields, "lon_taps": lon_taps, "lat_taps": lat_taps, "cycle_taps": cycle_taps, "band_start": band_start, "band_width": band_width, "mixing": mixing}


def short_filter(fields, taps_now):
    total = jnp.zeros(fields.shape, jnp.float32)
    for offset in range(2 * REACH + 1):
        moved = jnp.roll(fields, REACH - offset, axis=1).astype(jnp.float32)
        total = total + taps_now[:, offset][:, None, None] * moved
    return total


def reference(fields, lon_taps, lat_taps, cycle_taps, band_start, band_width, mixing):
    columns = jnp.arange(NLON, dtype=jnp.int32)
    lag_table = (columns[:, None] - columns[None, :]) % NLON
    polar_ids = [p for p in range(POLAR)] + [NLAT - POLAR + p for p in range(POLAR)]

    def per_basis(mixed, inputs):
        lon_now, lat_now, cycle_now, mix_now = inputs
        filtered = short_filter(fields, lon_now).astype(jnp.bfloat16)
        for index in range(2 * POLAR):
            row_id = polar_ids[index]
            circ = cycle_now[index][lag_table]
            cycle_row = jnp.dot(circ, fields[row_id], preferred_element_type=jnp.float32)
            filtered = filtered.at[row_id].set(cycle_row.astype(jnp.bfloat16))
        hidden = jnp.zeros(fields.shape, jnp.float32)
        for step_t in range(BAND):
            source = band_start + step_t
            usable = (step_t < band_width) & (source >= 0) & (source < NLAT)
            picked = filtered[jnp.clip(source, 0, NLAT - 1).astype(jnp.int32)].astype(jnp.float32)
            weight = jnp.where(usable, lat_now[:, step_t].astype(jnp.float32), jnp.zeros((NLAT,), jnp.float32))
            hidden = hidden + weight[:, None, None] * picked
        hidden = hidden.astype(jnp.bfloat16)
        mixed = mixed + jnp.dot(hidden.reshape(NLAT * NLON, CHAN), mix_now, preferred_element_type=jnp.float32)
        return mixed, None

    start_sum = jnp.zeros((NLAT * NLON, CHAN), jnp.float32)
    inputs = (jnp.moveaxis(lon_taps, 1, 0), jnp.moveaxis(lat_taps, 1, 0), cycle_taps, mixing)
    mixed, unused = lax.scan(per_basis, start_sum, inputs)
    result = fields.astype(jnp.float32) + mixed.reshape(NLAT, NLON, CHAN)
    return result.astype(jnp.bfloat16)
```

```python
import functools

import jax
import jax.numpy as jnp
from jax import lax
from jax.experimental import pallas as pl
from jax.experimental.pallas import tpu as pltpu
from jax.sharding import PartitionSpec as P

HALO = 4
SWAP = [(0, 1), (1, 0)]


def ring(lat_count, step):
    pairs = []
    for lat in range(lat_count):
        for core in range(2):
            to = lat + (step if core == 0 else -step)
            if 0 <= to < lat_count:
                pairs.append((lat * 2 + core, to * 2 + core))
            else:
                pairs.append((lat * 2 + core, lat * 2 + 1 - core))
    return pairs


def circulants(h, out_ref, basis):
    cycle = h.shape[1]
    count = out_ref.shape[0] // basis
    for k in range(basis):
        wide = jnp.broadcast_to(h[k : k + 1], (count, cycle))
        turned = pltpu.roll(wide, 0, 1, stride=1, stride_axis=0)
        out_ref[k * count : (k + 1) * count, :] = turned.astype(jnp.bfloat16)
    return None


def own_kernel(
    lat_taps, band_start, band_width, fields, other, lon_taps, cycle_taps, mixing,
    acc, halo_mats, lag, flipped, mats, filt, hidden,
):
    rows, cols, chans = fields.shape
    basis, taps = lon_taps.shape[1:]
    reach = taps // 2
    band = lat_taps.shape[2]
    cycle = cycle_taps.shape[2]
    half = rows // 2
    lat_pos = lax.axis_index("lat")
    lat_count = lax.axis_size("lat")
    base = lat_pos * rows
    row_total = lat_count * rows

    lag[...] = jnp.zeros_like(lag)
    for slot in range(rows + 2 * HALO):
        row = jnp.clip(base - HALO + slot, 0, row_total - 1)
        lag[slot, :, 0:taps] = lon_taps[row]
    lags = pltpu.roll(lag[...].reshape(-1, cycle), cycle - reach, 1)
    lag[...] = lags.reshape(lag.shape)

    ids = lax.broadcasted_iota(jnp.int32, (cycle, cycle), 0) + lax.broadcasted_iota(
        jnp.int32, (cycle, cycle), 1
    )
    turn = jnp.where((ids == 0) | (ids == cycle), 1.0, 0.0).astype(jnp.bfloat16)
    flat = cycle_taps[...].reshape(basis * rows, cycle)
    flipped[...] = jnp.dot(flat, turn, preferred_element_type=jnp.float32).reshape(flipped.shape)
    for r in range(rows):
        polar = (lat_pos == 0) if r < half else (lat_pos == lat_count - 1)
        lag[HALO + r] = jnp.where(polar, flipped[:, r, :], lag[HALO + r])

    def halo_step(s, carry):
        circulants(lag[jnp.where(s < HALO, s, s + rows)], halo_mats.at[s], basis)
        return carry

    def own_step(r, carry):
        circulants(lag[HALO + r], mats, basis)
        cells = jnp.concatenate([fields[r], other[r]], axis=0)
        filt[r] = jnp.dot(mats[...], cells, preferred_element_type=jnp.float32)
        return carry

    lax.fori_loop(0, rows, own_step, 0)

    def band_step(n, carry):
        i = n // basis
        k = n % basis
        first = band_start[i]
        width = band_width[i]
        chunk = 32
        sums = [jnp.zeros((chunk, chans), jnp.float32) for _ in range(cols // chunk)]
        for t in range(band):
            r = first + t - base
            used = (t < width) & (r >= 0) & (r < rows)
            weight = jnp.where(used, lat_taps[i, k, t], 0.0)
            source = jnp.clip(r, 0, rows - 1)
            for c in range(cols // chunk):
                at = pl.multiple_of(k * cols + c * chunk, chunk)
                sums[c] = sums[c] + weight * filt[source, pl.ds(at, chunk), :]
        for c in range(cols // chunk):
            at = pl.multiple_of(i * cols + c * chunk, chunk)
            hidden[k, pl.ds(at, chunk), :] = sums[c].astype(jnp.bfloat16)
        return carry

    lax.fori_loop(0, rows * basis, band_step, 0)
    total = fields[...].reshape(rows * cols, chans).astype(jnp.float32)
    for k in range(basis):
        total = total + jnp.dot(hidden[k], mixing[k], preferred_element_type=jnp.float32)
    acc[...] = total.reshape(acc.shape)
    lax.fori_loop(0, 2 * HALO, halo_step, 0)


def halo_kernel(
    lat_taps, band_start, band_width, first_in, second_in, edges, halo_mats, acc, mixing,
    out, cells, filt, hidden,
):
    rows, cols, chans = out.shape
    basis = mixing.shape[0]
    reach = edges.shape[1] // 2
    band = lat_taps.shape[2]
    cycle = 2 * cols
    lat_pos = lax.axis_index("lat")
    lat_count = lax.axis_size("lat")
    core = lax.axis_index("lon")
    base = lat_pos * rows
    row_total = lat_count * rows

    is_first = core == 0
    zeros = jnp.zeros((cycle - cols - 2 * reach, chans), jnp.bfloat16)
    for s in range(2 * HALO):
        p = s % HALO
        mine, his = (first_in, second_in) if s < HALO else (second_in, first_in)
        a, b = (p + HALO, p) if s < HALO else (p, p + HALO)
        body = jnp.where(is_first, mine[p], his[p])
        edge = jnp.where(is_first, edges[a], edges[b])
        cells[s] = jnp.concatenate([body, edge[:reach], zeros, edge[reach:]], axis=0)

    def filter_step(s, carry):
        filt[s] = jnp.dot(halo_mats[s], cells[s], preferred_element_type=jnp.float32)
        return carry

    lax.fori_loop(0, 2 * HALO, filter_step, 0)

    chunk = 32

    def band_step(k, carry):
        for i in range(rows):
            slots = range(i, HALO) if i < HALO else range(HALO, i + 1)
            weights = []
            for s in slots:
                row = base - HALO + s + (0 if s < HALO else rows)
                t = row - band_start[i]
                used = (t >= 0) & (t < band_width[i]) & (row >= 0) & (row < row_total)
                weights.append(jnp.where(used, lat_taps[i, k, jnp.clip(t, 0, band - 1)], 0.0))
            for c in range(cols // chunk):
                at = pl.multiple_of(k * cols + c * chunk, chunk)
                total = None
                for s, weight in zip(slots, weights):
                    term = weight * filt[s, pl.ds(at, chunk), :]
                    total = term if total is None else total + term
                hidden[k, i * cols + c * chunk : i * cols + (c + 1) * chunk, :] = total.astype(
                    jnp.bfloat16
                )
        return carry

    lax.fori_loop(0, basis, band_step, 0)
    total = acc[...].reshape(rows * cols, chans)
    for k in range(basis):
        total = total + jnp.dot(hidden[k], mixing[k], preferred_element_type=jnp.float32)
    out[...] = total.reshape(out.shape).astype(out.dtype)


def shards(fields, lon_taps, lat_taps, cycle_taps, band_start, band_width, mixing):
    rows, cols, chans = fields.shape
    basis = lon_taps.shape[1]
    reach = (lon_taps.shape[2] - 1) // 2
    lat_count = lax.axis_size("lat")
    cycle = 2 * cols
    core = lax.axis_index("lon")
    axes = ("lat", "lon")
    other = lax.ppermute(fields, "lon", SWAP)
    head, tail = fields[:HALO], fields[rows - HALO :]
    first = lax.ppermute(jnp.where(core == 0, tail, head), axes, ring(lat_count, 1))
    second = lax.ppermute(jnp.where(core == 0, head, tail), axes, ring(lat_count, -1))

    weights = lat_taps.astype(jnp.float32)
    vmem = pl.BlockSpec(memory_space=pltpu.VMEM)
    smem = pl.BlockSpec(memory_space=pltpu.SMEM)
    f32, bf16 = jnp.float32, jnp.bfloat16
    acc, halo_mats = pl.pallas_call(
        own_kernel,
        out_shape=(
            jax.ShapeDtypeStruct((rows, cols, chans), f32),
            jax.ShapeDtypeStruct((2 * HALO, basis * cols, cycle), bf16),
        ),
        in_specs=[smem] * 3 + [vmem] * 5,
        out_specs=(vmem, vmem),
        scratch_shapes=[
            pltpu.VMEM((rows + 2 * HALO, basis, cycle), f32),
            pltpu.VMEM((basis, rows, cycle), f32),
            pltpu.VMEM((basis * cols, cycle), bf16),
            pltpu.VMEM((rows, basis * cols, chans), f32),
            pltpu.VMEM((basis, rows * cols, chans), bf16),
        ],
        compiler_params=pltpu.CompilerParams(vmem_limit_bytes=32 * 1024 * 1024),
        cost_estimate=pl.CostEstimate(
            flops=2_000_000_000, bytes_accessed=6_000_000, transcendentals=0
        ),
        name="own_rows",
    )(weights, band_start, band_width, fields, other, lon_taps, cycle_taps, mixing)

    arrived = jnp.concatenate([first, second], axis=0)
    edges = jnp.concatenate([arrived[:, :reach], arrived[:, cols - reach :]], axis=1)
    edges = lax.ppermute(edges, "lon", SWAP)
    return pl.pallas_call(
        halo_kernel,
        out_shape=jax.ShapeDtypeStruct((rows, cols, chans), bf16),
        in_specs=[smem] * 3 + [vmem] * 6,
        out_specs=vmem,
        scratch_shapes=[
            pltpu.VMEM((2 * HALO, cycle, chans), bf16),
            pltpu.VMEM((2 * HALO, basis * cols, chans), f32),
            pltpu.VMEM((basis, rows * cols, chans), bf16),
        ],
        compiler_params=pltpu.CompilerParams(vmem_limit_bytes=32 * 1024 * 1024),
        name="halo_rows",
    )(weights, band_start, band_width, first, second, edges, halo_mats, acc, mixing)


def solution(mesh):
    in_specs = (
        P(("ens", "lat"), "lon", None),
        P(),
        P("lat", None, None),
        P(),
        P("lat"),
        P("lat"),
        P(),
    )
    out_specs = P(("ens", "lat"), "lon", None)
    return jax.shard_map(shards, mesh=mesh, in_specs=in_specs, out_specs=out_specs, check_vma=False)
```

```python
import functools

import jax
import jax.numpy as jnp
from jax import lax
from jax.experimental import pallas as pl
from jax.experimental.pallas import tpu as pltpu
from jax.sharding import PartitionSpec as P

HALO = 4
SWAP = [(0, 1), (1, 0)]


def ring(lat_count, step):
    pairs = []
    for lat in range(lat_count):
        for core in range(2):
            to = lat + (step if core == 0 else -step)
            if 0 <= to < lat_count:
                pairs.append((lat * 2 + core, to * 2 + core))
            else:
                pairs.append((lat * 2 + core, lat * 2 + 1 - core))
    return pairs


def circulants(h, out_ref, basis):
    cycle = h.shape[1]
    count = out_ref.shape[0] // basis
    for k in range(basis):
        wide = jnp.broadcast_to(h[k : k + 1], (count, cycle))
        turned = pltpu.roll(wide, 0, 1, stride=1, stride_axis=0)
        out_ref[k * count : (k + 1) * count, :] = turned.astype(jnp.bfloat16)
    return None


def own_kernel(
    lat_taps, band_start, band_width, fields, other, lon_taps, cycle_taps, mixing,
    acc, halo_mats, lag, flipped, mats, filt, hidden,
):
    rows, cols, chans = fields.shape
    basis, taps = lon_taps.shape[1:]
    reach = taps // 2
    band = lat_taps.shape[2]
    cycle = cycle_taps.shape[2]
    half = rows // 2
    lat_pos = lax.axis_index("lat")
    lat_count = lax.axis_size("lat")
    base = lat_pos * rows
    row_total = lat_count * rows

    lag[...] = jnp.zeros_like(lag)
    for slot in range(rows + 2 * HALO):
        row = jnp.clip(base - HALO + slot, 0, row_total - 1)
        lag[slot, :, 0:taps] = lon_taps[row]
    lags = pltpu.roll(lag[...].reshape(-1, cycle), cycle - reach, 1)
    lag[...] = lags.reshape(lag.shape)

    ids = lax.broadcasted_iota(jnp.int32, (cycle, cycle), 0) + lax.broadcasted_iota(
        jnp.int32, (cycle, cycle), 1
    )
    turn = jnp.where((ids == 0) | (ids == cycle), 1.0, 0.0).astype(jnp.bfloat16)
    flat = cycle_taps[...].reshape(basis * rows, cycle)
    flipped[...] = jnp.dot(flat, turn, preferred_element_type=jnp.float32).reshape(flipped.shape)
    for r in range(rows):
        polar = (lat_pos == 0) if r < half else (lat_pos == lat_count - 1)
        lag[HALO + r] = jnp.where(polar, flipped[:, r, :], lag[HALO + r])

    def halo_step(s, carry):
        circulants(lag[jnp.where(s < HALO, s, s + rows)], halo_mats.at[s], basis)
        return carry

    def own_step(r, carry):
        circulants(lag[HALO + r], mats, basis)
        cells = jnp.concatenate([fields[r], other[r]], axis=0)
        filt[r] = jnp.dot(mats[...], cells, preferred_element_type=jnp.float32)
        return carry

    lax.fori_loop(0, rows, own_step, 0)

    def band_step(n, carry):
        i = n // basis
        k = n % basis
        first = band_start[i]
        width = band_width[i]
        chunk = 32
        sums = [jnp.zeros((chunk, chans), jnp.float32) for _ in range(cols // chunk)]
        for t in range(band):
            r = first + t - base
            used = (t < width) & (r >= 0) & (r < rows)
            weight = jnp.where(used, lat_taps[i, k, t], 0.0)
            source = jnp.clip(r, 0, rows - 1)
            for c in range(cols // chunk):
                at = pl.multiple_of(k * cols + c * chunk, chunk)
                sums[c] = sums[c] + weight * filt[source, pl.ds(at, chunk), :]
        for c in range(cols // chunk):
            at = pl.multiple_of(i * cols + c * chunk, chunk)
            hidden[k, pl.ds(at, chunk), :] = sums[c].astype(jnp.bfloat16)
        return carry

    lax.fori_loop(0, rows * basis, band_step, 0)
    total = fields[...].reshape(rows * cols, chans).astype(jnp.float32)
    for k in range(basis):
        total = total + jnp.dot(hidden[k], mixing[k], preferred_element_type=jnp.float32)
    acc[...] = total.reshape(acc.shape)
    lax.fori_loop(0, 2 * HALO, halo_step, 0)


def halo_kernel(
    lat_taps, band_start, band_width, first_in, second_in, edges, halo_mats, acc, mixing,
    out, cells, filt, hidden,
):
    rows, cols, chans = out.shape
    basis = mixing.shape[0]
    reach = edges.shape[1] // 2
    band = lat_taps.shape[2]
    cycle = 2 * cols
    lat_pos = lax.axis_index("lat")
    lat_count = lax.axis_size("lat")
    core = lax.axis_index("lon")
    base = lat_pos * rows
    row_total = lat_count * rows

    is_first = core == 0
    zeros = jnp.zeros((cycle - cols - 2 * reach, chans), jnp.bfloat16)
    for s in range(2 * HALO):
        p = s % HALO
        mine, his = (first_in, second_in) if s < HALO else (second_in, first_in)
        a, b = (p + HALO, p) if s < HALO else (p, p + HALO)
        body = jnp.where(is_first, mine[p], his[p])
        edge = jnp.where(is_first, edges[a], edges[b])
        cells[s] = jnp.concatenate([body, edge[:reach], zeros, edge[reach:]], axis=0)

    def filter_step(s, carry):
        filt[s] = jnp.dot(halo_mats[s], cells[s], preferred_element_type=jnp.float32)
        return carry

    lax.fori_loop(0, 2 * HALO, filter_step, 0)

    chunk = 32

    def band_step(k, carry):
        for i in range(rows):
            slots = range(i, HALO) if i < HALO else range(HALO, i + 1)
            weights = []
            for s in slots:
                row = base - HALO + s + (0 if s < HALO else rows)
                t = row - band_start[i]
                used = (t >= 0) & (t < band_width[i]) & (row >= 0) & (row < row_total)
                weights.append(jnp.where(used, lat_taps[i, k, jnp.clip(t, 0, band - 1)], 0.0))
            for c in range(cols // chunk):
                at = pl.multiple_of(k * cols + c * chunk, chunk)
                total = None
                for s, weight in zip(slots, weights):
                    term = weight * filt[s, pl.ds(at, chunk), :]
                    total = term if total is None else total + term
                hidden[k, i * cols + c * chunk : i * cols + (c + 1) * chunk, :] = total.astype(
                    jnp.bfloat16
                )
        return carry

    lax.fori_loop(0, basis, band_step, 0)
    total = acc[...].reshape(rows * cols, chans)
    for k in range(basis):
        total = total + jnp.dot(hidden[k], mixing[k], preferred_element_type=jnp.float32)
    out[...] = total.reshape(out.shape).astype(out.dtype)


def shards(fields, lon_taps, lat_taps, cycle_taps, band_start, band_width, mixing):
    rows, cols, chans = fields.shape
    basis = lon_taps.shape[1]
    reach = (lon_taps.shape[2] - 1) // 2
    lat_count = lax.axis_size("lat")
    cycle = 2 * cols
    core = lax.axis_index("lon")
    axes = ("lat", "lon")
    other = lax.ppermute(fields, "lon", SWAP)
    head, tail = fields[:HALO], fields[rows - HALO :]
    first = lax.ppermute(jnp.where(core == 0, tail, head), axes, ring(lat_count, 1))
    second = lax.ppermute(jnp.where(core == 0, head, tail), axes, ring(lat_count, -1))

    weights = lat_taps.astype(jnp.float32)
    vmem = pl.BlockSpec(memory_space=pltpu.VMEM)
    smem = pl.BlockSpec(memory_space=pltpu.SMEM)
    f32, bf16 = jnp.float32, jnp.bfloat16
    acc, halo_mats = pl.pallas_call(
        own_kernel,
        out_shape=(
            jax.ShapeDtypeStruct((rows, cols, chans), f32),
            jax.ShapeDtypeStruct((2 * HALO, basis * cols, cycle), bf16),
        ),
        in_specs=[smem] * 3 + [vmem] * 5,
        out_specs=(vmem, vmem),
        scratch_shapes=[
            pltpu.VMEM((rows + 2 * HALO, basis, cycle), f32),
            pltpu.VMEM((basis, rows, cycle), f32),
            pltpu.VMEM((basis * cols, cycle), bf16),
            pltpu.VMEM((rows, basis * cols, chans), f32),
            pltpu.VMEM((basis, rows * cols, chans), bf16),
        ],
        compiler_params=pltpu.CompilerParams(vmem_limit_bytes=32 * 1024 * 1024),
        cost_estimate=pl.CostEstimate(
            flops=2_000_000_000, bytes_accessed=6_000_000, transcendentals=0
        ),
        name="own_rows",
    )(weights, band_start, band_width, fields, other, lon_taps, cycle_taps, mixing)

    first, second, acc = lax.optimization_barrier((first, second, acc))
    arrived = jnp.concatenate([first, second], axis=0)
    edges = jnp.concatenate([arrived[:, :reach], arrived[:, cols - reach :]], axis=1)
    edges = lax.ppermute(edges, "lon", SWAP)
    return pl.pallas_call(
        halo_kernel,
        out_shape=jax.ShapeDtypeStruct((rows, cols, chans), bf16),
        in_specs=[smem] * 3 + [vmem] * 6,
        out_specs=vmem,
        scratch_shapes=[
            pltpu.VMEM((2 * HALO, cycle, chans), bf16),
            pltpu.VMEM((2 * HALO, basis * cols, chans), f32),
            pltpu.VMEM((basis, rows * cols, chans), bf16),
        ],
        compiler_params=pltpu.CompilerParams(vmem_limit_bytes=32 * 1024 * 1024),
        name="halo_rows",
    )(weights, band_start, band_width, first, second, edges, halo_mats, acc, mixing)


def solution(mesh):
    in_specs = (
        P(("ens", "lat"), "lon", None),
        P(),
        P("lat", None, None),
        P(),
        P("lat"),
        P("lat"),
        P(),
    )
    out_specs = P(("ens", "lat"), "lon", None)
    return jax.shard_map(shards, mesh=mesh, in_specs=in_specs, out_specs=out_specs, check_vma=False)
```

```python
import jax
import jax.numpy as jnp
from jax import lax
from jax.experimental import pallas as pl
from jax.experimental.pallas import tpu as pltpu
from jax.sharding import PartitionSpec as P

HALO = 4
BLOCK = 16
SPAN = 32
SWAP = [(0, 1), (1, 0)]
F32, BF16 = jnp.float32, jnp.bfloat16


def ring(lat_count, step):
    pairs = []
    for lat in range(lat_count):
        for core in range(2):
            to = lat + (step if core == 0 else -step)
            if 0 <= to < lat_count:
                pairs.append((lat * 2 + core, to * 2 + core))
            else:
                pairs.append((lat * 2 + core, lat * 2 + 1 - core))
    return pairs


def matmul(a, b):
    return jnp.dot(a, b, preferred_element_type=F32)


def staircase(line, steps):
    wide = jnp.broadcast_to(line, (steps, line.shape[1]))
    return pltpu.roll(wide, 0, 1, stride=1, stride_axis=0).astype(BF16)


def chosen(terms):
    total = None
    for mask, value in terms:
        term = jnp.where(mask, value, 0.0)
        total = term if total is None else total + term
    return total


def window_products(weights, ext, hidden, blocks, rows, basis, cols, chans):
    for b in blocks:
        cells = ext[:, BLOCK * b : BLOCK * b + SPAN, :].reshape(-1, chans)
        part = matmul(weights[...], cells).astype(BF16)
        for k in range(basis):
            for i in range(rows):
                at = (k * rows + i) * BLOCK
                hidden[
                    i * cols + BLOCK * b : i * cols + BLOCK * (b + 1),
                    k * chans : (k + 1) * chans,
                ] = part[at : at + BLOCK]


def own_kernel(
    start_in, width_in, lon_in, lat_in, fields_in, cycle_in, mixing_in, other,
    acc, halo_weights, mix,
    start, width, lon, lat, fields, cycle_taps, lon_wide, lat_wide, own_weights, ext, hidden,
    turned, cycle_rows, mixed_rows, sems,
):
    rows, cols, chans = fields.shape
    taps, basis, row_total = lon.shape
    band = lat.shape[0]
    reach = taps // 2
    polar = cycle_taps.shape[1] // 2
    cycle = cycle_taps.shape[2]
    lat_pos = lax.axis_index("lat")
    base = lat_pos * rows
    at_top = base == 0
    at_bottom = base == row_total - rows

    copies = []
    for n, (source, target) in enumerate(
        [
            (lon_in, lon), (lat_in, lat), (start_in, start), (width_in, width),
            (fields_in, fields), (cycle_in, cycle_taps), (mixing_in, mix),
        ]
    ):
        copies.append(pltpu.make_async_copy(source, target, sems.at[n]))
        copies[-1].start()
    lon_wide[...] = jnp.zeros_like(lon_wide)
    lat_wide[...] = jnp.zeros_like(lat_wide)
    for n in range(4):
        copies[n].wait()

    for d in range(taps):
        for k in range(basis):
            lon_wide[k * 16 + d : k * 16 + d + 1, 0:row_total] = lon[d, k : k + 1, :]
    lanes = lon_wide.shape[1]
    slots = pltpu.roll(lon_wide[...], lax.rem(lanes + HALO - base, lanes), 1)[:, :128]
    slots = jnp.transpose(slots)[: rows + 2 * HALO]
    is_tap = lax.broadcasted_iota(jnp.int32, slots.shape, 1) < taps
    own_taps, halo_taps = [], []
    for k in range(basis):
        moved = slots if k == 0 else pltpu.roll(slots, 128 - 16 * k, 1)
        moved = jnp.where(is_tap, moved, 0.0)
        for _ in range(2):
            moved = pltpu.roll(moved, 0, 1, stride=SPAN // 2, stride_axis=0)
        quads = [jnp.sum(moved[4 * q : 4 * q + 4], axis=0, keepdims=True) for q in range(4)]
        own_taps.append(jnp.concatenate([quads[1], quads[2]], axis=1))
        halo_taps.append(jnp.concatenate([quads[0], quads[3]], axis=1))

    for t in range(band):
        lat_wide[t * basis : (t + 1) * basis, 0:rows] = lat[t].astype(F32)
    lat_cols = jnp.transpose(lat_wide[...])[:rows]
    shape = (rows, rows * SPAN)
    lane = lax.broadcasted_iota(jnp.int32, shape, 1)
    out_row = lax.broadcasted_iota(jnp.int32, shape, 0)
    first = jnp.zeros(shape, jnp.int32)
    count = jnp.zeros(shape, jnp.int32)
    for i in range(rows):
        first = jnp.where(out_row == i, start[i], first)
        count = jnp.where(out_row == i, width[i], count)
    spread = [
        [
            jnp.broadcast_to(lat_cols[:, t * basis + k : t * basis + k + 1], shape)
            for k in range(basis)
        ]
        for t in range(band)
    ]
    slot = lane // SPAN
    own_row = base + slot
    halo_row = jnp.where(slot < HALO, own_row - HALO, own_row + rows - HALO)
    is_polar = (own_row < polar) | (own_row >= row_total - polar)
    in_grid = (halo_row >= 0) & (halo_row < row_total)
    own_step, halo_step = own_row - first, halo_row - first
    own_used = [(own_step == t) & (count > t) & ~is_polar for t in range(band)]
    halo_used = [(halo_step == t) & (count > t) & in_grid for t in range(band)]
    for k in range(basis):
        own_line = own_taps[k] * chosen([(own_used[t], spread[t][k]) for t in range(band)])
        halo_line = halo_taps[k] * chosen([(halo_used[t], spread[t][k]) for t in range(band)])
        for i in range(rows):
            at = (k * rows + i) * BLOCK
            own_weights[at : at + BLOCK, :] = staircase(own_line[i : i + 1], BLOCK)
            halo_weights[at : at + BLOCK, :] = staircase(halo_line[i : i + 1], BLOCK)

    copies[4].wait()
    pad = jnp.zeros((ext.shape[1] - cols - 2 * reach, chans), BF16)
    for r in range(rows):
        ext[r] = jnp.concatenate(
            [other[r, cols - reach :], fields[r], other[r, :reach], pad], axis=0
        )
    window_products(
        own_weights, ext, hidden, range(cols // BLOCK), rows, basis, cols, chans
    )
    copies[5].wait()
    copies[6].wait()
    half = rows // 2
    for n in range(2):
        total = matmul(hidden[n * half * cols : (n + 1) * half * cols], mix[...])
        acc[n * half : (n + 1) * half] = (
            total.reshape(half, cols, chans)
            + fields[n * half : (n + 1) * half].astype(F32)
        )

    @pl.when(at_top | at_bottom)
    def polar_part():
        offset = jnp.where(at_top, 0, rows - polar)
        total = lax.broadcasted_iota(jnp.int32, (cycle, cycle), 0) + lax.broadcasted_iota(
            jnp.int32, (cycle, cycle), 1
        )
        turn = jnp.where((total == 0) | (total == cycle), 1.0, 0.0).astype(BF16)
        negated = matmul(cycle_taps[...].reshape(-1, cycle), turn)
        for p in range(polar):
            for k in range(basis):
                n = k * 2 * polar + p
                line = jnp.where(at_top, negated[n : n + 1], negated[n + polar : n + polar + 1])
                turned[p, k * cols : (k + 1) * cols, :] = staircase(line, cols)
        for p in range(polar):
            whole = jnp.concatenate([fields[offset + p], other[offset + p]], axis=0)
            part = matmul(turned[p], whole).astype(BF16)
            for k in range(basis):
                cycle_rows[k, p * cols : (p + 1) * cols, :] = part[k * cols : (k + 1) * cols]
        for k in range(basis):
            part = matmul(cycle_rows[k], mix[k * chans : (k + 1) * chans, :]).astype(BF16)
            mixed_rows[k * polar : (k + 1) * polar] = part.reshape(polar, cols, chans)
        of_basis = lane // (polar * BLOCK)
        step = base + offset + lax.rem(lane // BLOCK, polar) - first
        at_start = lax.rem(lane, BLOCK) == 0
        terms = []
        for t in range(band):
            value = spread[t][0]
            for k in range(1, basis):
                value = jnp.where(of_basis == k, spread[t][k], value)
            terms.append(((step == t) & (count > t) & at_start, value))
        line = chosen(terms)
        weights = jnp.concatenate(
            [staircase(line[i : i + 1], BLOCK) for i in range(rows)], axis=0
        )
        for b in range(cols // BLOCK):
            at = slice(BLOCK * b, BLOCK * (b + 1))
            cells = mixed_rows[:, at, :].reshape(-1, chans)
            acc[:, at, :] = acc[:, at, :] + matmul(weights, cells).reshape(rows, BLOCK, chans)


def halo_kernel(first_in, second_in, edges, weights, acc, mix, out, ext, hidden):
    rows, cols, chans = out.shape
    basis = mix.shape[0] // chans
    reach = edges.shape[1] // 2
    is_first = lax.axis_index("lon") == 0
    pad = jnp.zeros((ext.shape[1] - cols - 2 * reach, chans), BF16)
    for s in range(2 * HALO):
        p = s % HALO
        mine, his = (first_in, second_in) if s < HALO else (second_in, first_in)
        a, b = (p + HALO, p) if s < HALO else (p, p + HALO)
        body = jnp.where(is_first, mine[p], his[p])
        edge = jnp.where(is_first, edges[a], edges[b])
        ext[s] = jnp.concatenate([edge[reach:], body, edge[:reach], pad], axis=0)
    window_products(weights, ext, hidden, range(cols // BLOCK), rows, basis, cols, chans)
    half = rows // 2
    for n in range(2):
        total = matmul(hidden[n * half * cols : (n + 1) * half * cols], mix[...])
        at = slice(n * half, (n + 1) * half)
        out[at] = (total.reshape(half, cols, chans) + acc[at]).astype(BF16)


def shards(fields, lon_taps, lat_taps, cycle_taps, band_start, band_width, mixing):
    rows, cols, chans = fields.shape
    row_total, basis, taps = lon_taps.shape
    band = lat_taps.shape[2]
    reach = (taps - 1) // 2
    polar = cycle_taps.shape[1] // 2
    cycle = cycle_taps.shape[2]
    lat_count = lax.axis_size("lat")
    core = lax.axis_index("lon")
    axes = ("lat", "lon")
    assert cycle == 2 * cols and rows == 2 * HALO and basis * polar * BLOCK == rows * SPAN
    other = lax.ppermute(fields, "lon", SWAP)
    head, tail = fields[:HALO], fields[rows - HALO :]
    first = lax.ppermute(jnp.where(core == 0, tail, head), axes, ring(lat_count, 1))
    second = lax.ppermute(jnp.where(core == 0, head, tail), axes, ring(lat_count, -1))

    vmem = pl.BlockSpec(memory_space=pltpu.VMEM)
    hbm = pl.BlockSpec(memory_space=pltpu.HBM)
    sds = jax.ShapeDtypeStruct
    group = basis * rows * BLOCK
    ext_cols = cols + SPAN - BLOCK
    acc, halo_weights, mix = pl.pallas_call(
        own_kernel,
        out_shape=(
            sds((rows, cols, chans), F32),
            sds((group, rows * SPAN), BF16),
            sds((basis * chans, chans), BF16),
        ),
        in_specs=[hbm] * 7 + [vmem],
        out_specs=(vmem, vmem, vmem),
        scratch_shapes=[
            pltpu.SMEM((rows,), jnp.int32),
            pltpu.SMEM((rows,), jnp.int32),
            pltpu.VMEM((taps, basis, row_total), F32),
            pltpu.VMEM((band, basis, rows), BF16),
            pltpu.VMEM((rows, cols, chans), BF16),
            pltpu.VMEM((basis, 2 * polar, cycle), BF16),
            pltpu.VMEM((128, -(-row_total // 128) * 128), F32),
            pltpu.VMEM((128, 128), F32),
            pltpu.VMEM((group, rows * SPAN), BF16),
            pltpu.VMEM((rows, ext_cols, chans), BF16),
            pltpu.VMEM((rows * cols, basis * chans), BF16),
            pltpu.VMEM((polar, basis * cols, cycle), BF16),
            pltpu.VMEM((basis, polar * cols, chans), BF16),
            pltpu.VMEM((basis * polar, cols, chans), BF16),
            pltpu.SemaphoreType.DMA((7,)),
        ],
        compiler_params=pltpu.CompilerParams(vmem_limit_bytes=32 * 1024 * 1024),
        cost_estimate=pl.CostEstimate(
            flops=2_000_000_000, bytes_accessed=6_000_000, transcendentals=0
        ),
        name="own_rows",
    )(
        band_start, band_width, jnp.transpose(lon_taps, (2, 1, 0)),
        jnp.transpose(lat_taps, (2, 1, 0)), fields, cycle_taps,
        mixing.reshape(basis * chans, chans), other,
    )

    first, second, acc = lax.optimization_barrier((first, second, acc))
    edges = jnp.concatenate(
        [
            jnp.concatenate([got[:, :reach], got[:, cols - reach :]], axis=1)
            for got in (first, second)
        ],
        axis=0,
    )
    edges = lax.ppermute(edges, "lon", SWAP)
    return pl.pallas_call(
        halo_kernel,
        out_shape=sds((rows, cols, chans), BF16),
        in_specs=[vmem] * 6,
        out_specs=vmem,
        scratch_shapes=[
            pltpu.VMEM((rows, ext_cols, chans), BF16),
            pltpu.VMEM((rows * cols, basis * chans), BF16),
        ],
        compiler_params=pltpu.CompilerParams(vmem_limit_bytes=32 * 1024 * 1024),
        name="halo_rows",
    )(first, second, edges, halo_weights, acc, mix)


def solution(mesh):
    in_specs = (
        P(("ens", "lat"), "lon", None),
        P(),
        P("lat", None, None),
        P(),
        P("lat"),
        P("lat"),
        P(),
    )
    out_specs = P(("ens", "lat"), "lon", None)
    return jax.shard_map(shards, mesh=mesh, in_specs=in_specs, out_specs=out_specs, check_vma=False)
```

```python
import jax
import jax.numpy as jnp
from jax import lax
from jax.experimental import pallas as pl
from jax.experimental.pallas import tpu as pltpu
from jax.sharding import PartitionSpec as P

HALO = 4
BLOCK = 16
SPAN = 32
SWAP = [(0, 1), (1, 0)]
F32, BF16 = jnp.float32, jnp.bfloat16


def ring(lat_count, step):
    pairs = []
    for lat in range(lat_count):
        for core in range(2):
            to = lat + (step if core == 0 else -step)
            if 0 <= to < lat_count:
                pairs.append((lat * 2 + core, to * 2 + core))
            else:
                pairs.append((lat * 2 + core, lat * 2 + 1 - core))
    return pairs


def matmul(a, b):
    return jnp.dot(a, b, preferred_element_type=F32)


def staircase(line, steps):
    wide = jnp.broadcast_to(line, (steps, line.shape[1]))
    return pltpu.roll(wide, 0, 1, stride=1, stride_axis=0).astype(BF16)


def chosen(terms):
    total = None
    for mask, value in terms:
        term = jnp.where(mask, value, 0.0)
        total = term if total is None else total + term
    return total


def window_products(weights, ext, hidden, blocks, rows, basis, cols, chans):
    for b in blocks:
        cells = ext[:, BLOCK * b : BLOCK * b + SPAN, :].reshape(-1, chans)
        part = matmul(weights[...], cells).astype(BF16)
        for k in range(basis):
            for i in range(rows):
                at = (k * rows + i) * BLOCK
                hidden[
                    i * cols + BLOCK * b : i * cols + BLOCK * (b + 1),
                    k * chans : (k + 1) * chans,
                ] = part[at : at + BLOCK]


def own_kernel(
    start_in, width_in, lon_in, lat_in, fields_in, cycle_in, mixing_in, other,
    acc, halo_weights, mix,
    start, width, lon, lat, fields, cycle_taps, lon_wide, lat_wide, own_weights, ext, hidden,
    turned, cycle_rows, mixed_rows, sems,
):
    rows, cols, chans = fields.shape
    taps, basis, row_total = lon.shape
    band = lat.shape[0]
    reach = taps // 2
    polar = cycle_taps.shape[1] // 2
    cycle = cycle_taps.shape[2]
    lat_pos = lax.axis_index("lat")
    base = lat_pos * rows
    at_top = base == 0
    at_bottom = base == row_total - rows

    copies = []
    for n, (source, target) in enumerate(
        [
            (lon_in, lon), (lat_in, lat), (start_in, start), (width_in, width),
            (fields_in, fields), (cycle_in, cycle_taps), (mixing_in, mix),
        ]
    ):
        copies.append(pltpu.make_async_copy(source, target, sems.at[n]))
        copies[-1].start()
    lon_wide[...] = jnp.zeros_like(lon_wide)
    lat_wide[...] = jnp.zeros_like(lat_wide)
    for n in range(4):
        copies[n].wait()

    for d in range(taps):
        for k in range(basis):
            lon_wide[k * 16 + d : k * 16 + d + 1, 0:row_total] = lon[d, k : k + 1, :]
    lanes = lon_wide.shape[1]
    slots = pltpu.roll(lon_wide[...], lax.rem(lanes + HALO - base, lanes), 1)[:, :128]
    slots = jnp.transpose(slots)[: rows + 2 * HALO]
    is_tap = lax.broadcasted_iota(jnp.int32, slots.shape, 1) < taps
    own_taps, halo_taps = [], []
    for k in range(basis):
        moved = slots if k == 0 else pltpu.roll(slots, 128 - 16 * k, 1)
        moved = jnp.where(is_tap, moved, 0.0)
        for _ in range(2):
            moved = pltpu.roll(moved, 0, 1, stride=SPAN // 2, stride_axis=0)
        quads = [jnp.sum(moved[4 * q : 4 * q + 4], axis=0, keepdims=True) for q in range(4)]
        own_taps.append(jnp.concatenate([quads[1], quads[2]], axis=1))
        halo_taps.append(jnp.concatenate([quads[0], quads[3]], axis=1))

    for t in range(band):
        lat_wide[t * basis : (t + 1) * basis, 0:rows] = lat[t].astype(F32)
    lat_cols = jnp.transpose(lat_wide[...])[:rows]
    shape = (rows, rows * SPAN)
    lane = lax.broadcasted_iota(jnp.int32, shape, 1)
    out_row = lax.broadcasted_iota(jnp.int32, shape, 0)
    first = jnp.zeros(shape, jnp.int32)
    count = jnp.zeros(shape, jnp.int32)
    for i in range(rows):
        first = jnp.where(out_row == i, start[i], first)
        count = jnp.where(out_row == i, width[i], count)
    spread = [
        [
            jnp.broadcast_to(lat_cols[:, t * basis + k : t * basis + k + 1], shape)
            for k in range(basis)
        ]
        for t in range(band)
    ]
    slot = lane // SPAN
    own_row = base + slot
    halo_row = jnp.where(slot < HALO, own_row - HALO, own_row + rows - HALO)
    is_polar = (own_row < polar) | (own_row >= row_total - polar)
    in_grid = (halo_row >= 0) & (halo_row < row_total)
    own_step, halo_step = own_row - first, halo_row - first
    own_used = [(own_step == t) & (count > t) & ~is_polar for t in range(band)]
    halo_used = [(halo_step == t) & (count > t) & in_grid for t in range(band)]
    for k in range(basis):
        own_line = own_taps[k] * chosen([(own_used[t], spread[t][k]) for t in range(band)])
        halo_line = halo_taps[k] * chosen([(halo_used[t], spread[t][k]) for t in range(band)])
        for i in range(rows):
            at = (k * rows + i) * BLOCK
            own_weights[at : at + BLOCK, :] = staircase(own_line[i : i + 1], BLOCK)
            halo_weights[at : at + BLOCK, :] = staircase(halo_line[i : i + 1], BLOCK)

    copies[4].wait()
    pad = jnp.zeros((ext.shape[1] - cols - 2 * reach, chans), BF16)
    for r in range(rows):
        ext[r] = jnp.concatenate(
            [other[r, cols - reach :], fields[r], other[r, :reach], pad], axis=0
        )
    window_products(
        own_weights, ext, hidden, range(cols // BLOCK), rows, basis, cols, chans
    )
    copies[5].wait()
    copies[6].wait()
    half = rows // 2
    for n in range(2):
        total = matmul(hidden[n * half * cols : (n + 1) * half * cols], mix[...])
        acc[n * half : (n + 1) * half] = (
            total.reshape(half, cols, chans)
            + fields[n * half : (n + 1) * half].astype(F32)
        )

    @pl.when(at_top | at_bottom)
    def polar_part():
        offset = jnp.where(at_top, 0, rows - polar)
        total = lax.broadcasted_iota(jnp.int32, (cycle, cycle), 0) + lax.broadcasted_iota(
            jnp.int32, (cycle, cycle), 1
        )
        turn = jnp.where((total == 0) | (total == cycle), 1.0, 0.0).astype(BF16)
        negated = matmul(cycle_taps[...].reshape(-1, cycle), turn)
        for p in range(polar):
            for k in range(basis):
                n = k * 2 * polar + p
                line = jnp.where(at_top, negated[n : n + 1], negated[n + polar : n + polar + 1])
                turned[p, k * cols : (k + 1) * cols, :] = staircase(line, cols)
        for p in range(polar):
            whole = jnp.concatenate([fields[offset + p], other[offset + p]], axis=0)
            part = matmul(turned[p], whole).astype(BF16)
            for k in range(basis):
                cycle_rows[k, p * cols : (p + 1) * cols, :] = part[k * cols : (k + 1) * cols]
        for k in range(basis):
            part = matmul(cycle_rows[k], mix[k * chans : (k + 1) * chans, :]).astype(BF16)
            mixed_rows[k * polar : (k + 1) * polar] = part.reshape(polar, cols, chans)
        of_basis = lane // (polar * BLOCK)
        step = base + offset + lax.rem(lane // BLOCK, polar) - first
        at_start = lax.rem(lane, BLOCK) == 0
        terms = []
        for t in range(band):
            value = spread[t][0]
            for k in range(1, basis):
                value = jnp.where(of_basis == k, spread[t][k], value)
            terms.append(((step == t) & (count > t) & at_start, value))
        line = chosen(terms)
        weights = jnp.concatenate(
            [staircase(line[i : i + 1], BLOCK) for i in range(rows)], axis=0
        )
        for b in range(cols // BLOCK):
            at = slice(BLOCK * b, BLOCK * (b + 1))
            cells = mixed_rows[:, at, :].reshape(-1, chans)
            acc[:, at, :] = acc[:, at, :] + matmul(weights, cells).reshape(rows, BLOCK, chans)


def halo_kernel(
    first_in, second_in, first_edges, second_edges, weights, acc, mix, out, ext, hidden,
):
    rows, cols, chans = out.shape
    basis = mix.shape[0] // chans
    reach = first_edges.shape[1] // 2
    is_first = lax.axis_index("lon") == 0
    pad = jnp.zeros((ext.shape[1] - cols - 2 * reach, chans), BF16)
    for s in range(2 * HALO):
        p = s % HALO
        by = (first_in, second_in) if s < HALO else (second_in, first_in)
        body = jnp.where(is_first, by[0][p], by[1][p])
        by = (first_edges, second_edges) if s < HALO else (second_edges, first_edges)
        edge = jnp.where(is_first, by[0][p], by[1][p])
        ext[s] = jnp.concatenate([edge[reach:], body, edge[:reach], pad], axis=0)
    window_products(weights, ext, hidden, range(cols // BLOCK), rows, basis, cols, chans)
    half = rows // 2
    for n in range(2):
        total = matmul(hidden[n * half * cols : (n + 1) * half * cols], mix[...])
        at = slice(n * half, (n + 1) * half)
        out[at] = (total.reshape(half, cols, chans) + acc[at]).astype(BF16)


def shards(fields, lon_taps, lat_taps, cycle_taps, band_start, band_width, mixing):
    rows, cols, chans = fields.shape
    row_total, basis, taps = lon_taps.shape
    band = lat_taps.shape[2]
    reach = (taps - 1) // 2
    polar = cycle_taps.shape[1] // 2
    cycle = cycle_taps.shape[2]
    lat_count = lax.axis_size("lat")
    core = lax.axis_index("lon")
    axes = ("lat", "lon")
    assert cycle == 2 * cols and rows == 2 * HALO and basis * polar * BLOCK == rows * SPAN
    ahead, back = ring(lat_count, 1), ring(lat_count, -1)
    other = lax.ppermute(fields, "lon", SWAP)
    head, tail = fields[:HALO], fields[rows - HALO :]
    first = lax.ppermute(jnp.where(core == 0, tail, head), axes, ahead)
    second = lax.ppermute(jnp.where(core == 0, head, tail), axes, back)
    edges = jnp.concatenate([other[:, :reach], other[:, cols - reach :]], axis=1)
    head, tail = edges[:HALO], edges[rows - HALO :]
    first_edges = lax.ppermute(jnp.where(core == 0, tail, head), axes, ahead)
    second_edges = lax.ppermute(jnp.where(core == 0, head, tail), axes, back)

    vmem = pl.BlockSpec(memory_space=pltpu.VMEM)
    hbm = pl.BlockSpec(memory_space=pltpu.HBM)
    sds = jax.ShapeDtypeStruct
    group = basis * rows * BLOCK
    ext_cols = cols + SPAN - BLOCK
    acc, halo_weights, mix = pl.pallas_call(
        own_kernel,
        out_shape=(
            sds((rows, cols, chans), F32),
            sds((group, rows * SPAN), BF16),
            sds((basis * chans, chans), BF16),
        ),
        in_specs=[hbm] * 7 + [vmem],
        out_specs=(vmem, vmem, vmem),
        scratch_shapes=[
            pltpu.SMEM((rows,), jnp.int32),
            pltpu.SMEM((rows,), jnp.int32),
            pltpu.VMEM((taps, basis, row_total), F32),
            pltpu.VMEM((band, basis, rows), BF16),
            pltpu.VMEM((rows, cols, chans), BF16),
            pltpu.VMEM((basis, 2 * polar, cycle), BF16),
            pltpu.VMEM((128, -(-row_total // 128) * 128), F32),
            pltpu.VMEM((128, 128), F32),
            pltpu.VMEM((group, rows * SPAN), BF16),
            pltpu.VMEM((rows, ext_cols, chans), BF16),
            pltpu.VMEM((rows * cols, basis * chans), BF16),
            pltpu.VMEM((polar, basis * cols, cycle), BF16),
            pltpu.VMEM((basis, polar * cols, chans), BF16),
            pltpu.VMEM((basis * polar, cols, chans), BF16),
            pltpu.SemaphoreType.DMA((7,)),
        ],
        compiler_params=pltpu.CompilerParams(vmem_limit_bytes=32 * 1024 * 1024),
        cost_estimate=pl.CostEstimate(
            flops=2_000_000_000, bytes_accessed=6_000_000, transcendentals=0
        ),
        name="own_rows",
    )(
        *(
            pltpu.with_memory_space_constraint(x, pltpu.HBM)
            for x in (
                band_start, band_width, jnp.transpose(lon_taps, (2, 1, 0)),
                jnp.transpose(lat_taps, (2, 1, 0)), fields, cycle_taps,
                mixing.reshape(basis * chans, chans),
            )
        ),
        other,
    )

    first, second, first_edges, second_edges, acc = lax.optimization_barrier(
        (first, second, first_edges, second_edges, acc)
    )
    return pl.pallas_call(
        halo_kernel,
        out_shape=sds((rows, cols, chans), BF16),
        in_specs=[vmem] * 7,
        out_specs=vmem,
        scratch_shapes=[
            pltpu.VMEM((rows, ext_cols, chans), BF16),
            pltpu.VMEM((rows * cols, basis * chans), BF16),
        ],
        compiler_params=pltpu.CompilerParams(vmem_limit_bytes=32 * 1024 * 1024),
        name="halo_rows",
    )(first, second, first_edges, second_edges, halo_weights, acc, mix)


def solution(mesh):
    in_specs = (
        P(("ens", "lat"), "lon", None),
        P(),
        P("lat", None, None),
        P(),
        P("lat"),
        P("lat"),
        P(),
    )
    out_specs = P(("ens", "lat"), "lon", None)
    return jax.shard_map(shards, mesh=mesh, in_specs=in_specs, out_specs=out_specs, check_vma=False)
```

```python
import jax
import jax.numpy as jnp
from jax import lax
from jax.experimental import pallas as pl
from jax.experimental.pallas import tpu as pltpu
from jax.sharding import PartitionSpec as P

HALO = 4
BLOCK = 16
SPAN = 32
SWAP = [(0, 1), (1, 0)]
F32, BF16 = jnp.float32, jnp.bfloat16


def ring(lat_count, step):
    pairs = []
    for lat in range(lat_count):
        for core in range(2):
            to = lat + (step if core == 0 else -step)
            if 0 <= to < lat_count:
                pairs.append((lat * 2 + core, to * 2 + core))
            else:
                pairs.append((lat * 2 + core, lat * 2 + 1 - core))
    return pairs


def matmul(a, b):
    return jnp.dot(a, b, preferred_element_type=F32)


def staircase(line, steps):
    wide = jnp.broadcast_to(line, (steps, line.shape[1]))
    return pltpu.roll(wide, 0, 1, stride=1, stride_axis=0).astype(BF16)


def chosen(terms):
    total = None
    for mask, value in terms:
        term = jnp.where(mask, value, 0.0)
        total = term if total is None else total + term
    return total


def window_products(weights, ext, hidden, blocks, rows, basis, cols, chans):
    for b in blocks:
        cells = ext[:, BLOCK * b : BLOCK * b + SPAN, :].reshape(-1, chans)
        part = matmul(weights[...], cells).astype(BF16)
        for k in range(basis):
            for i in range(rows):
                at = (k * rows + i) * BLOCK
                hidden[
                    i * cols + BLOCK * b : i * cols + BLOCK * (b + 1),
                    k * chans : (k + 1) * chans,
                ] = part[at : at + BLOCK]


def own_kernel(
    start_in, width_in, lon_in, lat_in, fields_in, cycle_in, mixing_in, other,
    acc, halo_weights, mix,
    start, width, lon, lat, fields, cycle_taps, lon_wide, lat_wide, own_weights, ext, hidden,
    turned, cycle_rows, mixed_rows, sems,
):
    rows, cols, chans = fields.shape
    taps, basis, row_total = lon.shape
    band = lat.shape[0]
    reach = taps // 2
    polar = cycle_taps.shape[1] // 2
    cycle = cycle_taps.shape[2]
    lat_pos = lax.axis_index("lat")
    base = lat_pos * rows
    at_top = base == 0
    at_bottom = base == row_total - rows

    copies = []
    for n, (source, target) in enumerate(
        [
            (lon_in, lon), (lat_in, lat), (start_in, start), (width_in, width),
            (fields_in, fields), (cycle_in, cycle_taps), (mixing_in, mix),
        ]
    ):
        copies.append(pltpu.make_async_copy(source, target, sems.at[n]))
        copies[-1].start()
    lon_wide[...] = jnp.zeros_like(lon_wide)
    lat_wide[...] = jnp.zeros_like(lat_wide)
    for n in range(4):
        copies[n].wait()

    for d in range(taps):
        for k in range(basis):
            lon_wide[k * 16 + d : k * 16 + d + 1, 0:row_total] = lon[d, k : k + 1, :]
    lanes = lon_wide.shape[1]
    slots = pltpu.roll(lon_wide[...], lax.rem(lanes + HALO - base, lanes), 1)[:, :128]
    slots = jnp.transpose(slots)[: rows + 2 * HALO]
    is_tap = lax.broadcasted_iota(jnp.int32, slots.shape, 1) < taps
    own_taps, halo_taps = [], []
    for k in range(basis):
        moved = slots if k == 0 else pltpu.roll(slots, 128 - 16 * k, 1)
        moved = jnp.where(is_tap, moved, 0.0)
        for _ in range(2):
            moved = pltpu.roll(moved, 0, 1, stride=SPAN // 2, stride_axis=0)
        quads = [jnp.sum(moved[4 * q : 4 * q + 4], axis=0, keepdims=True) for q in range(4)]
        own_taps.append(jnp.concatenate([quads[1], quads[2]], axis=1))
        halo_taps.append(jnp.concatenate([quads[0], quads[3]], axis=1))

    for t in range(band):
        lat_wide[t * basis : (t + 1) * basis, 0:rows] = lat[t].astype(F32)
    lat_cols = jnp.transpose(lat_wide[...])[:rows]
    shape = (rows, rows * SPAN)
    lane = lax.broadcasted_iota(jnp.int32, shape, 1)
    out_row = lax.broadcasted_iota(jnp.int32, shape, 0)
    first = jnp.zeros(shape, jnp.int32)
    count = jnp.zeros(shape, jnp.int32)
    for i in range(rows):
        first = jnp.where(out_row == i, start[i], first)
        count = jnp.where(out_row == i, width[i], count)
    spread = [
        [
            jnp.broadcast_to(lat_cols[:, t * basis + k : t * basis + k + 1], shape)
            for k in range(basis)
        ]
        for t in range(band)
    ]
    slot = lane // SPAN
    own_row = base + slot
    halo_row = jnp.where(slot < HALO, own_row - HALO, own_row + rows - HALO)
    is_polar = (own_row < polar) | (own_row >= row_total - polar)
    in_grid = (halo_row >= 0) & (halo_row < row_total)
    own_step, halo_step = own_row - first, halo_row - first
    own_used = [(own_step == t) & (count > t) & ~is_polar for t in range(band)]
    halo_used = [(halo_step == t) & (count > t) & in_grid for t in range(band)]
    for k in range(basis):
        own_line = own_taps[k] * chosen([(own_used[t], spread[t][k]) for t in range(band)])
        halo_line = halo_taps[k] * chosen([(halo_used[t], spread[t][k]) for t in range(band)])
        for i in range(rows):
            at = (k * rows + i) * BLOCK
            own_weights[at : at + BLOCK, :] = staircase(own_line[i : i + 1], BLOCK)
            halo_weights[at : at + BLOCK, :] = staircase(halo_line[i : i + 1], BLOCK)

    copies[4].wait()
    pad = jnp.zeros((ext.shape[1] - cols - 2 * reach, chans), BF16)
    for r in range(rows):
        ext[r] = jnp.concatenate(
            [other[r, cols - reach :], fields[r], other[r, :reach], pad], axis=0
        )
    window_products(
        own_weights, ext, hidden, range(cols // BLOCK), rows, basis, cols, chans
    )
    copies[5].wait()
    copies[6].wait()
    half = rows // 2
    for n in range(2):
        total = matmul(hidden[n * half * cols : (n + 1) * half * cols], mix[...])
        acc[n * half : (n + 1) * half] = (
            total.reshape(half, cols, chans)
            + fields[n * half : (n + 1) * half].astype(F32)
        )

    @pl.when(at_top | at_bottom)
    def polar_part():
        offset = jnp.where(at_top, 0, rows - polar)
        total = lax.broadcasted_iota(jnp.int32, (cycle, cycle), 0) + lax.broadcasted_iota(
            jnp.int32, (cycle, cycle), 1
        )
        turn = jnp.where((total == 0) | (total == cycle), 1.0, 0.0).astype(BF16)
        negated = matmul(cycle_taps[...].reshape(-1, cycle), turn)
        for p in range(polar):
            for k in range(basis):
                n = k * 2 * polar + p
                line = jnp.where(at_top, negated[n : n + 1], negated[n + polar : n + polar + 1])
                turned[p, k * cols : (k + 1) * cols, :] = staircase(line, cols)
        for p in range(polar):
            whole = jnp.concatenate([fields[offset + p], other[offset + p]], axis=0)
            part = matmul(turned[p], whole).astype(BF16)
            for k in range(basis):
                cycle_rows[k, p * cols : (p + 1) * cols, :] = part[k * cols : (k + 1) * cols]
        for k in range(basis):
            part = matmul(cycle_rows[k], mix[k * chans : (k + 1) * chans, :]).astype(BF16)
            mixed_rows[k * polar : (k + 1) * polar] = part.reshape(polar, cols, chans)
        of_basis = lane // (polar * BLOCK)
        step = base + offset + lax.rem(lane // BLOCK, polar) - first
        at_start = lax.rem(lane, BLOCK) == 0
        terms = []
        for t in range(band):
            value = spread[t][0]
            for k in range(1, basis):
                value = jnp.where(of_basis == k, spread[t][k], value)
            terms.append(((step == t) & (count > t) & at_start, value))
        line = chosen(terms)
        weights = jnp.concatenate(
            [staircase(line[i : i + 1], BLOCK) for i in range(rows)], axis=0
        )
        for b in range(cols // BLOCK):
            at = slice(BLOCK * b, BLOCK * (b + 1))
            cells = mixed_rows[:, at, :].reshape(-1, chans)
            acc[:, at, :] = acc[:, at, :] + matmul(weights, cells).reshape(rows, BLOCK, chans)


def halo_kernel(
    second_in, first_in, second_edges, first_edges, weights, acc, mix, out, ext, hidden,
):
    rows, cols, chans = out.shape
    basis = mix.shape[0] // chans
    reach = first_edges.shape[1] // 2
    is_first = lax.axis_index("lon") == 0
    pad = jnp.zeros((ext.shape[1] - cols - 2 * reach, chans), BF16)
    for s in range(2 * HALO):
        p = s % HALO
        by = (first_in, second_in) if s < HALO else (second_in, first_in)
        body = jnp.where(is_first, by[0][p], by[1][p])
        by = (first_edges, second_edges) if s < HALO else (second_edges, first_edges)
        edge = jnp.where(is_first, by[0][p], by[1][p])
        ext[s] = jnp.concatenate([edge[reach:], body, edge[:reach], pad], axis=0)
    window_products(weights, ext, hidden, range(cols // BLOCK), rows, basis, cols, chans)
    half = rows // 2
    for n in range(2):
        total = matmul(hidden[n * half * cols : (n + 1) * half * cols], mix[...])
        at = slice(n * half, (n + 1) * half)
        out[at] = (total.reshape(half, cols, chans) + acc[at]).astype(BF16)


def shards(fields, lon_taps, lat_taps, cycle_taps, band_start, band_width, mixing):
    rows, cols, chans = fields.shape
    row_total, basis, taps = lon_taps.shape
    band = lat_taps.shape[2]
    reach = (taps - 1) // 2
    polar = cycle_taps.shape[1] // 2
    cycle = cycle_taps.shape[2]
    lat_count = lax.axis_size("lat")
    core = lax.axis_index("lon")
    axes = ("lat", "lon")
    assert cycle == 2 * cols and rows == 2 * HALO and basis * polar * BLOCK == rows * SPAN
    ahead, back = ring(lat_count, 1), ring(lat_count, -1)
    other = lax.ppermute(fields, "lon", SWAP)
    head, tail = fields[:HALO], fields[rows - HALO :]
    second = lax.ppermute(jnp.where(core == 0, head, tail), axes, back)
    first = lax.ppermute(jnp.where(core == 0, tail, head), axes, ahead)
    edges = jnp.concatenate([other[:, :reach], other[:, cols - reach :]], axis=1)
    head, tail = edges[:HALO], edges[rows - HALO :]
    second_edges = lax.ppermute(jnp.where(core == 0, head, tail), axes, back)
    first_edges = lax.ppermute(jnp.where(core == 0, tail, head), axes, ahead)

    vmem = pl.BlockSpec(memory_space=pltpu.VMEM)
    hbm = pl.BlockSpec(memory_space=pltpu.HBM)
    sds = jax.ShapeDtypeStruct
    group = basis * rows * BLOCK
    ext_cols = cols + SPAN - BLOCK
    acc, halo_weights, mix = pl.pallas_call(
        own_kernel,
        out_shape=(
            sds((rows, cols, chans), F32),
            sds((group, rows * SPAN), BF16),
            sds((basis * chans, chans), BF16),
        ),
        in_specs=[hbm] * 7 + [vmem],
        out_specs=(vmem, vmem, vmem),
        scratch_shapes=[
            pltpu.SMEM((rows,), jnp.int32),
            pltpu.SMEM((rows,), jnp.int32),
            pltpu.VMEM((taps, basis, row_total), F32),
            pltpu.VMEM((band, basis, rows), BF16),
            pltpu.VMEM((rows, cols, chans), BF16),
            pltpu.VMEM((basis, 2 * polar, cycle), BF16),
            pltpu.VMEM((128, -(-row_total // 128) * 128), F32),
            pltpu.VMEM((128, 128), F32),
            pltpu.VMEM((group, rows * SPAN), BF16),
            pltpu.VMEM((rows, ext_cols, chans), BF16),
            pltpu.VMEM((rows * cols, basis * chans), BF16),
            pltpu.VMEM((polar, basis * cols, cycle), BF16),
            pltpu.VMEM((basis, polar * cols, chans), BF16),
            pltpu.VMEM((basis * polar, cols, chans), BF16),
            pltpu.SemaphoreType.DMA((7,)),
        ],
        compiler_params=pltpu.CompilerParams(vmem_limit_bytes=32 * 1024 * 1024),
        cost_estimate=pl.CostEstimate(
            flops=2_000_000_000, bytes_accessed=6_000_000, transcendentals=0
        ),
        name="own_rows",
    )(
        *(
            pltpu.with_memory_space_constraint(x, pltpu.HBM)
            for x in (
                band_start, band_width, jnp.transpose(lon_taps, (2, 1, 0)),
                jnp.transpose(lat_taps, (2, 1, 0)), fields, cycle_taps,
                mixing.reshape(basis * chans, chans),
            )
        ),
        other,
    )

    second, first, second_edges, first_edges, acc = lax.optimization_barrier(
        (second, first, second_edges, first_edges, acc)
    )
    return pl.pallas_call(
        halo_kernel,
        out_shape=sds((rows, cols, chans), BF16),
        in_specs=[vmem] * 7,
        out_specs=vmem,
        scratch_shapes=[
            pltpu.VMEM((rows, ext_cols, chans), BF16),
            pltpu.VMEM((rows * cols, basis * chans), BF16),
        ],
        compiler_params=pltpu.CompilerParams(vmem_limit_bytes=32 * 1024 * 1024),
        name="halo_rows",
    )(second, first, second_edges, first_edges, halo_weights, acc, mix)


def solution(mesh):
    in_specs = (
        P(("ens", "lat"), "lon", None),
        P(),
        P("lat", None, None),
        P(),
        P("lat"),
        P("lat"),
        P(),
    )
    out_specs = P(("ens", "lat"), "lon", None)
    return jax.shard_map(shards, mesh=mesh, in_specs=in_specs, out_specs=out_specs, check_vma=False)
```

```python
import jax
import jax.numpy as jnp
from jax import lax
from jax.experimental import pallas as pl
from jax.experimental.pallas import tpu as pltpu
from jax.sharding import PartitionSpec as P

HALO = 4
BLOCK = 16
SPAN = 32
SWAP = [(0, 1), (1, 0)]
F32, BF16 = jnp.float32, jnp.bfloat16


def ring(lat_count, step):
    pairs = []
    for lat in range(lat_count):
        for core in range(2):
            to = lat + (step if core == 0 else -step)
            if 0 <= to < lat_count:
                pairs.append((lat * 2 + core, to * 2 + core))
            else:
                pairs.append((lat * 2 + core, lat * 2 + 1 - core))
    return pairs


def matmul(a, b):
    return jnp.dot(a, b, preferred_element_type=F32)


def staircase(line, steps):
    wide = jnp.broadcast_to(line, (steps, line.shape[1]))
    return pltpu.roll(wide, 0, 1, stride=1, stride_axis=0).astype(BF16)


def chosen(terms):
    total = None
    for mask, value in terms:
        term = jnp.where(mask, value, 0.0)
        total = term if total is None else total + term
    return total


def window_products(weights, ext, hidden, groups, cols, chans):
    for at in range(0, cols, BLOCK):
        cells = ext[:, at : at + SPAN, :].reshape(-1, chans)
        part = matmul(weights[...], cells).astype(BF16)
        for n, (i, k) in enumerate(groups):
            hidden[i * cols + at : i * cols + at + BLOCK, k * chans : (k + 1) * chans] = part[
                n * BLOCK : (n + 1) * BLOCK
            ]


def own_kernel(
    start_in, width_in, lon_in, lat_in, fields_in, cycle_in, mixing_in, other,
    acc, halo_weights, mix,
    start, width, lon, lat, fields, cycle_taps, lon_wide, lat_wide, own_weights, ext, hidden,
    turned, cycle_rows, mixed_rows, sems,
):
    rows, cols, chans = fields.shape
    taps, basis, row_total = lon.shape
    band = lat.shape[0]
    reach = taps // 2
    polar = cycle_taps.shape[1] // 2
    cycle = cycle_taps.shape[2]
    lat_pos = lax.axis_index("lat")
    base = lat_pos * rows
    at_top = base == 0
    at_bottom = base == row_total - rows

    copies = []
    for n, (source, target) in enumerate(
        [
            (lon_in, lon), (lat_in, lat), (start_in, start), (width_in, width),
            (fields_in, fields), (cycle_in, cycle_taps), (mixing_in, mix),
        ]
    ):
        copies.append(pltpu.make_async_copy(source, target, sems.at[n]))
        copies[-1].start()
    lon_wide[...] = jnp.zeros_like(lon_wide)
    lat_wide[...] = jnp.zeros_like(lat_wide)
    for n in range(4):
        copies[n].wait()

    for d in range(taps):
        for k in range(basis):
            lon_wide[k * 16 + d : k * 16 + d + 1, 0:row_total] = lon[d, k : k + 1, :]
    lanes = lon_wide.shape[1]
    slots = pltpu.roll(lon_wide[...], lax.rem(lanes + HALO - base, lanes), 1)[:, :128]
    slots = jnp.transpose(slots)[: rows + 2 * HALO]
    is_tap = lax.broadcasted_iota(jnp.int32, slots.shape, 1) < taps
    own_taps, halo_taps = [], []
    for k in range(basis):
        moved = slots if k == 0 else pltpu.roll(slots, 128 - 16 * k, 1)
        moved = jnp.where(is_tap, moved, 0.0)
        for _ in range(2):
            moved = pltpu.roll(moved, 0, 1, stride=SPAN // 2, stride_axis=0)
        quads = [jnp.sum(moved[4 * q : 4 * q + 4], axis=0, keepdims=True) for q in range(4)]
        own_taps.append(jnp.concatenate([quads[1], quads[2]], axis=1))
        halo_taps.append(jnp.concatenate([quads[0], quads[3]], axis=1))

    for t in range(band):
        lat_wide[t * basis : (t + 1) * basis, 0:rows] = lat[t].astype(F32)
    lat_cols = jnp.transpose(lat_wide[...])[:rows]
    shape = (rows, rows * SPAN)
    lane = lax.broadcasted_iota(jnp.int32, shape, 1)
    out_row = lax.broadcasted_iota(jnp.int32, shape, 0)
    first = jnp.zeros(shape, jnp.int32)
    count = jnp.zeros(shape, jnp.int32)
    for i in range(rows):
        first = jnp.where(out_row == i, start[i], first)
        count = jnp.where(out_row == i, width[i], count)
    spread = [
        [
            jnp.broadcast_to(lat_cols[:, t * basis + k : t * basis + k + 1], shape)
            for k in range(basis)
        ]
        for t in range(band)
    ]
    slot = lane // SPAN
    own_row = base + slot
    halo_row = jnp.where(slot < HALO, own_row - HALO, own_row + rows - HALO)
    is_polar = (own_row < polar) | (own_row >= row_total - polar)
    in_grid = (halo_row >= 0) & (halo_row < row_total)
    own_step, halo_step = own_row - first, halo_row - first
    own_used = [(own_step == t) & (count > t) & ~is_polar for t in range(band)]
    halo_used = [(halo_step == t) & (count > t) & in_grid for t in range(band)]
    for k in range(basis):
        own_line = own_taps[k] * chosen([(own_used[t], spread[t][k]) for t in range(band)])
        halo_line = halo_taps[k] * chosen([(halo_used[t], spread[t][k]) for t in range(band)])
        for i in range(rows):
            at = (k * rows + i) * BLOCK
            own_weights[at : at + BLOCK, :] = staircase(own_line[i : i + 1], BLOCK)
            at = ((i // HALO * basis + k) * HALO + i % HALO) * BLOCK
            halo_weights[at : at + BLOCK, :] = staircase(halo_line[i : i + 1], BLOCK)

    copies[4].wait()
    pad = jnp.zeros((ext.shape[1] - cols - 2 * reach, chans), BF16)
    for r in range(rows):
        ext[r] = jnp.concatenate(
            [other[r, cols - reach :], fields[r], other[r, :reach], pad], axis=0
        )
    groups = [(i, k) for k in range(basis) for i in range(rows)]
    window_products(own_weights, ext, hidden, groups, cols, chans)
    copies[5].wait()
    copies[6].wait()
    half = rows // 2
    for n in range(2):
        total = matmul(hidden[n * half * cols : (n + 1) * half * cols], mix[...])
        acc[n * half : (n + 1) * half] = (
            total.reshape(half, cols, chans)
            + fields[n * half : (n + 1) * half].astype(F32)
        )

    @pl.when(at_top | at_bottom)
    def polar_part():
        offset = jnp.where(at_top, 0, rows - polar)
        total = lax.broadcasted_iota(jnp.int32, (cycle, cycle), 0) + lax.broadcasted_iota(
            jnp.int32, (cycle, cycle), 1
        )
        turn = jnp.where((total == 0) | (total == cycle), 1.0, 0.0).astype(BF16)
        negated = matmul(cycle_taps[...].reshape(-1, cycle), turn)
        for p in range(polar):
            for k in range(basis):
                n = k * 2 * polar + p
                line = jnp.where(at_top, negated[n : n + 1], negated[n + polar : n + polar + 1])
                turned[p, k * cols : (k + 1) * cols, :] = staircase(line, cols)
        for p in range(polar):
            whole = jnp.concatenate([fields[offset + p], other[offset + p]], axis=0)
            part = matmul(turned[p], whole).astype(BF16)
            for k in range(basis):
                cycle_rows[k, p * cols : (p + 1) * cols, :] = part[k * cols : (k + 1) * cols]
        for k in range(basis):
            part = matmul(cycle_rows[k], mix[k * chans : (k + 1) * chans, :]).astype(BF16)
            mixed_rows[k * polar : (k + 1) * polar] = part.reshape(polar, cols, chans)
        of_basis = lane // (polar * BLOCK)
        step = base + offset + lax.rem(lane // BLOCK, polar) - first
        at_start = lax.rem(lane, BLOCK) == 0
        terms = []
        for t in range(band):
            value = spread[t][0]
            for k in range(1, basis):
                value = jnp.where(of_basis == k, spread[t][k], value)
            terms.append(((step == t) & (count > t) & at_start, value))
        line = chosen(terms)
        weights = jnp.concatenate(
            [staircase(line[i : i + 1], BLOCK) for i in range(rows)], axis=0
        )
        for b in range(cols // BLOCK):
            at = slice(BLOCK * b, BLOCK * (b + 1))
            cells = mixed_rows[:, at, :].reshape(-1, chans)
            acc[:, at, :] = acc[:, at, :] + matmul(weights, cells).reshape(rows, BLOCK, chans)


def halo_kernel(
    second_in, first_in, second_edges, first_edges, weights, acc, mix, out, ext, hidden,
):
    rows, cols, chans = out.shape
    basis = mix.shape[0] // chans
    reach = first_edges.shape[1] // 2
    is_first = lax.axis_index("lon") == 0
    has_upper = lax.axis_index("lat") != 0
    has_lower = lax.axis_index("lat") != lax.axis_size("lat") - 1
    half = rows // 2
    group = half * basis * BLOCK
    pad = jnp.zeros((ext.shape[1] - cols - 2 * reach, chans), BF16)

    def add(sides):
        groups = []
        for side in sides:
            by = [(first_in, second_in), (second_in, first_in)][side]
            by_edges = [(first_edges, second_edges), (second_edges, first_edges)][side]
            for p in range(HALO):
                body = jnp.where(is_first, by[0][p], by[1][p])
                edge = jnp.where(is_first, by_edges[0][p], by_edges[1][p])
                ext[side * HALO + p] = jnp.concatenate(
                    [edge[reach:], body, edge[:reach], pad], axis=0
                )
            groups += [(side * half + i, k) for k in range(basis) for i in range(half)]
        at, end = sides[0], sides[-1] + 1
        window_products(
            weights.at[at * group : end * group, at * HALO * SPAN : end * HALO * SPAN],
            ext.at[at * HALO : end * HALO], hidden, groups, cols, chans,
        )
        for side in sides:
            at = slice(side * half, (side + 1) * half)
            total = matmul(hidden[side * half * cols : (side + 1) * half * cols], mix[...])
            out[at] = (total.reshape(half, cols, chans) + acc[at]).astype(BF16)

    def keep(side):
        at = slice(side * half, (side + 1) * half)
        out[at] = acc[at].astype(BF16)

    @pl.when(has_upper & has_lower)
    def both_sides():
        add((0, 1))

    @pl.when(jnp.logical_not(has_upper))
    def lower_side():
        keep(0)
        add((1,))

    @pl.when(jnp.logical_not(has_lower))
    def upper_side():
        add((0,))
        keep(1)


def shards(fields, lon_taps, lat_taps, cycle_taps, band_start, band_width, mixing):
    rows, cols, chans = fields.shape
    row_total, basis, taps = lon_taps.shape
    band = lat_taps.shape[2]
    reach = (taps - 1) // 2
    polar = cycle_taps.shape[1] // 2
    cycle = cycle_taps.shape[2]
    lat_count = lax.axis_size("lat")
    core = lax.axis_index("lon")
    axes = ("lat", "lon")
    assert cycle == 2 * cols and rows == 2 * HALO and basis * polar * BLOCK == rows * SPAN
    ahead, back = ring(lat_count, 1), ring(lat_count, -1)
    other = lax.ppermute(fields, "lon", SWAP)
    head, tail = fields[:HALO], fields[rows - HALO :]
    second = lax.ppermute(jnp.where(core == 0, head, tail), axes, back)
    first = lax.ppermute(jnp.where(core == 0, tail, head), axes, ahead)
    edges = jnp.concatenate([other[:, :reach], other[:, cols - reach :]], axis=1)
    head, tail = edges[:HALO], edges[rows - HALO :]
    second_edges = lax.ppermute(jnp.where(core == 0, head, tail), axes, back)
    first_edges = lax.ppermute(jnp.where(core == 0, tail, head), axes, ahead)

    vmem = pl.BlockSpec(memory_space=pltpu.VMEM)
    hbm = pl.BlockSpec(memory_space=pltpu.HBM)
    sds = jax.ShapeDtypeStruct
    group = basis * rows * BLOCK
    ext_cols = cols + SPAN - BLOCK
    acc, halo_weights, mix = pl.pallas_call(
        own_kernel,
        out_shape=(
            sds((rows, cols, chans), F32),
            sds((group, rows * SPAN), BF16),
            sds((basis * chans, chans), BF16),
        ),
        in_specs=[hbm] * 7 + [vmem],
        out_specs=(vmem, vmem, vmem),
        scratch_shapes=[
            pltpu.SMEM((rows,), jnp.int32),
            pltpu.SMEM((rows,), jnp.int32),
            pltpu.VMEM((taps, basis, row_total), F32),
            pltpu.VMEM((band, basis, rows), BF16),
            pltpu.VMEM((rows, cols, chans), BF16),
            pltpu.VMEM((basis, 2 * polar, cycle), BF16),
            pltpu.VMEM((128, -(-row_total // 128) * 128), F32),
            pltpu.VMEM((128, 128), F32),
            pltpu.VMEM((group, rows * SPAN), BF16),
            pltpu.VMEM((rows, ext_cols, chans), BF16),
            pltpu.VMEM((rows * cols, basis * chans), BF16),
            pltpu.VMEM((polar, basis * cols, cycle), BF16),
            pltpu.VMEM((basis, polar * cols, chans), BF16),
            pltpu.VMEM((basis * polar, cols, chans), BF16),
            pltpu.SemaphoreType.DMA((7,)),
        ],
        compiler_params=pltpu.CompilerParams(vmem_limit_bytes=32 * 1024 * 1024),
        cost_estimate=pl.CostEstimate(
            flops=2_000_000_000, bytes_accessed=6_000_000, transcendentals=0
        ),
        name="own_rows",
    )(
        *(
            pltpu.with_memory_space_constraint(x, pltpu.HBM)
            for x in (
                band_start, band_width, jnp.transpose(lon_taps, (2, 1, 0)),
                jnp.transpose(lat_taps, (2, 1, 0)), fields, cycle_taps,
                mixing.reshape(basis * chans, chans),
            )
        ),
        other,
    )

    second, first, second_edges, first_edges, acc = lax.optimization_barrier(
        (second, first, second_edges, first_edges, acc)
    )
    return pl.pallas_call(
        halo_kernel,
        out_shape=sds((rows, cols, chans), BF16),
        in_specs=[vmem] * 7,
        out_specs=vmem,
        scratch_shapes=[
            pltpu.VMEM((rows, ext_cols, chans), BF16),
            pltpu.VMEM((rows * cols, basis * chans), BF16),
        ],
        compiler_params=pltpu.CompilerParams(vmem_limit_bytes=32 * 1024 * 1024),
        name="halo_rows",
    )(second, first, second_edges, first_edges, halo_weights, acc, mix)


def solution(mesh):
    in_specs = (
        P(("ens", "lat"), "lon", None),
        P(),
        P("lat", None, None),
        P(),
        P("lat"),
        P("lat"),
        P(),
    )
    out_specs = P(("ens", "lat"), "lon", None)
    return jax.shard_map(shards, mesh=mesh, in_specs=in_specs, out_specs=out_specs, check_vma=False)
```

```python
import jax
import jax.numpy as jnp
from jax import lax
from jax.experimental import pallas as pl
from jax.experimental.pallas import tpu as pltpu
from jax.sharding import PartitionSpec as P

HALO = 4
BLOCK = 16
SPAN = 32
SWAP = [(0, 1), (1, 0)]
F32, BF16 = jnp.float32, jnp.bfloat16


def ring(lat_count, step):
    pairs = []
    for lat in range(lat_count):
        for core in range(2):
            to = lat + (step if core == 0 else -step)
            if 0 <= to < lat_count:
                pairs.append((lat * 2 + core, to * 2 + core))
            else:
                pairs.append((lat * 2 + core, lat * 2 + 1 - core))
    return pairs


def matmul(a, b):
    return jnp.dot(a, b, preferred_element_type=F32)


def staircase(line, steps):
    wide = jnp.broadcast_to(line, (steps, line.shape[1]))
    return pltpu.roll(wide, 0, 1, stride=1, stride_axis=0).astype(BF16)


def chosen(terms):
    total = None
    for mask, value in terms:
        term = jnp.where(mask, value, 0.0)
        total = term if total is None else total + term
    return total


def window_products(weights, ext, hidden, groups, cols, chans):
    for at in range(0, cols, BLOCK):
        cells = ext[:, at : at + SPAN, :].reshape(-1, chans)
        part = matmul(weights[...], cells).astype(BF16)
        for n, (i, k) in enumerate(groups):
            hidden[i * cols + at : i * cols + at + BLOCK, k * chans : (k + 1) * chans] = part[
                n * BLOCK : (n + 1) * BLOCK
            ]


def own_kernel(
    start_in, width_in, lon_in, lat_in, fields_in, cycle_in, mixing_in, other,
    acc, halo_weights, mix,
    start, width, lon, lat, fields, cycle_taps, lon_wide, lat_wide, own_weights, ext, hidden,
    turned, cycle_rows, mixed_rows, sems,
):
    rows, cols, chans = fields.shape
    taps, basis, row_total = lon.shape
    band = lat.shape[0]
    reach = taps // 2
    polar = cycle_taps.shape[1] // 2
    cycle = cycle_taps.shape[2]
    lat_pos = lax.axis_index("lat")
    base = lat_pos * rows
    at_top = base == 0
    at_bottom = base == row_total - rows

    copies = []
    for n, (source, target) in enumerate(
        [
            (lon_in, lon), (lat_in, lat), (start_in, start), (width_in, width),
            (fields_in, fields), (cycle_in, cycle_taps), (mixing_in, mix),
        ]
    ):
        copies.append(pltpu.make_async_copy(source, target, sems.at[n]))
        copies[-1].start()
    lon_wide[...] = jnp.zeros_like(lon_wide)
    lat_wide[...] = jnp.zeros_like(lat_wide)
    for n in range(4):
        copies[n].wait()

    for d in range(taps):
        for k in range(basis):
            lon_wide[k * 16 + d : k * 16 + d + 1, 0:row_total] = lon[d, k : k + 1, :]
    lanes = lon_wide.shape[1]
    slots = pltpu.roll(lon_wide[...], lax.rem(lanes + HALO - base, lanes), 1)[:, :128]
    slots = jnp.transpose(slots)[: rows + 2 * HALO]
    is_tap = lax.broadcasted_iota(jnp.int32, slots.shape, 1) < taps
    own_taps, halo_taps = [], []
    for k in range(basis):
        moved = slots if k == 0 else pltpu.roll(slots, 128 - 16 * k, 1)
        moved = jnp.where(is_tap, moved, 0.0)
        for _ in range(2):
            moved = pltpu.roll(moved, 0, 1, stride=SPAN // 2, stride_axis=0)
        quads = [jnp.sum(moved[4 * q : 4 * q + 4], axis=0, keepdims=True) for q in range(4)]
        own_taps.append(jnp.concatenate([quads[1], quads[2]], axis=1))
        halo_taps.append(jnp.concatenate([quads[0], quads[3]], axis=1))

    for t in range(band):
        lat_wide[t * basis : (t + 1) * basis, 0:rows] = lat[t].astype(F32)
    lat_cols = jnp.transpose(lat_wide[...])[:rows]
    shape = (rows, rows * SPAN)
    lane = lax.broadcasted_iota(jnp.int32, shape, 1)
    out_row = lax.broadcasted_iota(jnp.int32, shape, 0)
    first = jnp.zeros(shape, jnp.int32)
    count = jnp.zeros(shape, jnp.int32)
    for i in range(rows):
        first = jnp.where(out_row == i, start[i], first)
        count = jnp.where(out_row == i, width[i], count)
    spread = [
        [
            jnp.broadcast_to(lat_cols[:, t * basis + k : t * basis + k + 1], shape)
            for k in range(basis)
        ]
        for t in range(band)
    ]
    slot = lane // SPAN
    own_row = base + slot
    halo_row = jnp.where(slot < HALO, own_row - HALO, own_row + rows - HALO)
    is_polar = (own_row < polar) | (own_row >= row_total - polar)
    in_grid = (halo_row >= 0) & (halo_row < row_total)
    own_step, halo_step = own_row - first, halo_row - first
    own_used = [(own_step == t) & (count > t) & ~is_polar for t in range(band)]
    halo_used = [(halo_step == t) & (count > t) & in_grid for t in range(band)]
    for k in range(basis):
        own_line = own_taps[k] * chosen([(own_used[t], spread[t][k]) for t in range(band)])
        halo_line = halo_taps[k] * chosen([(halo_used[t], spread[t][k]) for t in range(band)])
        for i in range(rows):
            at = (k * rows + i) * BLOCK
            own_weights[at : at + BLOCK, :] = staircase(own_line[i : i + 1], BLOCK)
            side, at = i // HALO, (k * HALO + i % HALO) * BLOCK
            reached = halo_line[i : i + 1, side * HALO * SPAN : (side + 1) * HALO * SPAN]
            halo_weights[side, at : at + BLOCK, :] = staircase(reached, BLOCK)

    copies[4].wait()
    pad = jnp.zeros((ext.shape[1] - cols - 2 * reach, chans), BF16)
    for r in range(rows):
        ext[r] = jnp.concatenate(
            [other[r, cols - reach :], fields[r], other[r, :reach], pad], axis=0
        )
    groups = [(i, k) for k in range(basis) for i in range(rows)]
    window_products(own_weights, ext, hidden, groups, cols, chans)
    copies[5].wait()
    copies[6].wait()
    half = rows // 2
    for n in range(2):
        total = matmul(hidden[n * half * cols : (n + 1) * half * cols], mix[...])
        acc[n * half : (n + 1) * half] = (
            total.reshape(half, cols, chans)
            + fields[n * half : (n + 1) * half].astype(F32)
        )

    @pl.when(at_top | at_bottom)
    def polar_part():
        offset = jnp.where(at_top, 0, rows - polar)
        total = lax.broadcasted_iota(jnp.int32, (cycle, cycle), 0) + lax.broadcasted_iota(
            jnp.int32, (cycle, cycle), 1
        )
        turn = jnp.where((total == 0) | (total == cycle), 1.0, 0.0).astype(BF16)
        negated = matmul(cycle_taps[...].reshape(-1, cycle), turn)
        for p in range(polar):
            for k in range(basis):
                n = k * 2 * polar + p
                line = jnp.where(at_top, negated[n : n + 1], negated[n + polar : n + polar + 1])
                turned[p, k * cols : (k + 1) * cols, :] = staircase(line, cols)
        for p in range(polar):
            whole = jnp.concatenate([fields[offset + p], other[offset + p]], axis=0)
            part = matmul(turned[p], whole).astype(BF16)
            for k in range(basis):
                cycle_rows[k, p * cols : (p + 1) * cols, :] = part[k * cols : (k + 1) * cols]
        for k in range(basis):
            part = matmul(cycle_rows[k], mix[k * chans : (k + 1) * chans, :]).astype(BF16)
            mixed_rows[k * polar : (k + 1) * polar] = part.reshape(polar, cols, chans)
        of_basis = lane // (polar * BLOCK)
        step = base + offset + lax.rem(lane // BLOCK, polar) - first
        at_start = lax.rem(lane, BLOCK) == 0
        terms = []
        for t in range(band):
            value = spread[t][0]
            for k in range(1, basis):
                value = jnp.where(of_basis == k, spread[t][k], value)
            terms.append(((step == t) & (count > t) & at_start, value))
        line = chosen(terms)
        weights = jnp.concatenate(
            [staircase(line[i : i + 1], BLOCK) for i in range(rows)], axis=0
        )
        for b in range(cols // BLOCK):
            at = slice(BLOCK * b, BLOCK * (b + 1))
            cells = mixed_rows[:, at, :].reshape(-1, chans)
            acc[:, at, :] = acc[:, at, :] + matmul(weights, cells).reshape(rows, BLOCK, chans)


def side_rows(side, halo, edges, weights, acc, mix, ext, hidden, present, result):
    half, cols, chans = result.shape
    basis = mix.shape[0] // chans
    reach = edges.shape[1] // 2
    rows = pl.ds(side * half, half)

    @pl.when(present)
    def arrived():
        pad = jnp.zeros((ext.shape[1] - cols - 2 * reach, chans), BF16)
        for p in range(HALO):
            edge = edges[p]
            ext[p] = jnp.concatenate([edge[reach:], halo[p], edge[:reach], pad], axis=0)
        groups = [(i, k) for k in range(basis) for i in range(half)]
        window_products(weights.at[side], ext, hidden, groups, cols, chans)
        total = matmul(hidden[...], mix[...]).reshape(half, cols, chans)
        result[...] = (total + acc[rows]).astype(BF16)

    @pl.when(jnp.logical_not(present))
    def absent():
        result[...] = acc[rows].astype(BF16)


def from_side(which):
    core = lax.axis_index("lon")
    side = 1 - core if which == 0 else core
    lat_pos = lax.axis_index("lat")
    last = lax.axis_size("lat") - 1
    present = jnp.where(side == 0, lat_pos != 0, lat_pos != last)
    return side, present


def early_kernel(halo, edges, weights, acc, mix, result, ext, hidden):
    side, present = from_side(0)
    side_rows(side, halo, edges, weights, acc, mix, ext, hidden, present, result)


def late_kernel(early, halo, edges, weights, acc, mix, out, ext, hidden, result, sems):
    half = result.shape[0]
    side, present = from_side(1)
    first = pltpu.make_async_copy(early, out.at[pl.ds((1 - side) * half, half)], sems.at[0])
    first.start()
    side_rows(side, halo, edges, weights, acc, mix, ext, hidden, present, result)
    second = pltpu.make_async_copy(result, out.at[pl.ds(side * half, half)], sems.at[1])
    second.start()
    first.wait()
    second.wait()


def shards(fields, lon_taps, lat_taps, cycle_taps, band_start, band_width, mixing):
    rows, cols, chans = fields.shape
    row_total, basis, taps = lon_taps.shape
    band = lat_taps.shape[2]
    reach = (taps - 1) // 2
    polar = cycle_taps.shape[1] // 2
    cycle = cycle_taps.shape[2]
    lat_count = lax.axis_size("lat")
    core = lax.axis_index("lon")
    axes = ("lat", "lon")
    assert cycle == 2 * cols and rows == 2 * HALO and basis * polar * BLOCK == rows * SPAN
    ahead, back = ring(lat_count, 1), ring(lat_count, -1)
    other = lax.ppermute(fields, "lon", SWAP)
    head, tail = fields[:HALO], fields[rows - HALO :]
    second = lax.ppermute(jnp.where(core == 0, head, tail), axes, back)
    first = lax.ppermute(jnp.where(core == 0, tail, head), axes, ahead)
    edges = jnp.concatenate([other[:, :reach], other[:, cols - reach :]], axis=1)
    head, tail = edges[:HALO], edges[rows - HALO :]
    second_edges = lax.ppermute(jnp.where(core == 0, head, tail), axes, back)
    first_edges = lax.ppermute(jnp.where(core == 0, tail, head), axes, ahead)

    vmem = pl.BlockSpec(memory_space=pltpu.VMEM)
    hbm = pl.BlockSpec(memory_space=pltpu.HBM)
    sds = jax.ShapeDtypeStruct
    group = basis * rows * BLOCK
    ext_cols = cols + SPAN - BLOCK
    acc, halo_weights, mix = pl.pallas_call(
        own_kernel,
        out_shape=(
            sds((rows, cols, chans), F32),
            sds((2, group // 2, HALO * SPAN), BF16),
            sds((basis * chans, chans), BF16),
        ),
        in_specs=[hbm] * 7 + [vmem],
        out_specs=(vmem, vmem, vmem),
        scratch_shapes=[
            pltpu.SMEM((rows,), jnp.int32),
            pltpu.SMEM((rows,), jnp.int32),
            pltpu.VMEM((taps, basis, row_total), F32),
            pltpu.VMEM((band, basis, rows), BF16),
            pltpu.VMEM((rows, cols, chans), BF16),
            pltpu.VMEM((basis, 2 * polar, cycle), BF16),
            pltpu.VMEM((128, -(-row_total // 128) * 128), F32),
            pltpu.VMEM((128, 128), F32),
            pltpu.VMEM((group, rows * SPAN), BF16),
            pltpu.VMEM((rows, ext_cols, chans), BF16),
            pltpu.VMEM((rows * cols, basis * chans), BF16),
            pltpu.VMEM((polar, basis * cols, cycle), BF16),
            pltpu.VMEM((basis, polar * cols, chans), BF16),
            pltpu.VMEM((basis * polar, cols, chans), BF16),
            pltpu.SemaphoreType.DMA((7,)),
        ],
        compiler_params=pltpu.CompilerParams(vmem_limit_bytes=32 * 1024 * 1024),
        cost_estimate=pl.CostEstimate(
            flops=2_000_000_000, bytes_accessed=6_000_000, transcendentals=0
        ),
        name="own_rows",
    )(
        *(
            pltpu.with_memory_space_constraint(x, pltpu.HBM)
            for x in (
                band_start, band_width, jnp.transpose(lon_taps, (2, 1, 0)),
                jnp.transpose(lat_taps, (2, 1, 0)), fields, cycle_taps,
                mixing.reshape(basis * chans, chans),
            )
        ),
        other,
    )

    half = rows // 2
    scratch = [
        pltpu.VMEM((HALO, ext_cols, chans), BF16),
        pltpu.VMEM((half * cols, basis * chans), BF16),
    ]
    limit = pltpu.CompilerParams(vmem_limit_bytes=32 * 1024 * 1024)
    second, second_edges, acc = lax.optimization_barrier((second, second_edges, acc))
    early = pl.pallas_call(
        early_kernel,
        out_shape=sds((half, cols, chans), BF16),
        in_specs=[vmem] * 5,
        out_specs=vmem,
        scratch_shapes=scratch,
        compiler_params=limit,
        cost_estimate=pl.CostEstimate(
            flops=300_000_000, bytes_accessed=1_000_000, transcendentals=0
        ),
        name="early_side",
    )(second, second_edges, halo_weights, acc, mix)
    first, first_edges, early = lax.optimization_barrier((first, first_edges, early))
    return pl.pallas_call(
        late_kernel,
        out_shape=sds((rows, cols, chans), BF16),
        in_specs=[vmem] * 6,
        out_specs=hbm,
        scratch_shapes=[
            *scratch,
            pltpu.VMEM((half, cols, chans), BF16),
            pltpu.SemaphoreType.DMA((2,)),
        ],
        compiler_params=limit,
        name="late_side",
    )(early, first, first_edges, halo_weights, acc, mix)


def solution(mesh):
    in_specs = (
        P(("ens", "lat"), "lon", None),
        P(),
        P("lat", None, None),
        P(),
        P("lat"),
        P("lat"),
        P(),
    )
    out_specs = P(("ens", "lat"), "lon", None)
    return jax.shard_map(shards, mesh=mesh, in_specs=in_specs, out_specs=out_specs, check_vma=False)
```

```python
import jax
import jax.numpy as jnp
from jax import lax
from jax.experimental import pallas as pl
from jax.experimental.pallas import tpu as pltpu
from jax.sharding import PartitionSpec as P

HALO = 4
BLOCK = 16
SPAN = 32
SWAP = [(0, 1), (1, 0)]
F32, BF16 = jnp.float32, jnp.bfloat16


def ring(lat_count, step):
    pairs = []
    for lat in range(lat_count):
        for core in range(2):
            to = lat + (step if core == 0 else -step)
            if 0 <= to < lat_count:
                pairs.append((lat * 2 + core, to * 2 + core))
            else:
                pairs.append((lat * 2 + core, lat * 2 + 1 - core))
    return pairs


def matmul(a, b):
    return jnp.dot(a, b, preferred_element_type=F32)


def staircase(line, steps):
    wide = jnp.broadcast_to(line, (steps, line.shape[1]))
    return pltpu.roll(wide, 0, 1, stride=1, stride_axis=0).astype(BF16)


def chosen(terms):
    total = None
    for mask, value in terms:
        term = jnp.where(mask, value, 0.0)
        total = term if total is None else total + term
    return total


def window_products(weights, cells, hidden, groups, width, offset, chans):
    part = matmul(weights[...], cells.reshape(-1, chans)).astype(BF16)
    for n, (i, k) in enumerate(groups):
        at = i * width + offset
        hidden[at : at + BLOCK, k * chans : (k + 1) * chans] = part[n * BLOCK : (n + 1) * BLOCK]


def weight_kernel(
    start_in, width_in, lon_in, lat_in, fields_in, cycle_in, mixing_in,
    halo_weights, own_weights, polar_weights, cycle_taps, fields, mix,
    start, width, lon, lat, lon_wide, lat_wide, sems,
):
    rows, cols, chans = fields.shape
    taps, basis, row_total = lon.shape
    band = lat.shape[0]
    polar = cycle_taps.shape[1] // 2
    lat_pos = lax.axis_index("lat")
    base = lat_pos * rows
    at_top = base == 0

    copies = []
    for n, (source, target) in enumerate(
        [
            (lon_in, lon), (lat_in, lat), (start_in, start), (width_in, width),
            (fields_in, fields), (cycle_in, cycle_taps), (mixing_in, mix),
        ]
    ):
        copies.append(pltpu.make_async_copy(source, target, sems.at[n]))
        copies[-1].start()
    lon_wide[...] = jnp.zeros_like(lon_wide)
    lat_wide[...] = jnp.zeros_like(lat_wide)
    for n in range(4):
        copies[n].wait()

    for d in range(taps):
        for k in range(basis):
            lon_wide[k * 16 + d : k * 16 + d + 1, 0:row_total] = lon[d, k : k + 1, :]
    lanes = lon_wide.shape[1]
    slots = pltpu.roll(lon_wide[...], lax.rem(lanes + HALO - base, lanes), 1)[:, :128]
    slots = jnp.transpose(slots)[: rows + 2 * HALO]
    is_tap = lax.broadcasted_iota(jnp.int32, slots.shape, 1) < taps
    own_taps, halo_taps = [], []
    for k in range(basis):
        moved = slots if k == 0 else pltpu.roll(slots, 128 - 16 * k, 1)
        moved = jnp.where(is_tap, moved, 0.0)
        for _ in range(2):
            moved = pltpu.roll(moved, 0, 1, stride=SPAN // 2, stride_axis=0)
        quads = [jnp.sum(moved[4 * q : 4 * q + 4], axis=0, keepdims=True) for q in range(4)]
        own_taps.append(jnp.concatenate([quads[1], quads[2]], axis=1))
        halo_taps.append(jnp.concatenate([quads[0], quads[3]], axis=1))

    for t in range(band):
        lat_wide[t * basis : (t + 1) * basis, 0:rows] = lat[t].astype(F32)
    lat_cols = jnp.transpose(lat_wide[...])[:rows]
    shape = (rows, rows * SPAN)
    lane = lax.broadcasted_iota(jnp.int32, shape, 1)
    out_row = lax.broadcasted_iota(jnp.int32, shape, 0)
    first = jnp.zeros(shape, jnp.int32)
    count = jnp.zeros(shape, jnp.int32)
    for i in range(rows):
        first = jnp.where(out_row == i, start[i], first)
        count = jnp.where(out_row == i, width[i], count)
    spread = [
        [
            jnp.broadcast_to(lat_cols[:, t * basis + k : t * basis + k + 1], shape)
            for k in range(basis)
        ]
        for t in range(band)
    ]
    slot = lane // SPAN
    own_row = base + slot
    halo_row = jnp.where(slot < HALO, own_row - HALO, own_row + rows - HALO)
    is_polar = (own_row < polar) | (own_row >= row_total - polar)
    in_grid = (halo_row >= 0) & (halo_row < row_total)
    own_step, halo_step = own_row - first, halo_row - first
    own_used = [(own_step == t) & (count > t) & ~is_polar for t in range(band)]
    halo_used = [(halo_step == t) & (count > t) & in_grid for t in range(band)]
    for k in range(basis):
        own_line = own_taps[k] * chosen([(own_used[t], spread[t][k]) for t in range(band)])
        halo_line = halo_taps[k] * chosen([(halo_used[t], spread[t][k]) for t in range(band)])
        for i in range(rows):
            at = (k * rows + i) * BLOCK
            own_weights[at : at + BLOCK, :] = staircase(own_line[i : i + 1], BLOCK)
            side, at = i // HALO, (k * HALO + i % HALO) * BLOCK
            reached = halo_line[i : i + 1, side * HALO * SPAN : (side + 1) * HALO * SPAN]
            halo_weights[side, at : at + BLOCK, :] = staircase(reached, BLOCK)

    offset = jnp.where(at_top, 0, rows - polar)
    of_basis = lane // (polar * BLOCK)
    step = base + offset + lax.rem(lane // BLOCK, polar) - first
    at_start = lax.rem(lane, BLOCK) == 0
    terms = []
    for t in range(band):
        value = spread[t][0]
        for k in range(1, basis):
            value = jnp.where(of_basis == k, spread[t][k], value)
        terms.append(((step == t) & (count > t) & at_start, value))
    line = chosen(terms)
    for i in range(rows):
        polar_weights[i * BLOCK : (i + 1) * BLOCK, :] = staircase(line[i : i + 1], BLOCK)
    for n in range(4, 7):
        copies[n].wait()


def own_kernel(own_weights, cycle_taps, fields, mix, acc, turned, ext, hidden):
    rows, cols, chans = fields.shape
    basis = mix.shape[0] // chans
    polar = cycle_taps.shape[1] // 2
    cycle = cycle_taps.shape[2]
    near = (SPAN - BLOCK) // 4
    lat_pos = lax.axis_index("lat")
    at_top = lat_pos == 0
    at_bottom = lat_pos == lax.axis_size("lat") - 1

    @pl.when(at_top | at_bottom)
    def polar_matrices():
        total = lax.broadcasted_iota(jnp.int32, (cycle, cycle), 0) + lax.broadcasted_iota(
            jnp.int32, (cycle, cycle), 1
        )
        turn = jnp.where((total == 0) | (total == cycle), 1.0, 0.0).astype(BF16)
        negated = matmul(cycle_taps[...].reshape(-1, cycle), turn)
        for p in range(polar):
            for k in range(basis):
                n = k * 2 * polar + p
                line = jnp.where(at_top, negated[n : n + 1], negated[n + polar : n + polar + 1])
                turned[p, k * cols : (k + 1) * cols, :] = staircase(line, cols)

    blank = jnp.zeros((near, chans), BF16)
    pad = jnp.zeros((ext.shape[1] - cols - near, chans), BF16)
    for r in range(rows):
        ext[r] = jnp.concatenate([blank, fields[r], pad], axis=0)
    groups = [(i, k) for k in range(basis) for i in range(rows)]
    inner = cols - 2 * BLOCK
    for at in range(BLOCK, cols - BLOCK, BLOCK):
        window_products(
            own_weights, ext[:, at : at + SPAN, :], hidden, groups, inner, at - BLOCK, chans
        )
    half = rows // 2
    for n in range(2):
        at = slice(n * half, (n + 1) * half)
        total = matmul(hidden[n * half * inner : (n + 1) * half * inner], mix[...])
        acc[at, BLOCK : cols - BLOCK, :] = total.reshape(half, inner, chans) + fields[
            at, BLOCK : cols - BLOCK, :
        ].astype(F32)


def partner_kernel(
    acc_in, own_weights, polar_weights, turned, fields, mix, other,
    acc, hidden, cycle_rows, mixed_rows,
):
    del acc_in
    rows, cols, chans = fields.shape
    polar = turned.shape[0]
    basis = mix.shape[0] // chans
    reach = (SPAN - BLOCK) // 4
    lat_pos = lax.axis_index("lat")
    at_top = lat_pos == 0
    at_bottom = lat_pos == lax.axis_size("lat") - 1
    groups = [(i, k) for k in range(basis) for i in range(rows)]
    left, right = [], []
    pad = jnp.zeros((SPAN - BLOCK - 2 * reach, chans), BF16)
    for r in range(rows):
        left.append(
            jnp.concatenate([other[r, cols - reach :], fields[r, : SPAN - reach]], axis=0)
        )
        right.append(
            jnp.concatenate(
                [fields[r, cols - BLOCK - reach :], other[r, :reach], pad], axis=0
            )
        )
    for n, cells in enumerate((left, right)):
        window_products(
            own_weights, jnp.concatenate(cells, axis=0), hidden, groups, 2 * BLOCK, n * BLOCK,
            chans,
        )
    total = matmul(hidden[...], mix[...]).reshape(rows, 2 * BLOCK, chans)
    for n, at in enumerate((slice(0, BLOCK), slice(cols - BLOCK, cols))):
        acc[:, at, :] = total[:, n * BLOCK : (n + 1) * BLOCK] + fields[:, at, :].astype(F32)

    @pl.when(at_top | at_bottom)
    def polar_part():
        offset = jnp.where(at_top, 0, rows - polar)
        for p in range(polar):
            whole = jnp.concatenate([fields[offset + p], other[offset + p]], axis=0)
            part = matmul(turned[p], whole).astype(BF16)
            for k in range(basis):
                cycle_rows[k, p * cols : (p + 1) * cols, :] = part[k * cols : (k + 1) * cols]
        for k in range(basis):
            part = matmul(cycle_rows[k], mix[k * chans : (k + 1) * chans, :]).astype(BF16)
            mixed_rows[k * polar : (k + 1) * polar] = part.reshape(polar, cols, chans)
        for b in range(cols // BLOCK):
            at = slice(BLOCK * b, BLOCK * (b + 1))
            cells = mixed_rows[:, at, :].reshape(-1, chans)
            acc[:, at, :] = acc[:, at, :] + matmul(polar_weights[...], cells).reshape(
                rows, BLOCK, chans
            )


def side_rows(side, halo, edges, weights, acc, mix, ext, hidden, present, result):
    half, cols, chans = result.shape
    basis = mix.shape[0] // chans
    reach = edges.shape[1] // 2
    rows = pl.ds(side * half, half)

    @pl.when(present)
    def arrived():
        pad = jnp.zeros((ext.shape[1] - cols - 2 * reach, chans), BF16)
        for p in range(HALO):
            edge = edges[p]
            ext[p] = jnp.concatenate([edge[reach:], halo[p], edge[:reach], pad], axis=0)
        groups = [(i, k) for k in range(basis) for i in range(half)]
        for at in range(0, cols, BLOCK):
            window_products(
                weights.at[side], ext[:, at : at + SPAN, :], hidden, groups, cols, at, chans
            )
        total = matmul(hidden[...], mix[...]).reshape(half, cols, chans)
        result[...] = (total + acc[rows]).astype(BF16)

    @pl.when(jnp.logical_not(present))
    def absent():
        result[...] = acc[rows].astype(BF16)


def from_side(which):
    core = lax.axis_index("lon")
    side = 1 - core if which == 0 else core
    lat_pos = lax.axis_index("lat")
    last = lax.axis_size("lat") - 1
    present = jnp.where(side == 0, lat_pos != 0, lat_pos != last)
    return side, present


def early_kernel(halo, edges, weights, acc, mix, result, ext, hidden):
    side, present = from_side(0)
    side_rows(side, halo, edges, weights, acc, mix, ext, hidden, present, result)


def late_kernel(early, halo, edges, weights, acc, mix, out, ext, hidden, result, sems):
    half = result.shape[0]
    side, present = from_side(1)
    first = pltpu.make_async_copy(early, out.at[pl.ds((1 - side) * half, half)], sems.at[0])
    first.start()
    side_rows(side, halo, edges, weights, acc, mix, ext, hidden, present, result)
    second = pltpu.make_async_copy(result, out.at[pl.ds(side * half, half)], sems.at[1])
    second.start()
    first.wait()
    second.wait()


def shards(fields, lon_taps, lat_taps, cycle_taps, band_start, band_width, mixing):
    rows, cols, chans = fields.shape
    row_total, basis, taps = lon_taps.shape
    band = lat_taps.shape[2]
    reach = (taps - 1) // 2
    polar = cycle_taps.shape[1] // 2
    cycle = cycle_taps.shape[2]
    lat_count = lax.axis_size("lat")
    core = lax.axis_index("lon")
    axes = ("lat", "lon")
    assert cycle == 2 * cols and rows == 2 * HALO and basis * polar * BLOCK == rows * SPAN
    assert reach == (SPAN - BLOCK) // 4
    ahead, back = ring(lat_count, 1), ring(lat_count, -1)
    head, tail = fields[:HALO], fields[rows - HALO :]
    down = jnp.where(core == 0, head, tail)
    up = jnp.where(core == 0, tail, head)
    other = lax.ppermute(fields, "lon", SWAP)
    second = lax.ppermute(down, axes, back)
    down, band_start = lax.optimization_barrier((down, band_start))

    vmem = pl.BlockSpec(memory_space=pltpu.VMEM)
    hbm = pl.BlockSpec(memory_space=pltpu.HBM)
    sds = jax.ShapeDtypeStruct
    group = basis * rows * BLOCK
    ext_cols = cols + SPAN - BLOCK
    limit = pltpu.CompilerParams(vmem_limit_bytes=32 * 1024 * 1024)
    halo_weights, own_weights, polar_weights, turns, whole, mix = pl.pallas_call(
        weight_kernel,
        out_shape=(
            sds((2, group // 2, HALO * SPAN), BF16),
            sds((group, rows * SPAN), BF16),
            sds((rows * BLOCK, rows * SPAN), BF16),
            sds((basis, 2 * polar, cycle), BF16),
            sds((rows, cols, chans), BF16),
            sds((basis * chans, chans), BF16),
        ),
        in_specs=[hbm] * 7,
        out_specs=[vmem] * 6,
        scratch_shapes=[
            pltpu.SMEM((rows,), jnp.int32),
            pltpu.SMEM((rows,), jnp.int32),
            pltpu.VMEM((taps, basis, row_total), F32),
            pltpu.VMEM((band, basis, rows), BF16),
            pltpu.VMEM((128, -(-row_total // 128) * 128), F32),
            pltpu.VMEM((128, 128), F32),
            pltpu.SemaphoreType.DMA((7,)),
        ],
        compiler_params=limit,
        cost_estimate=pl.CostEstimate(
            flops=100_000, bytes_accessed=1_000, transcendentals=0
        ),
        name="filter_weights",
    )(
        *(
            pltpu.with_memory_space_constraint(x, pltpu.HBM)
            for x in (
                band_start, band_width, jnp.transpose(lon_taps, (2, 1, 0)),
                jnp.transpose(lat_taps, (2, 1, 0)), fields, cycle_taps,
                mixing.reshape(basis * chans, chans),
            )
        ),
    )
    edges = jnp.concatenate([other[:, :reach], other[:, cols - reach :]], axis=1)
    head, tail = edges[:HALO], edges[rows - HALO :]
    second_edges = lax.ppermute(jnp.where(core == 0, head, tail), axes, back)
    up, own_weights = lax.optimization_barrier((up, own_weights))
    first = lax.ppermute(up, axes, ahead)
    first_edges = lax.ppermute(jnp.where(core == 0, tail, head), axes, ahead)
    acc, turned = pl.pallas_call(
        own_kernel,
        out_shape=(
            sds((rows, cols, chans), F32),
            sds((polar, basis * cols, cycle), BF16),
        ),
        in_specs=[vmem] * 4,
        out_specs=(vmem, vmem),
        scratch_shapes=[
            pltpu.VMEM((rows, ext_cols, chans), BF16),
            pltpu.VMEM((rows * (cols - 2 * BLOCK), basis * chans), BF16),
        ],
        compiler_params=limit,
        cost_estimate=pl.CostEstimate(
            flops=100_000, bytes_accessed=1_000, transcendentals=0
        ),
        name="own_rows",
    )(own_weights, turns, whole, mix)

    acc = pl.pallas_call(
        partner_kernel,
        out_shape=sds((rows, cols, chans), F32),
        in_specs=[vmem] * 7,
        out_specs=vmem,
        input_output_aliases={0: 0},
        scratch_shapes=[
            pltpu.VMEM((rows * 2 * BLOCK, basis * chans), BF16),
            pltpu.VMEM((basis, polar * cols, chans), BF16),
            pltpu.VMEM((basis * polar, cols, chans), BF16),
        ],
        compiler_params=limit,
        cost_estimate=pl.CostEstimate(
            flops=100_000, bytes_accessed=1_000, transcendentals=0
        ),
        name="partner_columns",
    )(acc, own_weights, polar_weights, turned, whole, mix, other)

    half = rows // 2
    scratch = [
        pltpu.VMEM((HALO, ext_cols, chans), BF16),
        pltpu.VMEM((half * cols, basis * chans), BF16),
    ]
    limit = pltpu.CompilerParams(vmem_limit_bytes=32 * 1024 * 1024)
    second, second_edges, acc = lax.optimization_barrier((second, second_edges, acc))
    early = pl.pallas_call(
        early_kernel,
        out_shape=sds((half, cols, chans), BF16),
        in_specs=[vmem] * 5,
        out_specs=vmem,
        scratch_shapes=scratch,
        compiler_params=limit,
        cost_estimate=pl.CostEstimate(
            flops=300_000_000, bytes_accessed=1_000_000, transcendentals=0
        ),
        name="early_side",
    )(second, second_edges, halo_weights, acc, mix)
    first, first_edges, early = lax.optimization_barrier((first, first_edges, early))
    return pl.pallas_call(
        late_kernel,
        out_shape=sds((rows, cols, chans), BF16),
        in_specs=[vmem] * 6,
        out_specs=hbm,
        scratch_shapes=[
            *scratch,
            pltpu.VMEM((half, cols, chans), BF16),
            pltpu.SemaphoreType.DMA((2,)),
        ],
        compiler_params=limit,
        name="late_side",
    )(early, first, first_edges, halo_weights, acc, mix)


def solution(mesh):
    in_specs = (
        P(("ens", "lat"), "lon", None),
        P(),
        P("lat", None, None),
        P(),
        P("lat"),
        P("lat"),
        P(),
    )
    out_specs = P(("ens", "lat"), "lon", None)
    return jax.shard_map(shards, mesh=mesh, in_specs=in_specs, out_specs=out_specs, check_vma=False)
```

```python
import jax
import jax.numpy as jnp
from jax import lax
from jax.experimental import pallas as pl
from jax.experimental.pallas import tpu as pltpu
from jax.sharding import PartitionSpec as P

HALO = 4
BLOCK = 16
SPAN = 32
SWAP = [(0, 1), (1, 0)]
F32, BF16 = jnp.float32, jnp.bfloat16


def ring(lat_count, step):
    pairs = []
    for lat in range(lat_count):
        for core in range(2):
            to = lat + (step if core == 0 else -step)
            if 0 <= to < lat_count:
                pairs.append((lat * 2 + core, to * 2 + core))
            else:
                pairs.append((lat * 2 + core, lat * 2 + 1 - core))
    return pairs


def matmul(a, b):
    return jnp.dot(a, b, preferred_element_type=F32)


def staircase(line, steps):
    wide = jnp.broadcast_to(line, (steps, line.shape[1]))
    return pltpu.roll(wide, 0, 1, stride=1, stride_axis=0).astype(BF16)


def chosen(terms):
    total = None
    for mask, value in terms:
        term = jnp.where(mask, value, 0.0)
        total = term if total is None else total + term
    return total


def window_products(weights, cells, hidden, groups, width, offset, chans):
    part = matmul(weights[...], cells.reshape(-1, chans)).astype(BF16)
    for n, (i, k) in enumerate(groups):
        at = i * width + offset
        hidden[at : at + BLOCK, k * chans : (k + 1) * chans] = part[n * BLOCK : (n + 1) * BLOCK]


def polar_matrices(cycle_taps, turned, at_top):
    basis, twice, cycle = cycle_taps.shape
    polar = twice // 2
    cols = turned.shape[1] // basis
    total = lax.broadcasted_iota(jnp.int32, (cycle, cycle), 0) + lax.broadcasted_iota(
        jnp.int32, (cycle, cycle), 1
    )
    turn = jnp.where((total == 0) | (total == cycle), 1.0, 0.0).astype(BF16)
    negated = matmul(cycle_taps[...].reshape(-1, cycle), turn)
    for p in range(polar):
        for k in range(basis):
            n = k * twice + (p if at_top else p + polar)
            turned[p, k * cols : (k + 1) * cols, :] = staircase(negated[n : n + 1], cols)


def fetch_kernel(
    start_in, width_in, lon_in, lat_in, cycle_in, fields_in, mixing_in,
    start, width, lon, lat, cycle_taps, fields, mix, turned, sems,
):
    copies = []
    for n, (source, target) in enumerate(
        [
            (cycle_in, cycle_taps), (lon_in, lon), (lat_in, lat), (start_in, start),
            (width_in, width), (fields_in, fields), (mixing_in, mix),
        ]
    ):
        copies.append(pltpu.make_async_copy(source, target, sems.at[n]))
        copies[-1].start()
    copies[0].wait()

    @pl.when(lax.axis_index("lat") == 0)
    def top():
        polar_matrices(cycle_taps, turned, True)

    for copy in copies[1:]:
        copy.wait()


def weight_kernel(
    start, width, lon, lat, cycle_taps, halo_weights, own_weights, polar_weights,
    lon_wide, lat_wide,
):
    rows = halo_weights.shape[0] * HALO
    taps, basis, row_total = lon.shape
    band = lat.shape[0]
    polar = cycle_taps.shape[1] // 2
    base = lax.axis_index("lat") * rows
    at_top = base == 0
    lon_wide[...] = jnp.zeros_like(lon_wide)
    lat_wide[...] = jnp.zeros_like(lat_wide)

    for d in range(taps):
        for k in range(basis):
            lon_wide[k * 16 + d : k * 16 + d + 1, 0:row_total] = lon[d, k : k + 1, :]
    lanes = lon_wide.shape[1]
    slots = pltpu.roll(lon_wide[...], lax.rem(lanes + HALO - base, lanes), 1)[:, :128]
    slots = jnp.transpose(slots)[: rows + 2 * HALO]
    is_tap = lax.broadcasted_iota(jnp.int32, slots.shape, 1) < taps
    own_taps, halo_taps = [], []
    for k in range(basis):
        moved = slots if k == 0 else pltpu.roll(slots, 128 - 16 * k, 1)
        moved = jnp.where(is_tap, moved, 0.0)
        for _ in range(2):
            moved = pltpu.roll(moved, 0, 1, stride=SPAN // 2, stride_axis=0)
        quads = [jnp.sum(moved[4 * q : 4 * q + 4], axis=0, keepdims=True) for q in range(4)]
        own_taps.append(jnp.concatenate([quads[1], quads[2]], axis=1))
        halo_taps.append(jnp.concatenate([quads[0], quads[3]], axis=1))

    for t in range(band):
        lat_wide[t * basis : (t + 1) * basis, 0:rows] = lat[t].astype(F32)
    at = band * basis
    lat_wide[at : at + 1, 0:rows] = start[...].reshape(1, rows).astype(F32)
    lat_wide[at + 1 : at + 2, 0:rows] = width[...].reshape(1, rows).astype(F32)
    lat_cols = jnp.transpose(lat_wide[...])[:rows]
    shape = (rows, rows * SPAN)
    lane = lax.broadcasted_iota(jnp.int32, shape, 1)
    first = jnp.broadcast_to(lat_cols[:, at : at + 1], shape).astype(jnp.int32)
    count = jnp.broadcast_to(lat_cols[:, at + 1 : at + 2], shape).astype(jnp.int32)
    spread = [
        [
            jnp.broadcast_to(lat_cols[:, t * basis + k : t * basis + k + 1], shape)
            for k in range(basis)
        ]
        for t in range(band)
    ]
    slot = lane // SPAN
    own_row = base + slot
    halo_row = jnp.where(slot < HALO, own_row - HALO, own_row + rows - HALO)
    is_polar = (own_row < polar) | (own_row >= row_total - polar)
    in_grid = (halo_row >= 0) & (halo_row < row_total)
    own_step, halo_step = own_row - first, halo_row - first
    own_used = [(own_step == t) & (count > t) & ~is_polar for t in range(band)]
    halo_used = [(halo_step == t) & (count > t) & in_grid for t in range(band)]
    for k in range(basis):
        own_line = own_taps[k] * chosen([(own_used[t], spread[t][k]) for t in range(band)])
        halo_line = halo_taps[k] * chosen([(halo_used[t], spread[t][k]) for t in range(band)])
        for i in range(rows):
            at = (k * rows + i) * BLOCK
            own_weights[at : at + BLOCK, :] = staircase(own_line[i : i + 1], BLOCK)
            side, at = i // HALO, (k * HALO + i % HALO) * BLOCK
            reached = halo_line[i : i + 1, side * HALO * SPAN : (side + 1) * HALO * SPAN]
            halo_weights[side, at : at + BLOCK, :] = staircase(reached, BLOCK)

    offset = jnp.where(at_top, 0, rows - polar)
    of_basis = lane // (polar * BLOCK)
    step = base + offset + lax.rem(lane // BLOCK, polar) - first
    at_start = lax.rem(lane, BLOCK) == 0
    terms = []
    for t in range(band):
        value = spread[t][0]
        for k in range(1, basis):
            value = jnp.where(of_basis == k, spread[t][k], value)
        terms.append(((step == t) & (count > t) & at_start, value))
    line = chosen(terms)
    for i in range(rows):
        polar_weights[i * BLOCK : (i + 1) * BLOCK, :] = staircase(line[i : i + 1], BLOCK)


def own_kernel(own_weights, fields, mix, acc, ext, hidden):
    rows, cols, chans = fields.shape
    basis = mix.shape[0] // chans
    near = (SPAN - BLOCK) // 4
    blank = jnp.zeros((near, chans), BF16)
    pad = jnp.zeros((ext.shape[1] - cols - near, chans), BF16)
    for r in range(rows):
        ext[r] = jnp.concatenate([blank, fields[r], pad], axis=0)
    groups = [(i, k) for k in range(basis) for i in range(rows)]
    inner = cols - 2 * BLOCK
    for at in range(BLOCK, cols - BLOCK, BLOCK):
        window_products(
            own_weights, ext[:, at : at + SPAN, :], hidden, groups, inner, at - BLOCK, chans
        )
    half = rows // 2
    for n in range(2):
        at = slice(n * half, (n + 1) * half)
        total = matmul(hidden[n * half * inner : (n + 1) * half * inner], mix[...])
        acc[at, BLOCK : cols - BLOCK, :] = total.reshape(half, inner, chans) + fields[
            at, BLOCK : cols - BLOCK, :
        ].astype(F32)


def partner_kernel(
    acc_in, turned_in, own_weights, polar_weights, cycle_taps, fields, mix, other,
    acc, turned, hidden, cycle_rows, mixed_rows,
):
    del acc_in, turned_in
    rows, cols, chans = fields.shape
    polar = turned.shape[0]
    basis = mix.shape[0] // chans
    reach = (SPAN - BLOCK) // 4
    lat_pos = lax.axis_index("lat")
    at_top = lat_pos == 0
    at_bottom = lat_pos == lax.axis_size("lat") - 1
    groups = [(i, k) for k in range(basis) for i in range(rows)]
    left, right = [], []
    pad = jnp.zeros((SPAN - BLOCK - 2 * reach, chans), BF16)
    for r in range(rows):
        left.append(
            jnp.concatenate([other[r, cols - reach :], fields[r, : SPAN - reach]], axis=0)
        )
        right.append(
            jnp.concatenate(
                [fields[r, cols - BLOCK - reach :], other[r, :reach], pad], axis=0
            )
        )
    for n, cells in enumerate((left, right)):
        window_products(
            own_weights, jnp.concatenate(cells, axis=0), hidden, groups, 2 * BLOCK, n * BLOCK,
            chans,
        )
    total = matmul(hidden[...], mix[...]).reshape(rows, 2 * BLOCK, chans)
    for n, at in enumerate((slice(0, BLOCK), slice(cols - BLOCK, cols))):
        acc[:, at, :] = total[:, n * BLOCK : (n + 1) * BLOCK] + fields[:, at, :].astype(F32)

    @pl.when(at_bottom)
    def bottom():
        polar_matrices(cycle_taps, turned, False)

    @pl.when(at_top | at_bottom)
    def polar_part():
        offset = jnp.where(at_top, 0, rows - polar)
        for p in range(polar):
            whole = jnp.concatenate([fields[offset + p], other[offset + p]], axis=0)
            part = matmul(turned[p], whole).astype(BF16)
            for k in range(basis):
                cycle_rows[k, p * cols : (p + 1) * cols, :] = part[k * cols : (k + 1) * cols]
        for k in range(basis):
            part = matmul(cycle_rows[k], mix[k * chans : (k + 1) * chans, :]).astype(BF16)
            mixed_rows[k * polar : (k + 1) * polar] = part.reshape(polar, cols, chans)
        for b in range(cols // BLOCK):
            at = slice(BLOCK * b, BLOCK * (b + 1))
            cells = mixed_rows[:, at, :].reshape(-1, chans)
            acc[:, at, :] = acc[:, at, :] + matmul(polar_weights[...], cells).reshape(
                rows, BLOCK, chans
            )


def side_rows(side, halo, edges, weights, acc, mix, ext, hidden, present, result):
    half, cols, chans = result.shape
    basis = mix.shape[0] // chans
    reach = edges.shape[1] // 2
    rows = pl.ds(side * half, half)

    @pl.when(present)
    def arrived():
        pad = jnp.zeros((ext.shape[1] - cols - 2 * reach, chans), BF16)
        for p in range(HALO):
            edge = edges[p]
            ext[p] = jnp.concatenate([edge[reach:], halo[p], edge[:reach], pad], axis=0)
        groups = [(i, k) for k in range(basis) for i in range(half)]
        wide = cols // 2
        for n in range(2):
            for at in range(0, wide, BLOCK):
                cells = ext[:, n * wide + at : n * wide + at + SPAN, :]
                window_products(
                    weights.at[side], cells, hidden.at[n], groups, wide, at, chans
                )
        for n in range(2):
            total = matmul(hidden[n], mix[...]).reshape(half, wide, chans)
            at = slice(n * wide, (n + 1) * wide)
            result[:, at, :] = (total + acc[rows, at, :]).astype(BF16)

    @pl.when(jnp.logical_not(present))
    def absent():
        result[...] = acc[rows].astype(BF16)


def from_side(which):
    core = lax.axis_index("lon")
    side = 1 - core if which == 0 else core
    lat_pos = lax.axis_index("lat")
    last = lax.axis_size("lat") - 1
    present = jnp.where(side == 0, lat_pos != 0, lat_pos != last)
    return side, present


def early_kernel(halo, edges, weights, acc, mix, result, ext, hidden):
    side, present = from_side(0)
    side_rows(side, halo, edges, weights, acc, mix, ext, hidden, present, result)


def late_kernel(early, halo, edges, weights, acc, mix, out, ext, hidden, result, sems):
    half = result.shape[0]
    side, present = from_side(1)
    first = pltpu.make_async_copy(early, out.at[pl.ds((1 - side) * half, half)], sems.at[0])
    first.start()
    side_rows(side, halo, edges, weights, acc, mix, ext, hidden, present, result)
    second = pltpu.make_async_copy(result, out.at[pl.ds(side * half, half)], sems.at[1])
    second.start()
    first.wait()
    second.wait()


def shards(fields, lon_taps, lat_taps, cycle_taps, band_start, band_width, mixing):
    rows, cols, chans = fields.shape
    row_total, basis, taps = lon_taps.shape
    band = lat_taps.shape[2]
    reach = (taps - 1) // 2
    polar = cycle_taps.shape[1] // 2
    cycle = cycle_taps.shape[2]
    lat_count = lax.axis_size("lat")
    core = lax.axis_index("lon")
    axes = ("lat", "lon")
    assert cycle == 2 * cols and rows == 2 * HALO and basis * polar * BLOCK == rows * SPAN
    assert reach == (SPAN - BLOCK) // 4
    ahead, back = ring(lat_count, 1), ring(lat_count, -1)
    head, tail = fields[:HALO], fields[rows - HALO :]
    down = jnp.where(core == 0, head, tail)
    up = jnp.where(core == 0, tail, head)
    other = lax.ppermute(fields, "lon", SWAP)
    second = lax.ppermute(down, axes, back)
    down, band_start = lax.optimization_barrier((down, band_start))

    vmem = pl.BlockSpec(memory_space=pltpu.VMEM)
    hbm = pl.BlockSpec(memory_space=pltpu.HBM)
    sds = jax.ShapeDtypeStruct
    group = basis * rows * BLOCK
    ext_cols = cols + SPAN - BLOCK
    limit = pltpu.CompilerParams(vmem_limit_bytes=32 * 1024 * 1024)
    small = pl.CostEstimate(flops=100_000, bytes_accessed=1_000, transcendentals=0)
    start, width, lon, lat, turns, whole, mix, turned = pl.pallas_call(
        fetch_kernel,
        out_shape=(
            sds((rows,), jnp.int32),
            sds((rows,), jnp.int32),
            sds((taps, basis, row_total), F32),
            sds((band, basis, rows), BF16),
            sds((basis, 2 * polar, cycle), BF16),
            sds((rows, cols, chans), BF16),
            sds((basis * chans, chans), BF16),
            sds((polar, basis * cols, cycle), BF16),
        ),
        in_specs=[hbm] * 7,
        out_specs=[vmem] * 8,
        scratch_shapes=[pltpu.SemaphoreType.DMA((7,))],
        compiler_params=limit,
        cost_estimate=small,
        name="fetch_operands",
    )(
        *(
            pltpu.with_memory_space_constraint(x, pltpu.HBM)
            for x in (
                band_start, band_width, jnp.transpose(lon_taps, (2, 1, 0)),
                jnp.transpose(lat_taps, (2, 1, 0)), cycle_taps, fields,
                mixing.reshape(basis * chans, chans),
            )
        ),
    )
    up, start = lax.optimization_barrier((up, start))
    first = lax.ppermute(up, axes, ahead)
    halo_weights, own_weights, polar_weights = pl.pallas_call(
        weight_kernel,
        out_shape=(
            sds((2, group // 2, HALO * SPAN), BF16),
            sds((group, rows * SPAN), BF16),
            sds((rows * BLOCK, rows * SPAN), BF16),
        ),
        in_specs=[vmem] * 5,
        out_specs=[vmem] * 3,
        scratch_shapes=[
            pltpu.VMEM((128, -(-row_total // 128) * 128), F32),
            pltpu.VMEM((128, 128), F32),
        ],
        compiler_params=limit,
        cost_estimate=small,
        name="filter_weights",
    )(start, width, lon, lat, turns)

    edges = jnp.concatenate([other[:, :reach], other[:, cols - reach :]], axis=1)
    head, tail = edges[:HALO], edges[rows - HALO :]
    second_edges = lax.ppermute(jnp.where(core == 0, head, tail), axes, back)
    first_edges = lax.ppermute(jnp.where(core == 0, tail, head), axes, ahead)
    acc = pl.pallas_call(
        own_kernel,
        out_shape=sds((rows, cols, chans), F32),
        in_specs=[vmem] * 3,
        out_specs=vmem,
        scratch_shapes=[
            pltpu.VMEM((rows, ext_cols, chans), BF16),
            pltpu.VMEM((rows * (cols - 2 * BLOCK), basis * chans), BF16),
        ],
        compiler_params=limit,
        cost_estimate=small,
        name="own_rows",
    )(own_weights, whole, mix)

    acc, _ = pl.pallas_call(
        partner_kernel,
        out_shape=(
            sds((rows, cols, chans), F32),
            sds((polar, basis * cols, cycle), BF16),
        ),
        in_specs=[vmem] * 8,
        out_specs=(vmem, vmem),
        input_output_aliases={0: 0, 1: 1},
        scratch_shapes=[
            pltpu.VMEM((rows * 2 * BLOCK, basis * chans), BF16),
            pltpu.VMEM((basis, polar * cols, chans), BF16),
            pltpu.VMEM((basis * polar, cols, chans), BF16),
        ],
        compiler_params=limit,
        cost_estimate=small,
        name="partner_columns",
    )(acc, turned, own_weights, polar_weights, turns, whole, mix, other)

    half = rows // 2
    scratch = [
        pltpu.VMEM((HALO, ext_cols, chans), BF16),
        pltpu.VMEM((2, half * cols // 2, basis * chans), BF16),
    ]
    second, second_edges, acc = lax.optimization_barrier((second, second_edges, acc))
    early = pl.pallas_call(
        early_kernel,
        out_shape=sds((half, cols, chans), BF16),
        in_specs=[vmem] * 5,
        out_specs=vmem,
        scratch_shapes=scratch,
        compiler_params=limit,
        cost_estimate=small,
        name="early_side",
    )(second, second_edges, halo_weights, acc, mix)
    first, first_edges, early = lax.optimization_barrier((first, first_edges, early))
    return pl.pallas_call(
        late_kernel,
        out_shape=sds((rows, cols, chans), BF16),
        in_specs=[vmem] * 6,
        out_specs=hbm,
        scratch_shapes=[
            *scratch,
            pltpu.VMEM((half, cols, chans), BF16),
            pltpu.SemaphoreType.DMA((2,)),
        ],
        compiler_params=limit,
        name="late_side",
    )(early, first, first_edges, halo_weights, acc, mix)


def solution(mesh):
    in_specs = (
        P(("ens", "lat"), "lon", None),
        P(),
        P("lat", None, None),
        P(),
        P("lat"),
        P("lat"),
        P(),
    )
    out_specs = P(("ens", "lat"), "lon", None)
    return jax.shard_map(shards, mesh=mesh, in_specs=in_specs, out_specs=out_specs, check_vma=False)
```

```python
import jax
import jax.numpy as jnp
from jax import lax
from jax.experimental import pallas as pl
from jax.experimental.pallas import tpu as pltpu
from jax.sharding import PartitionSpec as P

HALO = 4
BLOCK = 16
SPAN = 32
SWAP = [(0, 1), (1, 0)]
F32, BF16 = jnp.float32, jnp.bfloat16


def ring(lat_count, step):
    pairs = []
    for lat in range(lat_count):
        for core in range(2):
            to = lat + (step if core == 0 else -step)
            if 0 <= to < lat_count:
                pairs.append((lat * 2 + core, to * 2 + core))
            else:
                pairs.append((lat * 2 + core, lat * 2 + 1 - core))
    return pairs


def matmul(a, b):
    return jnp.dot(a, b, preferred_element_type=F32)


def staircase(line, steps):
    wide = jnp.broadcast_to(line, (steps, line.shape[1]))
    return pltpu.roll(wide, 0, 1, stride=1, stride_axis=0).astype(BF16)


def chosen(terms):
    total = None
    for mask, value in terms:
        term = jnp.where(mask, value, 0.0)
        total = term if total is None else total + term
    return total


def window_products(weights, cells, hidden, groups, width, offset, chans):
    part = matmul(weights[...], cells.reshape(-1, chans)).astype(BF16)
    for n, (i, k) in enumerate(groups):
        at = i * width + offset
        hidden[at : at + BLOCK, k * chans : (k + 1) * chans] = part[n * BLOCK : (n + 1) * BLOCK]


def polar_matrices(cycle_taps, turned, at_top):
    basis, twice, cycle = cycle_taps.shape
    polar = twice // 2
    cols = turned.shape[1] // basis
    total = lax.broadcasted_iota(jnp.int32, (cycle, cycle), 0) + lax.broadcasted_iota(
        jnp.int32, (cycle, cycle), 1
    )
    turn = jnp.where((total == 0) | (total == cycle), 1.0, 0.0).astype(BF16)
    negated = matmul(cycle_taps[...].reshape(-1, cycle), turn)
    for p in range(polar):
        for k in range(basis):
            n = k * twice + (p if at_top else p + polar)
            turned[p, k * cols : (k + 1) * cols, :] = staircase(negated[n : n + 1], cols)


def weight_kernel(
    start_in, width_in, lon_in, lat_in, fields_in, cycle_in, mixing_in,
    halo_weights, own_weights, polar_weights, cycle_taps, fields, mix, turned,
    start, width, lon, lat, lon_wide, lat_wide, sems,
):
    rows, cols, chans = fields.shape
    taps, basis, row_total = lon.shape
    band = lat.shape[0]
    polar = cycle_taps.shape[1] // 2
    lat_pos = lax.axis_index("lat")
    base = lat_pos * rows
    at_top = base == 0

    copies = []
    for n, (source, target) in enumerate(
        [
            (lon_in, lon), (lat_in, lat), (start_in, start), (width_in, width),
            (fields_in, fields), (cycle_in, cycle_taps), (mixing_in, mix),
        ]
    ):
        copies.append(pltpu.make_async_copy(source, target, sems.at[n]))
        copies[-1].start()
    lon_wide[...] = jnp.zeros_like(lon_wide)
    lat_wide[...] = jnp.zeros_like(lat_wide)
    for n in range(4):
        copies[n].wait()

    for d in range(taps):
        for k in range(basis):
            lon_wide[k * 16 + d : k * 16 + d + 1, 0:row_total] = lon[d, k : k + 1, :]
    lanes = lon_wide.shape[1]
    slots = pltpu.roll(lon_wide[...], lax.rem(lanes + HALO - base, lanes), 1)[:, :128]
    slots = jnp.transpose(slots)[: rows + 2 * HALO]
    is_tap = lax.broadcasted_iota(jnp.int32, slots.shape, 1) < taps
    own_taps, halo_taps = [], []
    for k in range(basis):
        moved = slots if k == 0 else pltpu.roll(slots, 128 - 16 * k, 1)
        moved = jnp.where(is_tap, moved, 0.0)
        for _ in range(2):
            moved = pltpu.roll(moved, 0, 1, stride=SPAN // 2, stride_axis=0)
        quads = [jnp.sum(moved[4 * q : 4 * q + 4], axis=0, keepdims=True) for q in range(4)]
        own_taps.append(jnp.concatenate([quads[1], quads[2]], axis=1))
        halo_taps.append(jnp.concatenate([quads[0], quads[3]], axis=1))

    for t in range(band):
        lat_wide[t * basis : (t + 1) * basis, 0:rows] = lat[t].astype(F32)
    lat_cols = jnp.transpose(lat_wide[...])[:rows]
    shape = (rows, rows * SPAN)
    lane = lax.broadcasted_iota(jnp.int32, shape, 1)
    out_row = lax.broadcasted_iota(jnp.int32, shape, 0)
    first = jnp.zeros(shape, jnp.int32)
    count = jnp.zeros(shape, jnp.int32)
    for i in range(rows):
        first = jnp.where(out_row == i, start[i], first)
        count = jnp.where(out_row == i, width[i], count)
    spread = [
        [
            jnp.broadcast_to(lat_cols[:, t * basis + k : t * basis + k + 1], shape)
            for k in range(basis)
        ]
        for t in range(band)
    ]
    slot = lane // SPAN
    own_row = base + slot
    halo_row = jnp.where(slot < HALO, own_row - HALO, own_row + rows - HALO)
    is_polar = (own_row < polar) | (own_row >= row_total - polar)
    in_grid = (halo_row >= 0) & (halo_row < row_total)
    own_step, halo_step = own_row - first, halo_row - first
    own_used = [(own_step == t) & (count > t) & ~is_polar for t in range(band)]
    halo_used = [(halo_step == t) & (count > t) & in_grid for t in range(band)]
    for k in range(basis):
        own_line = own_taps[k] * chosen([(own_used[t], spread[t][k]) for t in range(band)])
        halo_line = halo_taps[k] * chosen([(halo_used[t], spread[t][k]) for t in range(band)])
        for i in range(rows):
            at = (k * rows + i) * BLOCK
            own_weights[at : at + BLOCK, :] = staircase(own_line[i : i + 1], BLOCK)
            side, at = i // HALO, (k * HALO + i % HALO) * BLOCK
            reached = halo_line[i : i + 1, side * HALO * SPAN : (side + 1) * HALO * SPAN]
            halo_weights[side, at : at + BLOCK, :] = staircase(reached, BLOCK)

    offset = jnp.where(at_top, 0, rows - polar)
    of_basis = lane // (polar * BLOCK)
    step = base + offset + lax.rem(lane // BLOCK, polar) - first
    at_start = lax.rem(lane, BLOCK) == 0
    terms = []
    for t in range(band):
        value = spread[t][0]
        for k in range(1, basis):
            value = jnp.where(of_basis == k, spread[t][k], value)
        terms.append(((step == t) & (count > t) & at_start, value))
    line = chosen(terms)
    for i in range(rows):
        polar_weights[i * BLOCK : (i + 1) * BLOCK, :] = staircase(line[i : i + 1], BLOCK)
    copies[5].wait()

    @pl.when(at_top)
    def top():
        polar_matrices(cycle_taps, turned, True)

    copies[4].wait()
    copies[6].wait()


def own_kernel(turned_in, own_weights, cycle_taps, fields, mix, acc, turned, ext, hidden):
    del turned_in
    rows, cols, chans = fields.shape
    basis = mix.shape[0] // chans
    near = (SPAN - BLOCK) // 4

    @pl.when(lax.axis_index("lat") == lax.axis_size("lat") - 1)
    def bottom():
        polar_matrices(cycle_taps, turned, False)

    blank = jnp.zeros((near, chans), BF16)
    pad = jnp.zeros((ext.shape[1] - cols - near, chans), BF16)
    for r in range(rows):
        ext[r] = jnp.concatenate([blank, fields[r], pad], axis=0)
    groups = [(i, k) for k in range(basis) for i in range(rows)]
    inner = cols - 2 * BLOCK
    for at in range(BLOCK, cols - BLOCK, BLOCK):
        window_products(
            own_weights, ext[:, at : at + SPAN, :], hidden, groups, inner, at - BLOCK, chans
        )
    half = rows // 2
    for n in range(2):
        at = slice(n * half, (n + 1) * half)
        total = matmul(hidden[n * half * inner : (n + 1) * half * inner], mix[...])
        acc[at, BLOCK : cols - BLOCK, :] = total.reshape(half, inner, chans) + fields[
            at, BLOCK : cols - BLOCK, :
        ].astype(F32)


def partner_kernel(
    acc_in, own_weights, polar_weights, turned, fields, mix, other,
    acc, hidden, cycle_rows, mixed_rows,
):
    del acc_in
    rows, cols, chans = fields.shape
    polar = turned.shape[0]
    basis = mix.shape[0] // chans
    reach = (SPAN - BLOCK) // 4
    lat_pos = lax.axis_index("lat")
    at_top = lat_pos == 0
    at_bottom = lat_pos == lax.axis_size("lat") - 1
    groups = [(i, k) for k in range(basis) for i in range(rows)]
    left, right = [], []
    pad = jnp.zeros((SPAN - BLOCK - 2 * reach, chans), BF16)
    for r in range(rows):
        left.append(
            jnp.concatenate([other[r, cols - reach :], fields[r, : SPAN - reach]], axis=0)
        )
        right.append(
            jnp.concatenate(
                [fields[r, cols - BLOCK - reach :], other[r, :reach], pad], axis=0
            )
        )
    for n, cells in enumerate((left, right)):
        window_products(
            own_weights, jnp.concatenate(cells, axis=0), hidden, groups, 2 * BLOCK, n * BLOCK,
            chans,
        )
    total = matmul(hidden[...], mix[...]).reshape(rows, 2 * BLOCK, chans)
    for n, at in enumerate((slice(0, BLOCK), slice(cols - BLOCK, cols))):
        acc[:, at, :] = total[:, n * BLOCK : (n + 1) * BLOCK] + fields[:, at, :].astype(F32)

    @pl.when(at_top | at_bottom)
    def polar_part():
        offset = jnp.where(at_top, 0, rows - polar)
        for p in range(polar):
            whole = jnp.concatenate([fields[offset + p], other[offset + p]], axis=0)
            part = matmul(turned[p], whole).astype(BF16)
            for k in range(basis):
                cycle_rows[k, p * cols : (p + 1) * cols, :] = part[k * cols : (k + 1) * cols]
        for k in range(basis):
            part = matmul(cycle_rows[k], mix[k * chans : (k + 1) * chans, :]).astype(BF16)
            mixed_rows[k * polar : (k + 1) * polar] = part.reshape(polar, cols, chans)
        for b in range(cols // BLOCK):
            at = slice(BLOCK * b, BLOCK * (b + 1))
            cells = mixed_rows[:, at, :].reshape(-1, chans)
            acc[:, at, :] = acc[:, at, :] + matmul(polar_weights[...], cells).reshape(
                rows, BLOCK, chans
            )


def side_rows(
    side, halo, edges, weights, acc, mix, ext, hidden, present, result, ready=lambda at: None
):
    half, cols, chans = result.shape
    basis = mix.shape[0] // chans
    reach = edges.shape[1] // 2
    rows = pl.ds(side * half, half)
    wide = cols // 2
    parts = [slice(n * wide, (n + 1) * wide) for n in range(2)]

    @pl.when(present)
    def arrived():
        pad = jnp.zeros((ext.shape[1] - cols - 2 * reach, chans), BF16)
        for p in range(HALO):
            edge = edges[p]
            ext[p] = jnp.concatenate([edge[reach:], halo[p], edge[:reach], pad], axis=0)
        groups = [(i, k) for k in range(basis) for i in range(half)]
        for n, part in enumerate(parts):
            for at in range(0, wide, BLOCK):
                cells = ext[:, part.start + at : part.start + at + SPAN, :]
                window_products(
                    weights.at[side], cells, hidden.at[n], groups, wide, at, chans
                )
        for n, part in enumerate(parts):
            total = matmul(hidden[n], mix[...]).reshape(half, wide, chans)
            result[:, part, :] = (total + acc[rows, part, :]).astype(BF16)
            ready(part)

    @pl.when(jnp.logical_not(present))
    def absent():
        for part in parts:
            result[:, part, :] = acc[rows, part, :].astype(BF16)
            ready(part)


def from_side(which):
    core = lax.axis_index("lon")
    side = 1 - core if which == 0 else core
    lat_pos = lax.axis_index("lat")
    last = lax.axis_size("lat") - 1
    present = jnp.where(side == 0, lat_pos != 0, lat_pos != last)
    return side, present


def early_kernel(halo, edges, weights, acc, mix, result, ext, hidden):
    side, present = from_side(0)
    side_rows(side, halo, edges, weights, acc, mix, ext, hidden, present, result)


def late_kernel(early, halo, edges, weights, acc, mix, out, ext, hidden, result, sems):
    half, cols, _ = result.shape
    side, present = from_side(1)
    rows = pl.ds(side * half, half)
    other_rows = pl.ds((1 - side) * half, half)

    def copy_of(part):
        n = 0 if part.start == 0 else 1
        return pltpu.make_async_copy(
            result.at[:, part, :], out.at[rows, part, :], sems.at[n]
        )

    first = pltpu.make_async_copy(early, out.at[other_rows], sems.at[2])
    first.start()
    side_rows(
        side, halo, edges, weights, acc, mix, ext, hidden, present, result,
        lambda part: copy_of(part).start(),
    )
    first.wait()
    for n in range(2):
        copy_of(slice(n * cols // 2, (n + 1) * cols // 2)).wait()


def shards(fields, lon_taps, lat_taps, cycle_taps, band_start, band_width, mixing):
    rows, cols, chans = fields.shape
    row_total, basis, taps = lon_taps.shape
    band = lat_taps.shape[2]
    reach = (taps - 1) // 2
    polar = cycle_taps.shape[1] // 2
    cycle = cycle_taps.shape[2]
    lat_count = lax.axis_size("lat")
    core = lax.axis_index("lon")
    axes = ("lat", "lon")
    assert cycle == 2 * cols and rows == 2 * HALO and basis * polar * BLOCK == rows * SPAN
    assert reach == (SPAN - BLOCK) // 4
    ahead, back = ring(lat_count, 1), ring(lat_count, -1)
    other = lax.ppermute(fields, "lon", SWAP)
    going = lax.dynamic_slice_in_dim(fields, core * HALO, HALO, 0)
    second = lax.ppermute(going, axes, back)
    going, band_start = lax.optimization_barrier((going, band_start))

    vmem = pl.BlockSpec(memory_space=pltpu.VMEM)
    hbm = pl.BlockSpec(memory_space=pltpu.HBM)
    sds = jax.ShapeDtypeStruct
    group = basis * rows * BLOCK
    ext_cols = cols + SPAN - BLOCK
    limit = pltpu.CompilerParams(vmem_limit_bytes=32 * 1024 * 1024)
    halo_weights, own_weights, polar_weights, turns, whole, mix, turned = pl.pallas_call(
        weight_kernel,
        out_shape=(
            sds((2, group // 2, HALO * SPAN), BF16),
            sds((group, rows * SPAN), BF16),
            sds((rows * BLOCK, rows * SPAN), BF16),
            sds((basis, 2 * polar, cycle), BF16),
            sds((rows, cols, chans), BF16),
            sds((basis * chans, chans), BF16),
            sds((polar, basis * cols, cycle), BF16),
        ),
        in_specs=[hbm] * 7,
        out_specs=[vmem] * 7,
        scratch_shapes=[
            pltpu.SMEM((rows,), jnp.int32),
            pltpu.SMEM((rows,), jnp.int32),
            pltpu.VMEM((taps, basis, row_total), F32),
            pltpu.VMEM((band, basis, rows), BF16),
            pltpu.VMEM((128, -(-row_total // 128) * 128), F32),
            pltpu.VMEM((128, 128), F32),
            pltpu.SemaphoreType.DMA((7,)),
        ],
        compiler_params=limit,
        cost_estimate=pl.CostEstimate(
            flops=100_000, bytes_accessed=1_000, transcendentals=0
        ),
        name="filter_weights",
    )(
        *(
            pltpu.with_memory_space_constraint(x, pltpu.HBM)
            for x in (
                band_start, band_width, jnp.transpose(lon_taps, (2, 1, 0)),
                jnp.transpose(lat_taps, (2, 1, 0)), fields, cycle_taps,
                mixing.reshape(basis * chans, chans),
            )
        ),
    )
    edges = jnp.concatenate([other[:, :reach], other[:, cols - reach :]], axis=1)
    upper, lower = edges[:HALO], edges[rows - HALO :]
    second_edges = lax.ppermute(jnp.where(core == 0, upper, lower), axes, back)
    head, tail = whole[:HALO], whole[rows - HALO :]
    first = lax.ppermute(jnp.where(core == 0, tail, head), axes, ahead)
    first_edges = lax.ppermute(jnp.where(core == 0, lower, upper), axes, ahead)
    acc, turned = pl.pallas_call(
        own_kernel,
        out_shape=(
            sds((rows, cols, chans), F32),
            sds((polar, basis * cols, cycle), BF16),
        ),
        in_specs=[vmem] * 5,
        out_specs=(vmem, vmem),
        input_output_aliases={0: 1},
        scratch_shapes=[
            pltpu.VMEM((rows, ext_cols, chans), BF16),
            pltpu.VMEM((rows * (cols - 2 * BLOCK), basis * chans), BF16),
        ],
        compiler_params=limit,
        cost_estimate=pl.CostEstimate(
            flops=100_000, bytes_accessed=1_000, transcendentals=0
        ),
        name="own_rows",
    )(turned, own_weights, turns, whole, mix)

    acc = pl.pallas_call(
        partner_kernel,
        out_shape=sds((rows, cols, chans), F32),
        in_specs=[vmem] * 7,
        out_specs=vmem,
        input_output_aliases={0: 0},
        scratch_shapes=[
            pltpu.VMEM((rows * 2 * BLOCK, basis * chans), BF16),
            pltpu.VMEM((basis, polar * cols, chans), BF16),
            pltpu.VMEM((basis * polar, cols, chans), BF16),
        ],
        compiler_params=limit,
        cost_estimate=pl.CostEstimate(
            flops=100_000, bytes_accessed=1_000, transcendentals=0
        ),
        name="partner_columns",
    )(acc, own_weights, polar_weights, turned, whole, mix, other)

    half = rows // 2
    scratch = [
        pltpu.VMEM((HALO, ext_cols, chans), BF16),
        pltpu.VMEM((2, half * cols // 2, basis * chans), BF16),
    ]
    limit = pltpu.CompilerParams(vmem_limit_bytes=32 * 1024 * 1024)
    second, second_edges, acc = lax.optimization_barrier((second, second_edges, acc))
    early = pl.pallas_call(
        early_kernel,
        out_shape=sds((half, cols, chans), BF16),
        in_specs=[vmem] * 5,
        out_specs=vmem,
        scratch_shapes=scratch,
        compiler_params=limit,
        cost_estimate=pl.CostEstimate(
            flops=300_000_000, bytes_accessed=1_000_000, transcendentals=0
        ),
        name="early_side",
    )(second, second_edges, halo_weights, acc, mix)
    first, first_edges, early = lax.optimization_barrier((first, first_edges, early))
    return pl.pallas_call(
        late_kernel,
        out_shape=sds((rows, cols, chans), BF16),
        in_specs=[vmem] * 6,
        out_specs=hbm,
        scratch_shapes=[
            *scratch,
            pltpu.VMEM((half, cols, chans), BF16),
            pltpu.SemaphoreType.DMA((3,)),
        ],
        compiler_params=limit,
        name="late_side",
    )(early, first, first_edges, halo_weights, acc, mix)


def solution(mesh):
    in_specs = (
        P(("ens", "lat"), "lon", None),
        P(),
        P("lat", None, None),
        P(),
        P("lat"),
        P("lat"),
        P(),
    )
    out_specs = P(("ens", "lat"), "lon", None)
    return jax.shard_map(shards, mesh=mesh, in_specs=in_specs, out_specs=out_specs, check_vma=False)
```

```python
import jax
import jax.numpy as jnp
from jax import lax
from jax.experimental import pallas as pl
from jax.experimental.pallas import tpu as pltpu
from jax.sharding import PartitionSpec as P

HALO = 4
BLOCK = 16
SPAN = 32
SWAP = [(0, 1), (1, 0)]
F32, BF16 = jnp.float32, jnp.bfloat16


def ring(lat_count, step):
    pairs = []
    for lat in range(lat_count):
        for core in range(2):
            to = lat + (step if core == 0 else -step)
            if 0 <= to < lat_count:
                pairs.append((lat * 2 + core, to * 2 + core))
            else:
                pairs.append((lat * 2 + core, lat * 2 + 1 - core))
    return pairs


def matmul(a, b):
    return jnp.dot(a, b, preferred_element_type=F32)


def staircase(line, steps):
    wide = jnp.broadcast_to(line, (steps, line.shape[1]))
    return pltpu.roll(wide, 0, 1, stride=1, stride_axis=0).astype(BF16)


def chosen(terms):
    total = None
    for mask, value in terms:
        term = jnp.where(mask, value, 0.0)
        total = term if total is None else total + term
    return total


def window_products(weights, cells, hidden, groups, width, offset, chans):
    part = matmul(weights[...], cells.reshape(-1, chans)).astype(BF16)
    for n, (i, k) in enumerate(groups):
        at = i * width + offset
        hidden[at : at + BLOCK, k * chans : (k + 1) * chans] = part[n * BLOCK : (n + 1) * BLOCK]


def polar_matrices(cycle_taps, turned, at_top):
    basis, twice, cycle = cycle_taps.shape
    polar = twice // 2
    cols = turned.shape[1] // basis
    total = lax.broadcasted_iota(jnp.int32, (cycle, cycle), 0) + lax.broadcasted_iota(
        jnp.int32, (cycle, cycle), 1
    )
    turn = jnp.where((total == 0) | (total == cycle), 1.0, 0.0).astype(BF16)
    negated = matmul(cycle_taps[...].reshape(-1, cycle), turn)
    for p in range(polar):
        for k in range(basis):
            n = k * twice + (p if at_top else p + polar)
            turned[p, k * cols : (k + 1) * cols, :] = staircase(negated[n : n + 1], cols)


def weight_kernel(
    start_in, width_in, lon_in, lat_in, fields_in, cycle_in, mixing_in,
    halo_weights, own_weights, polar_weights, cycle_taps, fields, mix, turned,
    start, width, lon, lat, lon_wide, lat_wide, sems,
):
    rows, cols, chans = fields.shape
    taps, basis, row_total = lon.shape
    band = lat.shape[0]
    polar = cycle_taps.shape[1] // 2
    lat_pos = lax.axis_index("lat")
    base = lat_pos * rows
    at_top = base == 0

    copies = []
    for n, (source, target) in enumerate(
        [
            (lon_in, lon), (lat_in, lat), (start_in, start), (width_in, width),
            (fields_in, fields), (cycle_in, cycle_taps), (mixing_in, mix),
        ]
    ):
        copies.append(pltpu.make_async_copy(source, target, sems.at[n]))
        copies[-1].start()
    lon_wide[...] = jnp.zeros_like(lon_wide)
    lat_wide[...] = jnp.zeros_like(lat_wide)
    for n in range(4):
        copies[n].wait()

    for d in range(taps):
        for k in range(basis):
            lon_wide[k * 16 + d : k * 16 + d + 1, 0:row_total] = lon[d, k : k + 1, :]
    lanes = lon_wide.shape[1]
    slots = pltpu.roll(lon_wide[...], lax.rem(lanes + HALO - base, lanes), 1)[:, :128]
    slots = jnp.transpose(slots)[: rows + 2 * HALO]
    is_tap = lax.broadcasted_iota(jnp.int32, slots.shape, 1) < taps
    own_taps, halo_taps = [], []
    for k in range(basis):
        moved = slots if k == 0 else pltpu.roll(slots, 128 - 16 * k, 1)
        moved = jnp.where(is_tap, moved, 0.0)
        for _ in range(2):
            moved = pltpu.roll(moved, 0, 1, stride=SPAN // 2, stride_axis=0)
        quads = [jnp.sum(moved[4 * q : 4 * q + 4], axis=0, keepdims=True) for q in range(4)]
        own_taps.append(jnp.concatenate([quads[1], quads[2]], axis=1))
        halo_taps.append(jnp.concatenate([quads[0], quads[3]], axis=1))

    for t in range(band):
        lat_wide[t * basis : (t + 1) * basis, 0:rows] = lat[t].astype(F32)
    lat_cols = jnp.transpose(lat_wide[...])[:rows]
    shape = (rows, rows * SPAN)
    lane = lax.broadcasted_iota(jnp.int32, shape, 1)
    out_row = lax.broadcasted_iota(jnp.int32, shape, 0)
    first = jnp.zeros(shape, jnp.int32)
    count = jnp.zeros(shape, jnp.int32)
    for i in range(rows):
        first = jnp.where(out_row == i, start[i], first)
        count = jnp.where(out_row == i, width[i], count)
    spread = [
        [
            jnp.broadcast_to(lat_cols[:, t * basis + k : t * basis + k + 1], shape)
            for k in range(basis)
        ]
        for t in range(band)
    ]
    slot = lane // SPAN
    own_row = base + slot
    halo_row = jnp.where(slot < HALO, own_row - HALO, own_row + rows - HALO)
    is_polar = (own_row < polar) | (own_row >= row_total - polar)
    in_grid = (halo_row >= 0) & (halo_row < row_total)
    own_step, halo_step = own_row - first, halo_row - first
    own_used = [(own_step == t) & (count > t) & ~is_polar for t in range(band)]
    halo_used = [(halo_step == t) & (count > t) & in_grid for t in range(band)]
    for k in range(basis):
        own_line = own_taps[k] * chosen([(own_used[t], spread[t][k]) for t in range(band)])
        halo_line = halo_taps[k] * chosen([(halo_used[t], spread[t][k]) for t in range(band)])
        for i in range(rows):
            at = (k * rows + i) * BLOCK
            own_weights[at : at + BLOCK, :] = staircase(own_line[i : i + 1], BLOCK)
            side, at = i // HALO, (k * HALO + i % HALO) * BLOCK
            reached = halo_line[i : i + 1, side * HALO * SPAN : (side + 1) * HALO * SPAN]
            halo_weights[side, at : at + BLOCK, :] = staircase(reached, BLOCK)

    offset = jnp.where(at_top, 0, rows - polar)
    of_basis = lane // (polar * BLOCK)
    step = base + offset + lax.rem(lane // BLOCK, polar) - first
    at_start = lax.rem(lane, BLOCK) == 0
    terms = []
    for t in range(band):
        value = spread[t][0]
        for k in range(1, basis):
            value = jnp.where(of_basis == k, spread[t][k], value)
        terms.append(((step == t) & (count > t) & at_start, value))
    line = chosen(terms)
    for i in range(rows):
        polar_weights[i * BLOCK : (i + 1) * BLOCK, :] = staircase(line[i : i + 1], BLOCK)
    copies[5].wait()

    @pl.when(at_top & (lax.axis_index("lon") == 0))
    def top():
        polar_matrices(cycle_taps, turned, True)

    copies[4].wait()
    copies[6].wait()


def own_kernel(turned_in, own_weights, cycle_taps, fields, mix, acc, turned, ext, hidden):
    del turned_in
    rows, cols, chans = fields.shape
    basis = mix.shape[0] // chans
    near = (SPAN - BLOCK) // 4

    lat_pos = lax.axis_index("lat")

    @pl.when((lat_pos == 0) & (lax.axis_index("lon") != 0))
    def top():
        polar_matrices(cycle_taps, turned, True)

    @pl.when(lat_pos == lax.axis_size("lat") - 1)
    def bottom():
        polar_matrices(cycle_taps, turned, False)

    blank = jnp.zeros((near, chans), BF16)
    pad = jnp.zeros((ext.shape[1] - cols - near, chans), BF16)
    for r in range(rows):
        ext[r] = jnp.concatenate([blank, fields[r], pad], axis=0)
    groups = [(i, k) for k in range(basis) for i in range(rows)]
    inner = cols - 2 * BLOCK
    for at in range(BLOCK, cols - BLOCK, BLOCK):
        window_products(
            own_weights, ext[:, at : at + SPAN, :], hidden, groups, inner, at - BLOCK, chans
        )
    half = rows // 2
    for n in range(2):
        at = slice(n * half, (n + 1) * half)
        total = matmul(hidden[n * half * inner : (n + 1) * half * inner], mix[...])
        acc[at, BLOCK : cols - BLOCK, :] = total.reshape(half, inner, chans) + fields[
            at, BLOCK : cols - BLOCK, :
        ].astype(F32)


def partner_kernel(
    acc_in, own_weights, polar_weights, turned, fields, mix, other,
    acc, hidden, cycle_rows, mixed_rows,
):
    del acc_in
    rows, cols, chans = fields.shape
    polar = turned.shape[0]
    basis = mix.shape[0] // chans
    reach = (SPAN - BLOCK) // 4
    lat_pos = lax.axis_index("lat")
    at_top = lat_pos == 0
    at_bottom = lat_pos == lax.axis_size("lat") - 1
    groups = [(i, k) for k in range(basis) for i in range(rows)]
    left, right = [], []
    pad = jnp.zeros((SPAN - BLOCK - 2 * reach, chans), BF16)
    for r in range(rows):
        left.append(
            jnp.concatenate([other[r, cols - reach :], fields[r, : SPAN - reach]], axis=0)
        )
        right.append(
            jnp.concatenate(
                [fields[r, cols - BLOCK - reach :], other[r, :reach], pad], axis=0
            )
        )
    for n, cells in enumerate((left, right)):
        window_products(
            own_weights, jnp.concatenate(cells, axis=0), hidden, groups, 2 * BLOCK, n * BLOCK,
            chans,
        )
    total = matmul(hidden[...], mix[...]).reshape(rows, 2 * BLOCK, chans)
    for n, at in enumerate((slice(0, BLOCK), slice(cols - BLOCK, cols))):
        acc[:, at, :] = total[:, n * BLOCK : (n + 1) * BLOCK] + fields[:, at, :].astype(F32)

    @pl.when(at_top | at_bottom)
    def polar_part():
        offset = jnp.where(at_top, 0, rows - polar)
        for p in range(polar):
            whole = jnp.concatenate([fields[offset + p], other[offset + p]], axis=0)
            part = matmul(turned[p], whole).astype(BF16)
            for k in range(basis):
                cycle_rows[k, p * cols : (p + 1) * cols, :] = part[k * cols : (k + 1) * cols]
        for k in range(basis):
            part = matmul(cycle_rows[k], mix[k * chans : (k + 1) * chans, :]).astype(BF16)
            mixed_rows[k * polar : (k + 1) * polar] = part.reshape(polar, cols, chans)
        for b in range(cols // BLOCK):
            at = slice(BLOCK * b, BLOCK * (b + 1))
            cells = mixed_rows[:, at, :].reshape(-1, chans)
            acc[:, at, :] = acc[:, at, :] + matmul(polar_weights[...], cells).reshape(
                rows, BLOCK, chans
            )


def side_rows(
    side, halo, edges, weights, acc, mix, ext, hidden, present, result, ready=lambda at: None
):
    half, cols, chans = result.shape
    basis = mix.shape[0] // chans
    reach = edges.shape[1] // 2
    rows = pl.ds(side * half, half)
    wide = cols // 2
    parts = [slice(n * wide, (n + 1) * wide) for n in range(2)]

    @pl.when(present)
    def arrived():
        pad = jnp.zeros((ext.shape[1] - cols - 2 * reach, chans), BF16)
        for p in range(HALO):
            edge = edges[p]
            ext[p] = jnp.concatenate([edge[reach:], halo[p], edge[:reach], pad], axis=0)
        groups = [(i, k) for k in range(basis) for i in range(half)]
        for n, part in enumerate(parts):
            for at in range(0, wide, BLOCK):
                cells = ext[:, part.start + at : part.start + at + SPAN, :]
                window_products(
                    weights.at[side], cells, hidden.at[n], groups, wide, at, chans
                )
        for n, part in enumerate(parts):
            total = matmul(hidden[n], mix[...]).reshape(half, wide, chans)
            result[:, part, :] = (total + acc[rows, part, :]).astype(BF16)
            ready(part)

    @pl.when(jnp.logical_not(present))
    def absent():
        for part in parts:
            result[:, part, :] = acc[rows, part, :].astype(BF16)
            ready(part)


def from_side(which):
    core = lax.axis_index("lon")
    side = 1 - core if which == 0 else core
    lat_pos = lax.axis_index("lat")
    last = lax.axis_size("lat") - 1
    present = jnp.where(side == 0, lat_pos != 0, lat_pos != last)
    return side, present


def early_kernel(halo, edges, weights, acc, mix, result, ext, hidden):
    side, present = from_side(0)
    side_rows(side, halo, edges, weights, acc, mix, ext, hidden, present, result)


def late_kernel(early, halo, edges, weights, acc, mix, out, ext, hidden, result, sems):
    half, cols, _ = result.shape
    side, present = from_side(1)
    rows = pl.ds(side * half, half)
    other_rows = pl.ds((1 - side) * half, half)

    def copy_of(part):
        n = 0 if part.start == 0 else 1
        return pltpu.make_async_copy(
            result.at[:, part, :], out.at[rows, part, :], sems.at[n]
        )

    first = pltpu.make_async_copy(early, out.at[other_rows], sems.at[2])
    first.start()
    side_rows(
        side, halo, edges, weights, acc, mix, ext, hidden, present, result,
        lambda part: copy_of(part).start(),
    )
    first.wait()
    for n in range(2):
        copy_of(slice(n * cols // 2, (n + 1) * cols // 2)).wait()


def shards(fields, lon_taps, lat_taps, cycle_taps, band_start, band_width, mixing):
    rows, cols, chans = fields.shape
    row_total, basis, taps = lon_taps.shape
    band = lat_taps.shape[2]
    reach = (taps - 1) // 2
    polar = cycle_taps.shape[1] // 2
    cycle = cycle_taps.shape[2]
    lat_count = lax.axis_size("lat")
    core = lax.axis_index("lon")
    axes = ("lat", "lon")
    assert cycle == 2 * cols and rows == 2 * HALO and basis * polar * BLOCK == rows * SPAN
    assert reach == (SPAN - BLOCK) // 4
    ahead, back = ring(lat_count, 1), ring(lat_count, -1)
    other = lax.ppermute(fields, "lon", SWAP)
    going = jnp.where(core == 0, fields[:HALO], fields[rows - HALO :])
    second = lax.ppermute(going, axes, back)
    going, band_start = lax.optimization_barrier((going, band_start))

    vmem = pl.BlockSpec(memory_space=pltpu.VMEM)
    hbm = pl.BlockSpec(memory_space=pltpu.HBM)
    sds = jax.ShapeDtypeStruct
    group = basis * rows * BLOCK
    ext_cols = cols + SPAN - BLOCK
    limit = pltpu.CompilerParams(vmem_limit_bytes=32 * 1024 * 1024)
    halo_weights, own_weights, polar_weights, turns, whole, mix, turned = pl.pallas_call(
        weight_kernel,
        out_shape=(
            sds((2, group // 2, HALO * SPAN), BF16),
            sds((group, rows * SPAN), BF16),
            sds((rows * BLOCK, rows * SPAN), BF16),
            sds((basis, 2 * polar, cycle), BF16),
            sds((rows, cols, chans), BF16),
            sds((basis * chans, chans), BF16),
            sds((polar, basis * cols, cycle), BF16),
        ),
        in_specs=[hbm] * 7,
        out_specs=[vmem] * 7,
        scratch_shapes=[
            pltpu.SMEM((rows,), jnp.int32),
            pltpu.SMEM((rows,), jnp.int32),
            pltpu.VMEM((taps, basis, row_total), F32),
            pltpu.VMEM((band, basis, rows), BF16),
            pltpu.VMEM((128, -(-row_total // 128) * 128), F32),
            pltpu.VMEM((128, 128), F32),
            pltpu.SemaphoreType.DMA((7,)),
        ],
        compiler_params=limit,
        cost_estimate=pl.CostEstimate(
            flops=100_000, bytes_accessed=1_000, transcendentals=0
        ),
        name="filter_weights",
    )(
        *(
            pltpu.with_memory_space_constraint(x, pltpu.HBM)
            for x in (
                band_start, band_width, jnp.transpose(lon_taps, (2, 1, 0)),
                jnp.transpose(lat_taps, (2, 1, 0)), fields, cycle_taps,
                mixing.reshape(basis * chans, chans),
            )
        ),
    )
    edges = jnp.concatenate([other[:, :reach], other[:, cols - reach :]], axis=1)
    upper, lower = edges[:HALO], edges[rows - HALO :]
    second_edges = lax.ppermute(jnp.where(core == 0, upper, lower), axes, back)
    head, tail = whole[:HALO], whole[rows - HALO :]
    first = lax.ppermute(jnp.where(core == 0, tail, head), axes, ahead)
    first_edges = lax.ppermute(jnp.where(core == 0, lower, upper), axes, ahead)
    acc, turned = pl.pallas_call(
        own_kernel,
        out_shape=(
            sds((rows, cols, chans), F32),
            sds((polar, basis * cols, cycle), BF16),
        ),
        in_specs=[vmem] * 5,
        out_specs=(vmem, vmem),
        input_output_aliases={0: 1},
        scratch_shapes=[
            pltpu.VMEM((rows, ext_cols, chans), BF16),
            pltpu.VMEM((rows * (cols - 2 * BLOCK), basis * chans), BF16),
        ],
        compiler_params=limit,
        cost_estimate=pl.CostEstimate(
            flops=100_000, bytes_accessed=1_000, transcendentals=0
        ),
        name="own_rows",
    )(turned, own_weights, turns, whole, mix)

    acc = pl.pallas_call(
        partner_kernel,
        out_shape=sds((rows, cols, chans), F32),
        in_specs=[vmem] * 7,
        out_specs=vmem,
        input_output_aliases={0: 0},
        scratch_shapes=[
            pltpu.VMEM((rows * 2 * BLOCK, basis * chans), BF16),
            pltpu.VMEM((basis, polar * cols, chans), BF16),
            pltpu.VMEM((basis * polar, cols, chans), BF16),
        ],
        compiler_params=limit,
        cost_estimate=pl.CostEstimate(
            flops=100_000, bytes_accessed=1_000, transcendentals=0
        ),
        name="partner_columns",
    )(acc, own_weights, polar_weights, turned, whole, mix, other)

    half = rows // 2
    scratch = [
        pltpu.VMEM((HALO, ext_cols, chans), BF16),
        pltpu.VMEM((2, half * cols // 2, basis * chans), BF16),
    ]
    limit = pltpu.CompilerParams(vmem_limit_bytes=32 * 1024 * 1024)
    second, second_edges, acc = lax.optimization_barrier((second, second_edges, acc))
    early = pl.pallas_call(
        early_kernel,
        out_shape=sds((half, cols, chans), BF16),
        in_specs=[vmem] * 5,
        out_specs=vmem,
        scratch_shapes=scratch,
        compiler_params=limit,
        cost_estimate=pl.CostEstimate(
            flops=300_000_000, bytes_accessed=1_000_000, transcendentals=0
        ),
        name="early_side",
    )(second, second_edges, halo_weights, acc, mix)
    first, first_edges, early = lax.optimization_barrier((first, first_edges, early))
    return pl.pallas_call(
        late_kernel,
        out_shape=sds((rows, cols, chans), BF16),
        in_specs=[vmem] * 6,
        out_specs=hbm,
        scratch_shapes=[
            *scratch,
            pltpu.VMEM((half, cols, chans), BF16),
            pltpu.SemaphoreType.DMA((3,)),
        ],
        compiler_params=limit,
        name="late_side",
    )(early, first, first_edges, halo_weights, acc, mix)


def solution(mesh):
    in_specs = (
        P(("ens", "lat"), "lon", None),
        P(),
        P("lat", None, None),
        P(),
        P("lat"),
        P("lat"),
        P(),
    )
    out_specs = P(("ens", "lat"), "lon", None)
    return jax.shard_map(shards, mesh=mesh, in_specs=in_specs, out_specs=out_specs, check_vma=False)
```

```python
import jax
import jax.numpy as jnp
from jax import lax
from jax.experimental import pallas as pl
from jax.experimental.pallas import tpu as pltpu
from jax.sharding import PartitionSpec as P

HALO = 4
BLOCK = 16
SPAN = 32
SWAP = [(0, 1), (1, 0)]
F32, BF16 = jnp.float32, jnp.bfloat16


def ring(lat_count, step):
    pairs = []
    for lat in range(lat_count):
        for core in range(2):
            to = lat + (step if core == 0 else -step)
            if 0 <= to < lat_count:
                pairs.append((lat * 2 + core, to * 2 + core))
            else:
                pairs.append((lat * 2 + core, lat * 2 + 1 - core))
    return pairs


def matmul(a, b):
    return jnp.dot(a, b, preferred_element_type=F32)


def staircase(line, steps):
    wide = jnp.broadcast_to(line, (steps, line.shape[1]))
    return pltpu.roll(wide, 0, 1, stride=1, stride_axis=0).astype(BF16)


def chosen(terms):
    total = None
    for mask, value in terms:
        term = jnp.where(mask, value, 0.0)
        total = term if total is None else total + term
    return total


def window_products(weights, cells, hidden, groups, width, offset, chans):
    part = matmul(weights[...], cells.reshape(-1, chans)).astype(BF16)
    for n, (i, k) in enumerate(groups):
        at = i * width + offset
        hidden[at : at + BLOCK, k * chans : (k + 1) * chans] = part[n * BLOCK : (n + 1) * BLOCK]


def polar_matrices(cycle_taps, turned, at_top):
    basis, twice, cycle = cycle_taps.shape
    polar = twice // 2
    cols = turned.shape[1] // basis
    total = lax.broadcasted_iota(jnp.int32, (cycle, cycle), 0) + lax.broadcasted_iota(
        jnp.int32, (cycle, cycle), 1
    )
    turn = jnp.where((total == 0) | (total == cycle), 1.0, 0.0).astype(BF16)
    negated = matmul(cycle_taps[...].reshape(-1, cycle), turn)
    for p in range(polar):
        for k in range(basis):
            n = k * twice + (p if at_top else p + polar)
            turned[p, k * cols : (k + 1) * cols, :] = staircase(negated[n : n + 1], cols)


def weight_kernel(
    start_in, width_in, lon_in, lat_in, fields_in, cycle_in, mixing_in,
    halo_weights, own_weights, polar_weights, cycle_taps, fields, mix, turned,
    start, width, lon, lat, lon_wide, lat_wide, sems,
):
    rows, cols, chans = fields.shape
    taps, basis, row_total = lon.shape
    band = lat.shape[0]
    polar = cycle_taps.shape[1] // 2
    lat_pos = lax.axis_index("lat")
    base = lat_pos * rows
    at_top = base == 0

    copies = []
    for n, (source, target) in enumerate(
        [
            (lon_in, lon), (lat_in, lat), (start_in, start), (width_in, width),
            (fields_in, fields), (cycle_in, cycle_taps), (mixing_in, mix),
        ]
    ):
        copies.append(pltpu.make_async_copy(source, target, sems.at[n]))
        copies[-1].start()
    lon_wide[...] = jnp.zeros_like(lon_wide)
    lat_wide[...] = jnp.zeros_like(lat_wide)
    for n in range(4):
        copies[n].wait()

    for d in range(taps):
        for k in range(basis):
            lon_wide[k * 16 + d : k * 16 + d + 1, 0:row_total] = lon[d, k : k + 1, :]
    lanes = lon_wide.shape[1]
    slots = pltpu.roll(lon_wide[...], lax.rem(lanes + HALO - base, lanes), 1)[:, :128]
    slots = jnp.transpose(slots)[: rows + 2 * HALO]
    is_tap = lax.broadcasted_iota(jnp.int32, slots.shape, 1) < taps
    own_taps, halo_taps = [], []
    for k in range(basis):
        moved = slots if k == 0 else pltpu.roll(slots, 128 - 16 * k, 1)
        moved = jnp.where(is_tap, moved, 0.0)
        for _ in range(2):
            moved = pltpu.roll(moved, 0, 1, stride=SPAN // 2, stride_axis=0)
        quads = [jnp.sum(moved[4 * q : 4 * q + 4], axis=0, keepdims=True) for q in range(4)]
        own_taps.append(jnp.concatenate([quads[1], quads[2]], axis=1))
        halo_taps.append(jnp.concatenate([quads[0], quads[3]], axis=1))

    for t in range(band):
        lat_wide[t * basis : (t + 1) * basis, 0:rows] = lat[t].astype(F32)
    lat_cols = jnp.transpose(lat_wide[...])[:rows]
    shape = (rows, rows * SPAN)
    lane = lax.broadcasted_iota(jnp.int32, shape, 1)
    out_row = lax.broadcasted_iota(jnp.int32, shape, 0)
    first = jnp.zeros(shape, jnp.int32)
    count = jnp.zeros(shape, jnp.int32)
    for i in range(rows):
        first = jnp.where(out_row == i, start[i], first)
        count = jnp.where(out_row == i, width[i], count)
    spread = [
        [
            jnp.broadcast_to(lat_cols[:, t * basis + k : t * basis + k + 1], shape)
            for k in range(basis)
        ]
        for t in range(band)
    ]
    slot = lane // SPAN
    own_row = base + slot
    halo_row = jnp.where(slot < HALO, own_row - HALO, own_row + rows - HALO)
    is_polar = (own_row < polar) | (own_row >= row_total - polar)
    in_grid = (halo_row >= 0) & (halo_row < row_total)
    own_step, halo_step = own_row - first, halo_row - first
    own_used = [(own_step == t) & (count > t) & ~is_polar for t in range(band)]
    halo_used = [(halo_step == t) & (count > t) & in_grid for t in range(band)]
    for k in range(basis):
        own_line = own_taps[k] * chosen([(own_used[t], spread[t][k]) for t in range(band)])
        halo_line = halo_taps[k] * chosen([(halo_used[t], spread[t][k]) for t in range(band)])
        for i in range(rows):
            at = (k * rows + i) * BLOCK
            own_weights[at : at + BLOCK, :] = staircase(own_line[i : i + 1], BLOCK)
            side, at = i // HALO, (k * HALO + i % HALO) * BLOCK
            reached = halo_line[i : i + 1, side * HALO * SPAN : (side + 1) * HALO * SPAN]
            halo_weights[side, at : at + BLOCK, :] = staircase(reached, BLOCK)

    offset = jnp.where(at_top, 0, rows - polar)
    of_basis = lane // (polar * BLOCK)
    step = base + offset + lax.rem(lane // BLOCK, polar) - first
    at_start = lax.rem(lane, BLOCK) == 0
    terms = []
    for t in range(band):
        value = spread[t][0]
        for k in range(1, basis):
            value = jnp.where(of_basis == k, spread[t][k], value)
        terms.append(((step == t) & (count > t) & at_start, value))
    line = chosen(terms)
    for i in range(rows):
        polar_weights[i * BLOCK : (i + 1) * BLOCK, :] = staircase(line[i : i + 1], BLOCK)
    copies[5].wait()

    @pl.when(at_top & (lax.axis_index("lon") != 0))
    def top():
        polar_matrices(cycle_taps, turned, True)

    copies[4].wait()
    copies[6].wait()


def own_kernel(turned_in, own_weights, cycle_taps, fields, mix, acc, turned, ext, hidden):
    del turned_in
    rows, cols, chans = fields.shape
    basis = mix.shape[0] // chans
    near = (SPAN - BLOCK) // 4

    lat_pos = lax.axis_index("lat")

    @pl.when((lat_pos == 0) & (lax.axis_index("lon") == 0))
    def top():
        polar_matrices(cycle_taps, turned, True)

    @pl.when(lat_pos == lax.axis_size("lat") - 1)
    def bottom():
        polar_matrices(cycle_taps, turned, False)

    blank = jnp.zeros((near, chans), BF16)
    pad = jnp.zeros((ext.shape[1] - cols - near, chans), BF16)
    for r in range(rows):
        ext[r] = jnp.concatenate([blank, fields[r], pad], axis=0)
    groups = [(i, k) for k in range(basis) for i in range(rows)]
    inner = cols - 2 * BLOCK
    for at in range(BLOCK, cols - BLOCK, BLOCK):
        window_products(
            own_weights, ext[:, at : at + SPAN, :], hidden, groups, inner, at - BLOCK, chans
        )
    half = rows // 2
    for n in range(2):
        at = slice(n * half, (n + 1) * half)
        total = matmul(hidden[n * half * inner : (n + 1) * half * inner], mix[...])
        acc[at, BLOCK : cols - BLOCK, :] = total.reshape(half, inner, chans) + fields[
            at, BLOCK : cols - BLOCK, :
        ].astype(F32)


def partner_kernel(
    acc_in, own_weights, polar_weights, turned, fields, mix, other,
    acc, hidden, cycle_rows, mixed_rows,
):
    del acc_in
    rows, cols, chans = fields.shape
    polar = turned.shape[0]
    basis = mix.shape[0] // chans
    reach = (SPAN - BLOCK) // 4
    lat_pos = lax.axis_index("lat")
    at_top = lat_pos == 0
    at_bottom = lat_pos == lax.axis_size("lat") - 1
    groups = [(i, k) for k in range(basis) for i in range(rows)]
    left, right = [], []
    pad = jnp.zeros((SPAN - BLOCK - 2 * reach, chans), BF16)
    for r in range(rows):
        left.append(
            jnp.concatenate([other[r, cols - reach :], fields[r, : SPAN - reach]], axis=0)
        )
        right.append(
            jnp.concatenate(
                [fields[r, cols - BLOCK - reach :], other[r, :reach], pad], axis=0
            )
        )
    for n, cells in enumerate((left, right)):
        window_products(
            own_weights, jnp.concatenate(cells, axis=0), hidden, groups, 2 * BLOCK, n * BLOCK,
            chans,
        )
    total = matmul(hidden[...], mix[...]).reshape(rows, 2 * BLOCK, chans)
    for n, at in enumerate((slice(0, BLOCK), slice(cols - BLOCK, cols))):
        acc[:, at, :] = total[:, n * BLOCK : (n + 1) * BLOCK] + fields[:, at, :].astype(F32)

    @pl.when(at_top | at_bottom)
    def polar_part():
        offset = jnp.where(at_top, 0, rows - polar)
        for p in range(polar):
            whole = jnp.concatenate([fields[offset + p], other[offset + p]], axis=0)
            part = matmul(turned[p], whole).astype(BF16)
            for k in range(basis):
                cycle_rows[k, p * cols : (p + 1) * cols, :] = part[k * cols : (k + 1) * cols]
        for k in range(basis):
            part = matmul(cycle_rows[k], mix[k * chans : (k + 1) * chans, :]).astype(BF16)
            mixed_rows[k * polar : (k + 1) * polar] = part.reshape(polar, cols, chans)
        for b in range(cols // BLOCK):
            at = slice(BLOCK * b, BLOCK * (b + 1))
            cells = mixed_rows[:, at, :].reshape(-1, chans)
            acc[:, at, :] = acc[:, at, :] + matmul(polar_weights[...], cells).reshape(
                rows, BLOCK, chans
            )


def side_rows(
    side, halo, edges, weights, acc, mix, ext, hidden, present, result, ready=lambda at: None
):
    half, cols, chans = result.shape
    basis = mix.shape[0] // chans
    reach = edges.shape[1] // 2
    rows = pl.ds(side * half, half)
    wide = cols // 2
    parts = [slice(n * wide, (n + 1) * wide) for n in range(2)]

    @pl.when(present)
    def arrived():
        pad = jnp.zeros((ext.shape[1] - cols - 2 * reach, chans), BF16)
        for p in range(HALO):
            edge = edges[p]
            ext[p] = jnp.concatenate([edge[reach:], halo[p], edge[:reach], pad], axis=0)
        groups = [(i, k) for k in range(basis) for i in range(half)]
        for n, part in enumerate(parts):
            for at in range(0, wide, BLOCK):
                cells = ext[:, part.start + at : part.start + at + SPAN, :]
                window_products(
                    weights.at[side], cells, hidden.at[n], groups, wide, at, chans
                )
        for n, part in enumerate(parts):
            total = matmul(hidden[n], mix[...]).reshape(half, wide, chans)
            result[:, part, :] = (total + acc[rows, part, :]).astype(BF16)
            ready(part)

    @pl.when(jnp.logical_not(present))
    def absent():
        for part in parts:
            result[:, part, :] = acc[rows, part, :].astype(BF16)
            ready(part)


def from_side(which):
    core = lax.axis_index("lon")
    side = core if which == 0 else 1 - core
    lat_pos = lax.axis_index("lat")
    last = lax.axis_size("lat") - 1
    present = jnp.where(side == 0, lat_pos != 0, lat_pos != last)
    return side, present


def early_kernel(halo, edges, weights, acc, mix, result, ext, hidden):
    side, present = from_side(0)
    side_rows(side, halo, edges, weights, acc, mix, ext, hidden, present, result)


def late_kernel(early, halo, edges, weights, acc, mix, out, ext, hidden, result, sems):
    half, cols, _ = result.shape
    side, present = from_side(1)
    rows = pl.ds(side * half, half)
    other_rows = pl.ds((1 - side) * half, half)

    def copy_of(part):
        n = 0 if part.start == 0 else 1
        return pltpu.make_async_copy(
            result.at[:, part, :], out.at[rows, part, :], sems.at[n]
        )

    first = pltpu.make_async_copy(early, out.at[other_rows], sems.at[2])
    first.start()
    side_rows(
        side, halo, edges, weights, acc, mix, ext, hidden, present, result,
        lambda part: copy_of(part).start(),
    )
    first.wait()
    for n in range(2):
        copy_of(slice(n * cols // 2, (n + 1) * cols // 2)).wait()


def shards(fields, lon_taps, lat_taps, cycle_taps, band_start, band_width, mixing):
    rows, cols, chans = fields.shape
    row_total, basis, taps = lon_taps.shape
    band = lat_taps.shape[2]
    reach = (taps - 1) // 2
    polar = cycle_taps.shape[1] // 2
    cycle = cycle_taps.shape[2]
    lat_count = lax.axis_size("lat")
    core = lax.axis_index("lon")
    axes = ("lat", "lon")
    assert cycle == 2 * cols and rows == 2 * HALO and basis * polar * BLOCK == rows * SPAN
    assert reach == (SPAN - BLOCK) // 4
    ahead, back = ring(lat_count, 1), ring(lat_count, -1)
    other = lax.ppermute(fields, "lon", SWAP)
    going = jnp.where(core == 0, fields[rows - HALO :], fields[:HALO])
    early_halo = lax.ppermute(going, axes, ahead)
    going, band_start = lax.optimization_barrier((going, band_start))

    vmem = pl.BlockSpec(memory_space=pltpu.VMEM)
    hbm = pl.BlockSpec(memory_space=pltpu.HBM)
    sds = jax.ShapeDtypeStruct
    group = basis * rows * BLOCK
    ext_cols = cols + SPAN - BLOCK
    limit = pltpu.CompilerParams(vmem_limit_bytes=32 * 1024 * 1024)
    halo_weights, own_weights, polar_weights, turns, whole, mix, turned = pl.pallas_call(
        weight_kernel,
        out_shape=(
            sds((2, group // 2, HALO * SPAN), BF16),
            sds((group, rows * SPAN), BF16),
            sds((rows * BLOCK, rows * SPAN), BF16),
            sds((basis, 2 * polar, cycle), BF16),
            sds((rows, cols, chans), BF16),
            sds((basis * chans, chans), BF16),
            sds((polar, basis * cols, cycle), BF16),
        ),
        in_specs=[hbm] * 7,
        out_specs=[vmem] * 7,
        scratch_shapes=[
            pltpu.SMEM((rows,), jnp.int32),
            pltpu.SMEM((rows,), jnp.int32),
            pltpu.VMEM((taps, basis, row_total), F32),
            pltpu.VMEM((band, basis, rows), BF16),
            pltpu.VMEM((128, -(-row_total // 128) * 128), F32),
            pltpu.VMEM((128, 128), F32),
            pltpu.SemaphoreType.DMA((7,)),
        ],
        compiler_params=limit,
        cost_estimate=pl.CostEstimate(
            flops=100_000, bytes_accessed=1_000, transcendentals=0
        ),
        name="filter_weights",
    )(
        *(
            pltpu.with_memory_space_constraint(x, pltpu.HBM)
            for x in (
                band_start, band_width, jnp.transpose(lon_taps, (2, 1, 0)),
                jnp.transpose(lat_taps, (2, 1, 0)), fields, cycle_taps,
                mixing.reshape(basis * chans, chans),
            )
        ),
    )
    edges = jnp.concatenate([other[:, :reach], other[:, cols - reach :]], axis=1)
    upper, lower = edges[:HALO], edges[rows - HALO :]
    early_edges = lax.ppermute(jnp.where(core == 0, lower, upper), axes, ahead)
    head, tail = whole[:HALO], whole[rows - HALO :]
    late_halo = lax.ppermute(jnp.where(core == 0, head, tail), axes, back)
    late_edges = lax.ppermute(jnp.where(core == 0, upper, lower), axes, back)
    acc, turned = pl.pallas_call(
        own_kernel,
        out_shape=(
            sds((rows, cols, chans), F32),
            sds((polar, basis * cols, cycle), BF16),
        ),
        in_specs=[vmem] * 5,
        out_specs=(vmem, vmem),
        input_output_aliases={0: 1},
        scratch_shapes=[
            pltpu.VMEM((rows, ext_cols, chans), BF16),
            pltpu.VMEM((rows * (cols - 2 * BLOCK), basis * chans), BF16),
        ],
        compiler_params=limit,
        cost_estimate=pl.CostEstimate(
            flops=100_000, bytes_accessed=1_000, transcendentals=0
        ),
        name="own_rows",
    )(turned, own_weights, turns, whole, mix)

    acc = pl.pallas_call(
        partner_kernel,
        out_shape=sds((rows, cols, chans), F32),
        in_specs=[vmem] * 7,
        out_specs=vmem,
        input_output_aliases={0: 0},
        scratch_shapes=[
            pltpu.VMEM((rows * 2 * BLOCK, basis * chans), BF16),
            pltpu.VMEM((basis, polar * cols, chans), BF16),
            pltpu.VMEM((basis * polar, cols, chans), BF16),
        ],
        compiler_params=limit,
        cost_estimate=pl.CostEstimate(
            flops=100_000, bytes_accessed=1_000, transcendentals=0
        ),
        name="partner_columns",
    )(acc, own_weights, polar_weights, turned, whole, mix, other)

    half = rows // 2
    scratch = [
        pltpu.VMEM((HALO, ext_cols, chans), BF16),
        pltpu.VMEM((2, half * cols // 2, basis * chans), BF16),
    ]
    limit = pltpu.CompilerParams(vmem_limit_bytes=32 * 1024 * 1024)
    early_halo, early_edges, acc = lax.optimization_barrier((early_halo, early_edges, acc))
    early = pl.pallas_call(
        early_kernel,
        out_shape=sds((half, cols, chans), BF16),
        in_specs=[vmem] * 5,
        out_specs=vmem,
        scratch_shapes=scratch,
        compiler_params=limit,
        cost_estimate=pl.CostEstimate(
            flops=300_000_000, bytes_accessed=1_000_000, transcendentals=0
        ),
        name="early_side",
    )(early_halo, early_edges, halo_weights, acc, mix)
    late_halo, late_edges, early = lax.optimization_barrier((late_halo, late_edges, early))
    return pl.pallas_call(
        late_kernel,
        out_shape=sds((rows, cols, chans), BF16),
        in_specs=[vmem] * 6,
        out_specs=hbm,
        scratch_shapes=[
            *scratch,
            pltpu.VMEM((half, cols, chans), BF16),
            pltpu.SemaphoreType.DMA((3,)),
        ],
        compiler_params=limit,
        name="late_side",
    )(early, late_halo, late_edges, halo_weights, acc, mix)


def solution(mesh):
    in_specs = (
        P(("ens", "lat"), "lon", None),
        P(),
        P("lat", None, None),
        P(),
        P("lat"),
        P("lat"),
        P(),
    )
    out_specs = P(("ens", "lat"), "lon", None)
    return jax.shard_map(shards, mesh=mesh, in_specs=in_specs, out_specs=out_specs, check_vma=False)
```

```python
import jax
import jax.numpy as jnp
from jax import lax
from jax.experimental import pallas as pl
from jax.experimental.pallas import tpu as pltpu
from jax.sharding import PartitionSpec as P

HALO = 4
BLOCK = 16
SPAN = 32
SWAP = [(0, 1), (1, 0)]
F32, BF16 = jnp.float32, jnp.bfloat16


def ring(lat_count, step):
    pairs = []
    for lat in range(lat_count):
        for core in range(2):
            to = lat + (step if core == 0 else -step)
            if 0 <= to < lat_count:
                pairs.append((lat * 2 + core, to * 2 + core))
            else:
                pairs.append((lat * 2 + core, lat * 2 + 1 - core))
    return pairs


def matmul(a, b):
    return jnp.dot(a, b, preferred_element_type=F32)


def staircase(line, steps):
    wide = jnp.broadcast_to(line, (steps, line.shape[1]))
    return pltpu.roll(wide, 0, 1, stride=1, stride_axis=0).astype(BF16)


def chosen(terms):
    total = None
    for mask, value in terms:
        term = jnp.where(mask, value, 0.0)
        total = term if total is None else total + term
    return total


def window_products(weights, cells, hidden, groups, width, offset, chans):
    part = matmul(weights[...], cells.reshape(-1, chans)).astype(BF16)
    for n, (i, k) in enumerate(groups):
        at = i * width + offset
        hidden[at : at + BLOCK, k * chans : (k + 1) * chans] = part[n * BLOCK : (n + 1) * BLOCK]


def polar_matrices(cycle_taps, turned, at_top):
    basis, twice, cycle = cycle_taps.shape
    polar = twice // 2
    cols = turned.shape[1] // basis
    total = lax.broadcasted_iota(jnp.int32, (cycle, cycle), 0) + lax.broadcasted_iota(
        jnp.int32, (cycle, cycle), 1
    )
    turn = jnp.where((total == 0) | (total == cycle), 1.0, 0.0).astype(BF16)
    negated = matmul(cycle_taps[...].reshape(-1, cycle), turn)
    for p in range(polar):
        for k in range(basis):
            n = k * twice + (p if at_top else p + polar)
            turned[p, k * cols : (k + 1) * cols, :] = staircase(negated[n : n + 1], cols)


def weight_kernel(
    start_in, width_in, lon_in, lat_in, fields_in, cycle_in, mixing_in,
    halo_weights, own_weights, polar_weights, cycle_taps, fields, mix, turned,
    start, width, lon, lat, lon_wide, lat_wide, sems,
):
    rows, cols, chans = fields.shape
    taps, basis, row_total = lon.shape
    band = lat.shape[0]
    polar = cycle_taps.shape[1] // 2
    lat_pos = lax.axis_index("lat")
    base = lat_pos * rows
    at_top = base == 0

    copies = []
    for n, (source, target) in enumerate(
        [
            (lon_in, lon), (lat_in, lat), (start_in, start), (width_in, width),
            (fields_in, fields), (cycle_in, cycle_taps), (mixing_in, mix),
        ]
    ):
        copies.append(pltpu.make_async_copy(source, target, sems.at[n]))
        copies[-1].start()
    lon_wide[...] = jnp.zeros_like(lon_wide)
    lat_wide[...] = jnp.zeros_like(lat_wide)
    for n in range(4):
        copies[n].wait()

    for d in range(taps):
        for k in range(basis):
            lon_wide[k * 16 + d : k * 16 + d + 1, 0:row_total] = lon[d, k : k + 1, :]
    lanes = lon_wide.shape[1]
    slots = pltpu.roll(lon_wide[...], lax.rem(lanes + HALO - base, lanes), 1)[:, :128]
    slots = jnp.transpose(slots)[: rows + 2 * HALO]
    is_tap = lax.broadcasted_iota(jnp.int32, slots.shape, 1) < taps
    own_taps, halo_taps = [], []
    for k in range(basis):
        moved = slots if k == 0 else pltpu.roll(slots, 128 - 16 * k, 1)
        moved = jnp.where(is_tap, moved, 0.0)
        for _ in range(2):
            moved = pltpu.roll(moved, 0, 1, stride=SPAN // 2, stride_axis=0)
        quads = [jnp.sum(moved[4 * q : 4 * q + 4], axis=0, keepdims=True) for q in range(4)]
        own_taps.append(jnp.concatenate([quads[1], quads[2]], axis=1))
        halo_taps.append(jnp.concatenate([quads[0], quads[3]], axis=1))

    for t in range(band):
        lat_wide[t * basis : (t + 1) * basis, 0:rows] = lat[t].astype(F32)
    lat_cols = jnp.transpose(lat_wide[...])[:rows]
    shape = (rows, rows * SPAN)
    lane = lax.broadcasted_iota(jnp.int32, shape, 1)
    out_row = lax.broadcasted_iota(jnp.int32, shape, 0)
    first = jnp.zeros(shape, jnp.int32)
    count = jnp.zeros(shape, jnp.int32)
    for i in range(rows):
        first = jnp.where(out_row == i, start[i], first)
        count = jnp.where(out_row == i, width[i], count)
    spread = [
        [
            jnp.broadcast_to(lat_cols[:, t * basis + k : t * basis + k + 1], shape)
            for k in range(basis)
        ]
        for t in range(band)
    ]
    slot = lane // SPAN
    own_row = base + slot
    halo_row = jnp.where(slot < HALO, own_row - HALO, own_row + rows - HALO)
    is_polar = (own_row < polar) | (own_row >= row_total - polar)
    in_grid = (halo_row >= 0) & (halo_row < row_total)
    own_step, halo_step = own_row - first, halo_row - first
    own_used = [(own_step == t) & (count > t) & ~is_polar for t in range(band)]
    halo_used = [(halo_step == t) & (count > t) & in_grid for t in range(band)]
    for k in range(basis):
        own_line = own_taps[k] * chosen([(own_used[t], spread[t][k]) for t in range(band)])
        halo_line = halo_taps[k] * chosen([(halo_used[t], spread[t][k]) for t in range(band)])
        for i in range(rows):
            at = (k * rows + i) * BLOCK
            own_weights[at : at + BLOCK, :] = staircase(own_line[i : i + 1], BLOCK)
            side, at = i // HALO, (k * HALO + i % HALO) * BLOCK
            reached = halo_line[i : i + 1, side * HALO * SPAN : (side + 1) * HALO * SPAN]
            halo_weights[side, at : at + BLOCK, :] = staircase(reached, BLOCK)

    offset = jnp.where(at_top, 0, rows - polar)
    of_basis = lane // (polar * BLOCK)
    step = base + offset + lax.rem(lane // BLOCK, polar) - first
    at_start = lax.rem(lane, BLOCK) == 0
    terms = []
    for t in range(band):
        value = spread[t][0]
        for k in range(1, basis):
            value = jnp.where(of_basis == k, spread[t][k], value)
        terms.append(((step == t) & (count > t) & at_start, value))
    line = chosen(terms)
    for i in range(rows):
        polar_weights[i * BLOCK : (i + 1) * BLOCK, :] = staircase(line[i : i + 1], BLOCK)
    copies[5].wait()

    @pl.when(at_top & (lax.axis_index("lon") == 0))
    def top():
        polar_matrices(cycle_taps, turned, True)

    copies[4].wait()
    copies[6].wait()


def pack_kernel(fields, other, message):
    rows, cols, _ = fields.shape
    reach = (message.shape[1] - cols) // 2
    start = jnp.where(lax.axis_index("lon") == 0, rows - HALO, 0)
    for p in range(HALO):
        near = other[start + p]
        message[p] = jnp.concatenate(
            [near[cols - reach :], fields[start + p], near[:reach]], axis=0
        )


def own_kernel(turned_in, own_weights, cycle_taps, fields, mix, acc, turned, ext, hidden):
    del turned_in
    rows, cols, chans = fields.shape
    basis = mix.shape[0] // chans
    near = (SPAN - BLOCK) // 4

    lat_pos = lax.axis_index("lat")

    @pl.when((lat_pos == 0) & (lax.axis_index("lon") != 0))
    def top():
        polar_matrices(cycle_taps, turned, True)

    @pl.when(lat_pos == lax.axis_size("lat") - 1)
    def bottom():
        polar_matrices(cycle_taps, turned, False)

    blank = jnp.zeros((near, chans), BF16)
    pad = jnp.zeros((ext.shape[1] - cols - near, chans), BF16)
    for r in range(rows):
        ext[r] = jnp.concatenate([blank, fields[r], pad], axis=0)
    groups = [(i, k) for k in range(basis) for i in range(rows)]
    inner = cols - 2 * BLOCK
    for at in range(BLOCK, cols - BLOCK, BLOCK):
        window_products(
            own_weights, ext[:, at : at + SPAN, :], hidden, groups, inner, at - BLOCK, chans
        )
    half = rows // 2
    for n in range(2):
        at = slice(n * half, (n + 1) * half)
        total = matmul(hidden[n * half * inner : (n + 1) * half * inner], mix[...])
        acc[at, BLOCK : cols - BLOCK, :] = total.reshape(half, inner, chans) + fields[
            at, BLOCK : cols - BLOCK, :
        ].astype(F32)


def partner_kernel(
    acc_in, own_weights, polar_weights, turned, fields, mix, other,
    acc, hidden, cycle_rows, mixed_rows,
):
    del acc_in
    rows, cols, chans = fields.shape
    polar = turned.shape[0]
    basis = mix.shape[0] // chans
    reach = (SPAN - BLOCK) // 4
    lat_pos = lax.axis_index("lat")
    at_top = lat_pos == 0
    at_bottom = lat_pos == lax.axis_size("lat") - 1
    groups = [(i, k) for k in range(basis) for i in range(rows)]
    left, right = [], []
    pad = jnp.zeros((SPAN - BLOCK - 2 * reach, chans), BF16)
    for r in range(rows):
        left.append(
            jnp.concatenate([other[r, cols - reach :], fields[r, : SPAN - reach]], axis=0)
        )
        right.append(
            jnp.concatenate(
                [fields[r, cols - BLOCK - reach :], other[r, :reach], pad], axis=0
            )
        )
    for n, cells in enumerate((left, right)):
        window_products(
            own_weights, jnp.concatenate(cells, axis=0), hidden, groups, 2 * BLOCK, n * BLOCK,
            chans,
        )
    total = matmul(hidden[...], mix[...]).reshape(rows, 2 * BLOCK, chans)
    for n, at in enumerate((slice(0, BLOCK), slice(cols - BLOCK, cols))):
        acc[:, at, :] = total[:, n * BLOCK : (n + 1) * BLOCK] + fields[:, at, :].astype(F32)

    @pl.when(at_top | at_bottom)
    def polar_part():
        offset = jnp.where(at_top, 0, rows - polar)
        for p in range(polar):
            whole = jnp.concatenate([fields[offset + p], other[offset + p]], axis=0)
            part = matmul(turned[p], whole).astype(BF16)
            for k in range(basis):
                cycle_rows[k, p * cols : (p + 1) * cols, :] = part[k * cols : (k + 1) * cols]
        for k in range(basis):
            part = matmul(cycle_rows[k], mix[k * chans : (k + 1) * chans, :]).astype(BF16)
            mixed_rows[k * polar : (k + 1) * polar] = part.reshape(polar, cols, chans)
        for b in range(cols // BLOCK):
            at = slice(BLOCK * b, BLOCK * (b + 1))
            cells = mixed_rows[:, at, :].reshape(-1, chans)
            acc[:, at, :] = acc[:, at, :] + matmul(polar_weights[...], cells).reshape(
                rows, BLOCK, chans
            )


def side_rows(
    side, halo, weights, acc, mix, ext, hidden, present, result, ready=lambda at: None
):
    half, cols, chans = result.shape
    basis = mix.shape[0] // chans
    rows = pl.ds(side * half, half)
    wide = cols // 2
    parts = [slice(n * wide, (n + 1) * wide) for n in range(2)]

    @pl.when(present)
    def arrived():
        for p in range(HALO):
            cells = halo(p)
            pad = jnp.zeros((ext.shape[1] - cells.shape[0], chans), BF16)
            ext[p] = jnp.concatenate([cells, pad], axis=0)
        groups = [(i, k) for k in range(basis) for i in range(half)]
        for n, part in enumerate(parts):
            for at in range(0, wide, BLOCK):
                cells = ext[:, part.start + at : part.start + at + SPAN, :]
                window_products(
                    weights.at[side], cells, hidden.at[n], groups, wide, at, chans
                )
        for n, part in enumerate(parts):
            total = matmul(hidden[n], mix[...]).reshape(half, wide, chans)
            result[:, part, :] = (total + acc[rows, part, :]).astype(BF16)
            ready(part)

    @pl.when(jnp.logical_not(present))
    def absent():
        for part in parts:
            result[:, part, :] = acc[rows, part, :].astype(BF16)
            ready(part)


def from_side(which):
    core = lax.axis_index("lon")
    side = 1 - core if which == 0 else core
    lat_pos = lax.axis_index("lat")
    last = lax.axis_size("lat") - 1
    present = jnp.where(side == 0, lat_pos != 0, lat_pos != last)
    return side, present


def early_kernel(halo, edges, weights, acc, mix, result, ext, hidden):
    side, present = from_side(0)
    reach = edges.shape[1] // 2

    def cells(p):
        edge = edges[p]
        return jnp.concatenate([edge[reach:], halo[p], edge[:reach]], axis=0)

    side_rows(side, cells, weights, acc, mix, ext, hidden, present, result)


def late_kernel(early, halo, weights, acc, mix, out, ext, hidden, result, sems):
    half, cols, _ = result.shape
    side, present = from_side(1)
    rows = pl.ds(side * half, half)
    other_rows = pl.ds((1 - side) * half, half)

    def copy_of(part):
        n = 0 if part.start == 0 else 1
        return pltpu.make_async_copy(
            result.at[:, part, :], out.at[rows, part, :], sems.at[n]
        )

    first = pltpu.make_async_copy(early, out.at[other_rows], sems.at[2])
    first.start()
    side_rows(
        side, lambda p: halo[p], weights, acc, mix, ext, hidden, present, result,
        lambda part: copy_of(part).start(),
    )
    first.wait()
    for n in range(2):
        copy_of(slice(n * cols // 2, (n + 1) * cols // 2)).wait()


def shards(fields, lon_taps, lat_taps, cycle_taps, band_start, band_width, mixing):
    rows, cols, chans = fields.shape
    row_total, basis, taps = lon_taps.shape
    band = lat_taps.shape[2]
    reach = (taps - 1) // 2
    polar = cycle_taps.shape[1] // 2
    cycle = cycle_taps.shape[2]
    lat_count = lax.axis_size("lat")
    core = lax.axis_index("lon")
    axes = ("lat", "lon")
    assert cycle == 2 * cols and rows == 2 * HALO and basis * polar * BLOCK == rows * SPAN
    assert reach == (SPAN - BLOCK) // 4
    ahead, back = ring(lat_count, 1), ring(lat_count, -1)
    other = lax.ppermute(fields, "lon", SWAP)
    going = jnp.where(core == 0, fields[:HALO], fields[rows - HALO :])
    second = lax.ppermute(going, axes, back)
    going, band_start = lax.optimization_barrier((going, band_start))

    vmem = pl.BlockSpec(memory_space=pltpu.VMEM)
    hbm = pl.BlockSpec(memory_space=pltpu.HBM)
    sds = jax.ShapeDtypeStruct
    group = basis * rows * BLOCK
    ext_cols = cols + SPAN - BLOCK
    limit = pltpu.CompilerParams(vmem_limit_bytes=32 * 1024 * 1024)
    small = pl.CostEstimate(flops=100_000, bytes_accessed=1_000, transcendentals=0)
    halo_weights, own_weights, polar_weights, turns, whole, mix, turned = pl.pallas_call(
        weight_kernel,
        out_shape=(
            sds((2, group // 2, HALO * SPAN), BF16),
            sds((group, rows * SPAN), BF16),
            sds((rows * BLOCK, rows * SPAN), BF16),
            sds((basis, 2 * polar, cycle), BF16),
            sds((rows, cols, chans), BF16),
            sds((basis * chans, chans), BF16),
            sds((polar, basis * cols, cycle), BF16),
        ),
        in_specs=[hbm] * 7,
        out_specs=[vmem] * 7,
        scratch_shapes=[
            pltpu.SMEM((rows,), jnp.int32),
            pltpu.SMEM((rows,), jnp.int32),
            pltpu.VMEM((taps, basis, row_total), F32),
            pltpu.VMEM((band, basis, rows), BF16),
            pltpu.VMEM((128, -(-row_total // 128) * 128), F32),
            pltpu.VMEM((128, 128), F32),
            pltpu.SemaphoreType.DMA((7,)),
        ],
        compiler_params=limit,
        cost_estimate=pl.CostEstimate(
            flops=100_000, bytes_accessed=1_000, transcendentals=0
        ),
        name="filter_weights",
    )(
        *(
            pltpu.with_memory_space_constraint(x, pltpu.HBM)
            for x in (
                band_start, band_width, jnp.transpose(lon_taps, (2, 1, 0)),
                jnp.transpose(lat_taps, (2, 1, 0)), fields, cycle_taps,
                mixing.reshape(basis * chans, chans),
            )
        ),
    )
    message = pl.pallas_call(
        pack_kernel,
        out_shape=sds((HALO, cols + 2 * reach, chans), BF16),
        in_specs=[vmem] * 2,
        out_specs=vmem,
        compiler_params=limit,
        cost_estimate=small,
        name="late_message",
    )(whole, other)
    first = lax.ppermute(message, axes, ahead)
    edges = jnp.concatenate([other[:, :reach], other[:, cols - reach :]], axis=1)
    upper, lower = edges[:HALO], edges[rows - HALO :]
    second_edges = lax.ppermute(jnp.where(core == 0, upper, lower), axes, back)
    acc, turned = pl.pallas_call(
        own_kernel,
        out_shape=(
            sds((rows, cols, chans), F32),
            sds((polar, basis * cols, cycle), BF16),
        ),
        in_specs=[vmem] * 5,
        out_specs=(vmem, vmem),
        input_output_aliases={0: 1},
        scratch_shapes=[
            pltpu.VMEM((rows, ext_cols, chans), BF16),
            pltpu.VMEM((rows * (cols - 2 * BLOCK), basis * chans), BF16),
        ],
        compiler_params=limit,
        cost_estimate=pl.CostEstimate(
            flops=100_000, bytes_accessed=1_000, transcendentals=0
        ),
        name="own_rows",
    )(turned, own_weights, turns, whole, mix)

    acc = pl.pallas_call(
        partner_kernel,
        out_shape=sds((rows, cols, chans), F32),
        in_specs=[vmem] * 7,
        out_specs=vmem,
        input_output_aliases={0: 0},
        scratch_shapes=[
            pltpu.VMEM((rows * 2 * BLOCK, basis * chans), BF16),
            pltpu.VMEM((basis, polar * cols, chans), BF16),
            pltpu.VMEM((basis * polar, cols, chans), BF16),
        ],
        compiler_params=limit,
        cost_estimate=pl.CostEstimate(
            flops=100_000, bytes_accessed=1_000, transcendentals=0
        ),
        name="partner_columns",
    )(acc, own_weights, polar_weights, turned, whole, mix, other)

    half = rows // 2
    scratch = [
        pltpu.VMEM((HALO, ext_cols, chans), BF16),
        pltpu.VMEM((2, half * cols // 2, basis * chans), BF16),
    ]
    limit = pltpu.CompilerParams(vmem_limit_bytes=32 * 1024 * 1024)
    second, second_edges, acc = lax.optimization_barrier((second, second_edges, acc))
    early = pl.pallas_call(
        early_kernel,
        out_shape=sds((half, cols, chans), BF16),
        in_specs=[vmem] * 5,
        out_specs=vmem,
        scratch_shapes=scratch,
        compiler_params=limit,
        cost_estimate=pl.CostEstimate(
            flops=300_000_000, bytes_accessed=1_000_000, transcendentals=0
        ),
        name="early_side",
    )(second, second_edges, halo_weights, acc, mix)
    first, early = lax.optimization_barrier((first, early))
    return pl.pallas_call(
        late_kernel,
        out_shape=sds((rows, cols, chans), BF16),
        in_specs=[vmem] * 5,
        out_specs=hbm,
        scratch_shapes=[
            *scratch,
            pltpu.VMEM((half, cols, chans), BF16),
            pltpu.SemaphoreType.DMA((3,)),
        ],
        compiler_params=limit,
        name="late_side",
    )(early, first, halo_weights, acc, mix)


def solution(mesh):
    in_specs = (
        P(("ens", "lat"), "lon", None),
        P(),
        P("lat", None, None),
        P(),
        P("lat"),
        P("lat"),
        P(),
    )
    out_specs = P(("ens", "lat"), "lon", None)
    return jax.shard_map(shards, mesh=mesh, in_specs=in_specs, out_specs=out_specs, check_vma=False)
```

```python
import functools

import jax
import jax.numpy as jnp
from jax import lax
from jax.experimental import pallas as pl
from jax.experimental.pallas import tpu as pltpu
from jax.sharding import PartitionSpec as P

HALO = 4
BLOCK = 16
SPAN = 32
SWAP = [(0, 1), (1, 0)]
F32, BF16 = jnp.float32, jnp.bfloat16


def ring(lat_count, step):
    pairs = []
    for lat in range(lat_count):
        for core in range(2):
            to = lat + (step if core == 0 else -step)
            if 0 <= to < lat_count:
                pairs.append((lat * 2 + core, to * 2 + core))
            else:
                pairs.append((lat * 2 + core, lat * 2 + 1 - core))
    return pairs


def matmul(a, b):
    return jnp.dot(a, b, preferred_element_type=F32)


def staircase(line, steps):
    wide = jnp.broadcast_to(line, (steps, line.shape[1]))
    return pltpu.roll(wide, 0, 1, stride=1, stride_axis=0).astype(BF16)


def chosen(terms):
    total = None
    for mask, value in terms:
        term = jnp.where(mask, value, 0.0)
        total = term if total is None else total + term
    return total


def window_products(weights, cells, hidden, groups, width, offset, chans):
    part = matmul(weights[...], cells.reshape(-1, chans)).astype(BF16)
    for n, (i, k) in enumerate(groups):
        at = i * width + offset
        hidden[at : at + BLOCK, k * chans : (k + 1) * chans] = part[n * BLOCK : (n + 1) * BLOCK]


def polar_matrices(cycle_taps, turned, at_top):
    basis, twice, cycle = cycle_taps.shape
    polar = twice // 2
    cols = turned.shape[1] // basis
    total = lax.broadcasted_iota(jnp.int32, (cycle, cycle), 0) + lax.broadcasted_iota(
        jnp.int32, (cycle, cycle), 1
    )
    turn = jnp.where((total == 0) | (total == cycle), 1.0, 0.0).astype(BF16)
    negated = matmul(cycle_taps[...].reshape(-1, cycle), turn)
    for p in range(polar):
        for k in range(basis):
            n = k * twice + (p if at_top else p + polar)
            turned[p, k * cols : (k + 1) * cols, :] = staircase(negated[n : n + 1], cols)


def weight_kernel(
    late, start_in, width_in, lon_in, lat_in, cycle_in, mixing_in, *refs,
):
    if late:
        refs = refs[6:]
    halo_weights, own_weights, polar_weights, cycle_taps, mix, turned = refs[:6]
    start, width, lon, lat, lon_wide, lat_wide, sems = refs[6:]
    rows = halo_weights.shape[0] * HALO
    taps, basis, row_total = lon.shape
    band = lat.shape[0]
    polar = cycle_taps.shape[1] // 2
    lat_pos = lax.axis_index("lat")
    base = lat_pos * rows
    at_top = base == 0

    is_early = at_top & (lax.axis_index("lon") == 0)

    @pl.when(jnp.logical_not(is_early) if late else is_early)
    def make():
        copies = []
        for n, (source, target) in enumerate(
            [
                (lon_in, lon), (lat_in, lat), (start_in, start), (width_in, width),
                (cycle_in, cycle_taps), (mixing_in, mix),
            ]
        ):
            copies.append(pltpu.make_async_copy(source, target, sems.at[n]))
            copies[-1].start()
        lon_wide[...] = jnp.zeros_like(lon_wide)
        lat_wide[...] = jnp.zeros_like(lat_wide)
        for n in range(4):
            copies[n].wait()

        for d in range(taps):
            for k in range(basis):
                lon_wide[k * 16 + d : k * 16 + d + 1, 0:row_total] = lon[d, k : k + 1, :]
        lanes = lon_wide.shape[1]
        slots = pltpu.roll(lon_wide[...], lax.rem(lanes + HALO - base, lanes), 1)[:, :128]
        slots = jnp.transpose(slots)[: rows + 2 * HALO]
        is_tap = lax.broadcasted_iota(jnp.int32, slots.shape, 1) < taps
        own_taps, halo_taps = [], []
        for k in range(basis):
            moved = slots if k == 0 else pltpu.roll(slots, 128 - 16 * k, 1)
            moved = jnp.where(is_tap, moved, 0.0)
            for _ in range(2):
                moved = pltpu.roll(moved, 0, 1, stride=SPAN // 2, stride_axis=0)
            quads = [jnp.sum(moved[4 * q : 4 * q + 4], axis=0, keepdims=True) for q in range(4)]
            own_taps.append(jnp.concatenate([quads[1], quads[2]], axis=1))
            halo_taps.append(jnp.concatenate([quads[0], quads[3]], axis=1))

        for t in range(band):
            lat_wide[t * basis : (t + 1) * basis, 0:rows] = lat[t].astype(F32)
        lat_cols = jnp.transpose(lat_wide[...])[:rows]
        shape = (rows, rows * SPAN)
        lane = lax.broadcasted_iota(jnp.int32, shape, 1)
        out_row = lax.broadcasted_iota(jnp.int32, shape, 0)
        first = jnp.zeros(shape, jnp.int32)
        count = jnp.zeros(shape, jnp.int32)
        for i in range(rows):
            first = jnp.where(out_row == i, start[i], first)
            count = jnp.where(out_row == i, width[i], count)
        spread = [
            [
                jnp.broadcast_to(lat_cols[:, t * basis + k : t * basis + k + 1], shape)
                for k in range(basis)
            ]
            for t in range(band)
        ]
        slot = lane // SPAN
        own_row = base + slot
        halo_row = jnp.where(slot < HALO, own_row - HALO, own_row + rows - HALO)
        is_polar = (own_row < polar) | (own_row >= row_total - polar)
        in_grid = (halo_row >= 0) & (halo_row < row_total)
        own_step, halo_step = own_row - first, halo_row - first
        own_used = [(own_step == t) & (count > t) & ~is_polar for t in range(band)]
        halo_used = [(halo_step == t) & (count > t) & in_grid for t in range(band)]
        for k in range(basis):
            own_line = own_taps[k] * chosen([(own_used[t], spread[t][k]) for t in range(band)])
            halo_line = halo_taps[k] * chosen([(halo_used[t], spread[t][k]) for t in range(band)])
            for i in range(rows):
                at = (k * rows + i) * BLOCK
                own_weights[at : at + BLOCK, :] = staircase(own_line[i : i + 1], BLOCK)
                side, at = i // HALO, (k * HALO + i % HALO) * BLOCK
                reached = halo_line[i : i + 1, side * HALO * SPAN : (side + 1) * HALO * SPAN]
                halo_weights[side, at : at + BLOCK, :] = staircase(reached, BLOCK)

        offset = jnp.where(at_top, 0, rows - polar)
        of_basis = lane // (polar * BLOCK)
        step = base + offset + lax.rem(lane // BLOCK, polar) - first
        at_start = lax.rem(lane, BLOCK) == 0
        terms = []
        for t in range(band):
            value = spread[t][0]
            for k in range(1, basis):
                value = jnp.where(of_basis == k, spread[t][k], value)
            terms.append(((step == t) & (count > t) & at_start, value))
        line = chosen(terms)
        for i in range(rows):
            polar_weights[i * BLOCK : (i + 1) * BLOCK, :] = staircase(line[i : i + 1], BLOCK)
        copies[4].wait()

        @pl.when(at_top & (lax.axis_index("lon") == 0))
        def top():
            polar_matrices(cycle_taps, turned, True)

        copies[5].wait()


def stage_kernel(going, staying, whole, edges, polar_left, polar_right):
    cols = whole.shape[1]
    reach = edges.shape[1] // 2
    is_first = lax.axis_index("lon") == 0
    at_top = lax.axis_index("lat") == 0
    for p in range(HALO):
        upper = jnp.where(is_first, going[p], staying[p])
        lower = jnp.where(is_first, staying[p], going[p])
        polar = jnp.where(at_top, upper, lower)
        polar_left[p], polar_right[p] = polar[: cols // 2], polar[cols // 2 :]
        for r, row in ((p, upper), (HALO + p, lower)):
            whole[r] = row
            edges[r] = jnp.concatenate([row[:reach], row[cols - reach :]], axis=0)


def pack_kernel(whole, edges, message, corners):
    rows = whole.shape[0]
    reach = edges.shape[1] // 2
    start = jnp.where(lax.axis_index("lon") == 0, rows - HALO, 0)
    early = rows - HALO - start
    for p in range(HALO):
        near = edges[start + p]
        message[p] = jnp.concatenate([near[reach:], whole[start + p], near[:reach]], axis=0)
        corners[p] = edges[early + p]


def own_kernel(turned_in, own_weights, cycle_taps, fields, mix, acc, turned, ext, hidden):
    del turned_in
    rows, cols, chans = fields.shape
    basis = mix.shape[0] // chans
    near = (SPAN - BLOCK) // 4

    lat_pos = lax.axis_index("lat")

    @pl.when((lat_pos == 0) & (lax.axis_index("lon") != 0))
    def top():
        polar_matrices(cycle_taps, turned, True)

    @pl.when(lat_pos == lax.axis_size("lat") - 1)
    def bottom():
        polar_matrices(cycle_taps, turned, False)

    blank = jnp.zeros((near, chans), BF16)
    pad = jnp.zeros((ext.shape[1] - cols - near, chans), BF16)
    for r in range(rows):
        ext[r] = jnp.concatenate([blank, fields[r], pad], axis=0)
    groups = [(i, k) for k in range(basis) for i in range(rows)]
    inner = cols - 2 * BLOCK
    for at in range(BLOCK, cols - BLOCK, BLOCK):
        window_products(
            own_weights, ext[:, at : at + SPAN, :], hidden, groups, inner, at - BLOCK, chans
        )
    half = rows // 2
    for n in range(2):
        at = slice(n * half, (n + 1) * half)
        total = matmul(hidden[n * half * inner : (n + 1) * half * inner], mix[...])
        acc[at, BLOCK : cols - BLOCK, :] = total.reshape(half, inner, chans) + fields[
            at, BLOCK : cols - BLOCK, :
        ].astype(F32)


def partner_kernel(
    acc_in, own_weights, polar_weights, turned, fields, mix, edges, polar_left, polar_right,
    acc, hidden, cycle_rows, mixed_rows,
):
    del acc_in
    rows, cols, chans = fields.shape
    polar = turned.shape[0]
    basis = mix.shape[0] // chans
    reach = (SPAN - BLOCK) // 4
    lat_pos = lax.axis_index("lat")
    at_top = lat_pos == 0
    at_bottom = lat_pos == lax.axis_size("lat") - 1
    groups = [(i, k) for k in range(basis) for i in range(rows)]
    left, right = [], []
    pad = jnp.zeros((SPAN - BLOCK - 2 * reach, chans), BF16)
    for r in range(rows):
        left.append(
            jnp.concatenate([edges[r, reach:], fields[r, : SPAN - reach]], axis=0)
        )
        right.append(
            jnp.concatenate(
                [fields[r, cols - BLOCK - reach :], edges[r, :reach], pad], axis=0
            )
        )
    for n, cells in enumerate((left, right)):
        window_products(
            own_weights, jnp.concatenate(cells, axis=0), hidden, groups, 2 * BLOCK, n * BLOCK,
            chans,
        )
    total = matmul(hidden[...], mix[...]).reshape(rows, 2 * BLOCK, chans)
    for n, at in enumerate((slice(0, BLOCK), slice(cols - BLOCK, cols))):
        acc[:, at, :] = total[:, n * BLOCK : (n + 1) * BLOCK] + fields[:, at, :].astype(F32)

    @pl.when(at_top | at_bottom)
    def polar_part():
        offset = jnp.where(at_top, 0, rows - polar)
        for p in range(polar):
            whole = jnp.concatenate(
                [fields[offset + p], polar_left[p], polar_right[p]], axis=0
            )
            part = matmul(turned[p], whole).astype(BF16)
            for k in range(basis):
                cycle_rows[k, p * cols : (p + 1) * cols, :] = part[k * cols : (k + 1) * cols]
        for k in range(basis):
            part = matmul(cycle_rows[k], mix[k * chans : (k + 1) * chans, :]).astype(BF16)
            mixed_rows[k * polar : (k + 1) * polar] = part.reshape(polar, cols, chans)
        for b in range(cols // BLOCK):
            at = slice(BLOCK * b, BLOCK * (b + 1))
            cells = mixed_rows[:, at, :].reshape(-1, chans)
            acc[:, at, :] = acc[:, at, :] + matmul(polar_weights[...], cells).reshape(
                rows, BLOCK, chans
            )


def side_rows(
    side, halo, weights, acc, mix, ext, hidden, present, result, ready=lambda at: None
):
    half, cols, chans = result.shape
    basis = mix.shape[0] // chans
    rows = pl.ds(side * half, half)
    wide = cols // 2
    parts = [slice(n * wide, (n + 1) * wide) for n in range(2)]

    @pl.when(present)
    def arrived():
        for p in range(HALO):
            cells = halo(p)
            pad = jnp.zeros((ext.shape[1] - cells.shape[0], chans), BF16)
            ext[p] = jnp.concatenate([cells, pad], axis=0)
        groups = [(i, k) for k in range(basis) for i in range(half)]
        for n, part in enumerate(parts):
            for at in range(0, wide, BLOCK):
                cells = ext[:, part.start + at : part.start + at + SPAN, :]
                window_products(
                    weights.at[side], cells, hidden.at[n], groups, wide, at, chans
                )
        for n, part in enumerate(parts):
            total = matmul(hidden[n], mix[...]).reshape(half, wide, chans)
            result[:, part, :] = (total + acc[rows, part, :]).astype(BF16)
            ready(part)

    @pl.when(jnp.logical_not(present))
    def absent():
        for part in parts:
            result[:, part, :] = acc[rows, part, :].astype(BF16)
            ready(part)


def from_side(which):
    core = lax.axis_index("lon")
    side = 1 - core if which == 0 else core
    lat_pos = lax.axis_index("lat")
    last = lax.axis_size("lat") - 1
    present = jnp.where(side == 0, lat_pos != 0, lat_pos != last)
    return side, present


def early_kernel(halo, edges, weights, acc, mix, result, ext, hidden):
    side, present = from_side(0)
    reach = edges.shape[1] // 2

    def cells(p):
        edge = edges[p]
        return jnp.concatenate([edge[reach:], halo[p], edge[:reach]], axis=0)

    side_rows(side, cells, weights, acc, mix, ext, hidden, present, result)


def late_kernel(early, halo, weights, acc, mix, out, ext, hidden, result, sems):
    half, cols, _ = result.shape
    side, present = from_side(1)
    rows = pl.ds(side * half, half)
    other_rows = pl.ds((1 - side) * half, half)

    def copy_of(part):
        n = 0 if part.start == 0 else 1
        return pltpu.make_async_copy(
            result.at[:, part, :], out.at[rows, part, :], sems.at[n]
        )

    first = pltpu.make_async_copy(early, out.at[other_rows], sems.at[2])
    first.start()
    side_rows(
        side, lambda p: halo[p], weights, acc, mix, ext, hidden, present, result,
        lambda part: copy_of(part).start(),
    )
    first.wait()
    for n in range(2):
        copy_of(slice(n * cols // 2, (n + 1) * cols // 2)).wait()


def shards(fields, lon_taps, lat_taps, cycle_taps, band_start, band_width, mixing):
    rows, cols, chans = fields.shape
    row_total, basis, taps = lon_taps.shape
    band = lat_taps.shape[2]
    reach = (taps - 1) // 2
    polar = cycle_taps.shape[1] // 2
    cycle = cycle_taps.shape[2]
    lat_count = lax.axis_size("lat")
    core = lax.axis_index("lon")
    axes = ("lat", "lon")
    assert cycle == 2 * cols and rows == 2 * HALO and basis * polar * BLOCK == rows * SPAN
    assert reach == (SPAN - BLOCK) // 4 and polar == HALO
    ahead, back = ring(lat_count, 1), ring(lat_count, -1)
    head, tail = fields[:HALO], fields[rows - HALO :]
    going = jnp.where(core == 0, head, tail)
    staying = jnp.where(core == 0, tail, head)
    second = lax.ppermute(going, axes, back)
    going, staying, band_start = lax.optimization_barrier((going, staying, band_start))

    vmem = pl.BlockSpec(memory_space=pltpu.VMEM)
    hbm = pl.BlockSpec(memory_space=pltpu.HBM)
    sds = jax.ShapeDtypeStruct
    group = basis * rows * BLOCK
    ext_cols = cols + SPAN - BLOCK
    limit = pltpu.CompilerParams(vmem_limit_bytes=32 * 1024 * 1024)
    small = pl.CostEstimate(flops=100_000, bytes_accessed=1_000, transcendentals=0)
    large = pl.CostEstimate(flops=1_600_000_000, bytes_accessed=1_000, transcendentals=0)
    weight_shapes = (
        sds((2, group // 2, HALO * SPAN), BF16),
        sds((group, rows * SPAN), BF16),
        sds((rows * BLOCK, rows * SPAN), BF16),
        sds((basis, 2 * polar, cycle), BF16),
        sds((basis * chans, chans), BF16),
        sds((polar, basis * cols, cycle), BF16),
    )

    def weights(made):
        operands = [
            pltpu.with_memory_space_constraint(x, pltpu.HBM)
            for x in (
                band_start, band_width, jnp.transpose(lon_taps, (2, 1, 0)),
                jnp.transpose(lat_taps, (2, 1, 0)), cycle_taps,
                mixing.reshape(basis * chans, chans),
            )
        ]
        return pl.pallas_call(
            functools.partial(weight_kernel, bool(made)),
            out_shape=weight_shapes,
            in_specs=[hbm] * 6 + [vmem] * len(made),
            out_specs=[vmem] * 6,
            input_output_aliases={6 + n: n for n in range(len(made))},
            scratch_shapes=[
                pltpu.SMEM((rows,), jnp.int32),
                pltpu.SMEM((rows,), jnp.int32),
                pltpu.VMEM((taps, basis, row_total), F32),
                pltpu.VMEM((band, basis, rows), BF16),
                pltpu.VMEM((128, -(-row_total // 128) * 128), F32),
                pltpu.VMEM((128, 128), F32),
                pltpu.SemaphoreType.DMA((6,)),
            ],
            compiler_params=limit,
            cost_estimate=small,
            name="filter_weights" if made else "first_weights",
        )(*operands, *made)

    made = weights(())
    going, made = lax.optimization_barrier((going, made))
    whole, edges, polar_left, polar_right = pl.pallas_call(
        stage_kernel,
        out_shape=(
            sds((rows, cols, chans), BF16),
            sds((rows, 2 * reach, chans), BF16),
            sds((polar, cols // 2, chans), BF16),
            sds((polar, cols // 2, chans), BF16),
        ),
        in_specs=[vmem] * 2,
        out_specs=[vmem] * 4,
        compiler_params=limit,
        cost_estimate=small,
        name="stage_rows",
    )(going, staying)
    edges = lax.ppermute(edges, "lon", SWAP)
    polar_left = lax.ppermute(polar_left, "lon", SWAP)
    polar_right = lax.ppermute(polar_right, "lon", SWAP)
    message, corners = pl.pallas_call(
        pack_kernel,
        out_shape=(
            sds((HALO, cols + 2 * reach, chans), BF16),
            sds((HALO, 2 * reach, chans), BF16),
        ),
        in_specs=[vmem] * 2,
        out_specs=(vmem, vmem),
        compiler_params=limit,
        cost_estimate=small,
        name="pack_messages",
    )(whole, edges)
    first = lax.ppermute(message, axes, ahead)
    second_edges = lax.ppermute(corners, axes, back)
    corners, made = lax.optimization_barrier((corners, made))
    halo_weights, own_weights, polar_weights, turns, mix, turned = weights(made)
    acc, turned = pl.pallas_call(
        own_kernel,
        out_shape=(
            sds((rows, cols, chans), F32),
            sds((polar, basis * cols, cycle), BF16),
        ),
        in_specs=[vmem] * 5,
        out_specs=(vmem, vmem),
        input_output_aliases={0: 1},
        scratch_shapes=[
            pltpu.VMEM((rows, ext_cols, chans), BF16),
            pltpu.VMEM((rows * (cols - 2 * BLOCK), basis * chans), BF16),
        ],
        compiler_params=limit,
        cost_estimate=pl.CostEstimate(
            flops=100_000, bytes_accessed=1_000, transcendentals=0
        ),
        name="own_rows",
    )(turned, own_weights, turns, whole, mix)

    acc = pl.pallas_call(
        partner_kernel,
        out_shape=sds((rows, cols, chans), F32),
        in_specs=[vmem] * 9,
        out_specs=vmem,
        input_output_aliases={0: 0},
        scratch_shapes=[
            pltpu.VMEM((rows * 2 * BLOCK, basis * chans), BF16),
            pltpu.VMEM((basis, polar * cols, chans), BF16),
            pltpu.VMEM((basis * polar, cols, chans), BF16),
        ],
        compiler_params=limit,
        cost_estimate=pl.CostEstimate(
            flops=100_000, bytes_accessed=1_000, transcendentals=0
        ),
        name="partner_columns",
    )(acc, own_weights, polar_weights, turned, whole, mix, edges, polar_left, polar_right)

    half = rows // 2
    scratch = [
        pltpu.VMEM((HALO, ext_cols, chans), BF16),
        pltpu.VMEM((2, half * cols // 2, basis * chans), BF16),
    ]
    limit = pltpu.CompilerParams(vmem_limit_bytes=32 * 1024 * 1024)
    second, second_edges, acc = lax.optimization_barrier((second, second_edges, acc))
    early = pl.pallas_call(
        early_kernel,
        out_shape=sds((half, cols, chans), BF16),
        in_specs=[vmem] * 5,
        out_specs=vmem,
        scratch_shapes=scratch,
        compiler_params=limit,
        cost_estimate=large,
        name="early_side",
    )(second, second_edges, halo_weights, acc, mix)
    first, early = lax.optimization_barrier((first, early))
    return pl.pallas_call(
        late_kernel,
        out_shape=sds((rows, cols, chans), BF16),
        in_specs=[vmem] * 5,
        out_specs=hbm,
        scratch_shapes=[
            *scratch,
            pltpu.VMEM((half, cols, chans), BF16),
            pltpu.SemaphoreType.DMA((3,)),
        ],
        compiler_params=limit,
        name="late_side",
    )(early, first, halo_weights, acc, mix)


def solution(mesh):
    in_specs = (
        P(("ens", "lat"), "lon", None),
        P(),
        P("lat", None, None),
        P(),
        P("lat"),
        P("lat"),
        P(),
    )
    out_specs = P(("ens", "lat"), "lon", None)
    return jax.shard_map(shards, mesh=mesh, in_specs=in_specs, out_specs=out_specs, check_vma=False)
```

```python
import functools

import jax
import jax.numpy as jnp
from jax import lax
from jax.experimental import pallas as pl
from jax.experimental.pallas import tpu as pltpu
from jax.sharding import PartitionSpec as P

HALO = 4
BLOCK = 16
SPAN = 32
SWAP = [(0, 1), (1, 0)]
F32, BF16 = jnp.float32, jnp.bfloat16


def ring(lat_count, step):
    pairs = []
    for lat in range(lat_count):
        for core in range(2):
            to = lat + (step if core == 0 else -step)
            if 0 <= to < lat_count:
                pairs.append((lat * 2 + core, to * 2 + core))
            else:
                pairs.append((lat * 2 + core, lat * 2 + 1 - core))
    return pairs


def matmul(a, b):
    return jnp.dot(a, b, preferred_element_type=F32)


def staircase(line, steps):
    wide = jnp.broadcast_to(line, (steps, line.shape[1]))
    return pltpu.roll(wide, 0, 1, stride=1, stride_axis=0).astype(BF16)


def chosen(terms):
    total = None
    for mask, value in terms:
        term = jnp.where(mask, value, 0.0)
        total = term if total is None else total + term
    return total


def window_products(weights, cells, hidden, groups, width, offset, chans):
    part = matmul(weights[...], cells.reshape(-1, chans)).astype(BF16)
    for n, (i, k) in enumerate(groups):
        at = i * width + offset
        hidden[at : at + BLOCK, k * chans : (k + 1) * chans] = part[n * BLOCK : (n + 1) * BLOCK]


def polar_matrices(cycle_taps, turned, at_top):
    basis, twice, cycle = cycle_taps.shape
    polar = twice // 2
    cols = turned.shape[1] // basis
    total = lax.broadcasted_iota(jnp.int32, (cycle, cycle), 0) + lax.broadcasted_iota(
        jnp.int32, (cycle, cycle), 1
    )
    turn = jnp.where((total == 0) | (total == cycle), 1.0, 0.0).astype(BF16)
    negated = matmul(cycle_taps[...].reshape(-1, cycle), turn)
    for p in range(polar):
        for k in range(basis):
            n = k * twice + (p if at_top else p + polar)
            turned[p, k * cols : (k + 1) * cols, :] = staircase(negated[n : n + 1], cols)


def weight_kernel(
    late, start_in, width_in, lon_in, lat_in, cycle_in, mixing_in, *refs,
):
    if late:
        refs = refs[6:]
    halo_weights, own_weights, polar_weights, cycle_taps, mix, turned = refs[:6]
    start, width, lon, lat, lon_wide, lat_wide, sems = refs[6:]
    rows = halo_weights.shape[0] * HALO
    taps, basis, row_total = lon.shape
    band = lat.shape[0]
    polar = cycle_taps.shape[1] // 2
    lat_pos = lax.axis_index("lat")
    base = lat_pos * rows
    at_top = base == 0

    is_early = at_top & (lax.axis_index("lon") == 0) & (lax.axis_index("ens") == 0)

    @pl.when(jnp.logical_not(is_early) if late else is_early)
    def make():
        copies = []
        for n, (source, target) in enumerate(
            [
                (lon_in, lon), (lat_in, lat), (start_in, start), (width_in, width),
                (cycle_in, cycle_taps), (mixing_in, mix),
            ]
        ):
            copies.append(pltpu.make_async_copy(source, target, sems.at[n]))
            copies[-1].start()
        lon_wide[...] = jnp.zeros_like(lon_wide)
        lat_wide[...] = jnp.zeros_like(lat_wide)
        for n in range(4):
            copies[n].wait()

        for d in range(taps):
            for k in range(basis):
                lon_wide[k * 16 + d : k * 16 + d + 1, 0:row_total] = lon[d, k : k + 1, :]
        lanes = lon_wide.shape[1]
        slots = pltpu.roll(lon_wide[...], lax.rem(lanes + HALO - base, lanes), 1)[:, :128]
        slots = jnp.transpose(slots)[: rows + 2 * HALO]
        is_tap = lax.broadcasted_iota(jnp.int32, slots.shape, 1) < taps
        own_taps, halo_taps = [], []
        for k in range(basis):
            moved = slots if k == 0 else pltpu.roll(slots, 128 - 16 * k, 1)
            moved = jnp.where(is_tap, moved, 0.0)
            for _ in range(2):
                moved = pltpu.roll(moved, 0, 1, stride=SPAN // 2, stride_axis=0)
            quads = [jnp.sum(moved[4 * q : 4 * q + 4], axis=0, keepdims=True) for q in range(4)]
            own_taps.append(jnp.concatenate([quads[1], quads[2]], axis=1))
            halo_taps.append(jnp.concatenate([quads[0], quads[3]], axis=1))

        for t in range(band):
            lat_wide[t * basis : (t + 1) * basis, 0:rows] = lat[t].astype(F32)
        lat_cols = jnp.transpose(lat_wide[...])[:rows]
        shape = (rows, rows * SPAN)
        lane = lax.broadcasted_iota(jnp.int32, shape, 1)
        out_row = lax.broadcasted_iota(jnp.int32, shape, 0)
        first = jnp.zeros(shape, jnp.int32)
        count = jnp.zeros(shape, jnp.int32)
        for i in range(rows):
            first = jnp.where(out_row == i, start[i], first)
            count = jnp.where(out_row == i, width[i], count)
        spread = [
            [
                jnp.broadcast_to(lat_cols[:, t * basis + k : t * basis + k + 1], shape)
                for k in range(basis)
            ]
            for t in range(band)
        ]
        slot = lane // SPAN
        own_row = base + slot
        halo_row = jnp.where(slot < HALO, own_row - HALO, own_row + rows - HALO)
        is_polar = (own_row < polar) | (own_row >= row_total - polar)
        in_grid = (halo_row >= 0) & (halo_row < row_total)
        own_step, halo_step = own_row - first, halo_row - first
        own_used = [(own_step == t) & (count > t) & ~is_polar for t in range(band)]
        halo_used = [(halo_step == t) & (count > t) & in_grid for t in range(band)]
        for k in range(basis):
            own_line = own_taps[k] * chosen([(own_used[t], spread[t][k]) for t in range(band)])
            halo_line = halo_taps[k] * chosen([(halo_used[t], spread[t][k]) for t in range(band)])
            for i in range(rows):
                at = (k * rows + i) * BLOCK
                own_weights[at : at + BLOCK, :] = staircase(own_line[i : i + 1], BLOCK)
                side, at = i // HALO, (k * HALO + i % HALO) * BLOCK
                reached = halo_line[i : i + 1, side * HALO * SPAN : (side + 1) * HALO * SPAN]
                halo_weights[side, at : at + BLOCK, :] = staircase(reached, BLOCK)

        offset = jnp.where(at_top, 0, rows - polar)
        of_basis = lane // (polar * BLOCK)
        step = base + offset + lax.rem(lane // BLOCK, polar) - first
        at_start = lax.rem(lane, BLOCK) == 0
        terms = []
        for t in range(band):
            value = spread[t][0]
            for k in range(1, basis):
                value = jnp.where(of_basis == k, spread[t][k], value)
            terms.append(((step == t) & (count > t) & at_start, value))
        line = chosen(terms)
        for i in range(rows):
            polar_weights[i * BLOCK : (i + 1) * BLOCK, :] = staircase(line[i : i + 1], BLOCK)
        copies[4].wait()

        copies[5].wait()


def stage_kernel(going, staying, whole, edges, polar_left, polar_right):
    cols = whole.shape[1]
    reach = edges.shape[1] // 2
    is_first = lax.axis_index("lon") == 0
    at_top = lax.axis_index("lat") == 0
    for p in range(HALO):
        upper = jnp.where(is_first, going[p], staying[p])
        lower = jnp.where(is_first, staying[p], going[p])
        polar = jnp.where(at_top, upper, lower)
        polar_left[p], polar_right[p] = polar[: cols // 2], polar[cols // 2 :]
        for r, row in ((p, upper), (HALO + p, lower)):
            whole[r] = row
            edges[r] = jnp.concatenate([row[:reach], row[cols - reach :]], axis=0)


def pack_kernel(whole, edges, message, corners):
    rows = whole.shape[0]
    reach = edges.shape[1] // 2
    start = jnp.where(lax.axis_index("lon") == 0, rows - HALO, 0)
    early = rows - HALO - start
    for p in range(HALO):
        near = edges[start + p]
        message[p] = jnp.concatenate([near[reach:], whole[start + p], near[:reach]], axis=0)
        corners[p] = edges[early + p]


def own_kernel(turned_in, own_weights, cycle_taps, fields, mix, acc, turned, ext, hidden):
    del turned_in
    rows, cols, chans = fields.shape
    basis = mix.shape[0] // chans
    near = (SPAN - BLOCK) // 4

    lat_pos = lax.axis_index("lat")

    @pl.when(lat_pos == 0)
    def top():
        polar_matrices(cycle_taps, turned, True)

    @pl.when(lat_pos == lax.axis_size("lat") - 1)
    def bottom():
        polar_matrices(cycle_taps, turned, False)

    blank = jnp.zeros((near, chans), BF16)
    pad = jnp.zeros((ext.shape[1] - cols - near, chans), BF16)
    for r in range(rows):
        ext[r] = jnp.concatenate([blank, fields[r], pad], axis=0)
    groups = [(i, k) for k in range(basis) for i in range(rows)]
    inner = cols - 2 * BLOCK
    for at in range(BLOCK, cols - BLOCK, BLOCK):
        window_products(
            own_weights, ext[:, at : at + SPAN, :], hidden, groups, inner, at - BLOCK, chans
        )
    half = rows // 2
    for n in range(2):
        at = slice(n * half, (n + 1) * half)
        total = matmul(hidden[n * half * inner : (n + 1) * half * inner], mix[...])
        acc[at, BLOCK : cols - BLOCK, :] = total.reshape(half, inner, chans) + fields[
            at, BLOCK : cols - BLOCK, :
        ].astype(F32)


def partner_kernel(
    acc_in, own_weights, polar_weights, turned, fields, mix, edges, polar_left, polar_right,
    acc, hidden, cycle_rows, mixed_rows,
):
    del acc_in
    rows, cols, chans = fields.shape
    polar = turned.shape[0]
    basis = mix.shape[0] // chans
    reach = (SPAN - BLOCK) // 4
    lat_pos = lax.axis_index("lat")
    at_top = lat_pos == 0
    at_bottom = lat_pos == lax.axis_size("lat") - 1
    groups = [(i, k) for k in range(basis) for i in range(rows)]
    left, right = [], []
    pad = jnp.zeros((SPAN - BLOCK - 2 * reach, chans), BF16)
    for r in range(rows):
        left.append(
            jnp.concatenate([edges[r, reach:], fields[r, : SPAN - reach]], axis=0)
        )
        right.append(
            jnp.concatenate(
                [fields[r, cols - BLOCK - reach :], edges[r, :reach], pad], axis=0
            )
        )
    for n, cells in enumerate((left, right)):
        window_products(
            own_weights, jnp.concatenate(cells, axis=0), hidden, groups, 2 * BLOCK, n * BLOCK,
            chans,
        )
    total = matmul(hidden[...], mix[...]).reshape(rows, 2 * BLOCK, chans)
    for n, at in enumerate((slice(0, BLOCK), slice(cols - BLOCK, cols))):
        acc[:, at, :] = total[:, n * BLOCK : (n + 1) * BLOCK] + fields[:, at, :].astype(F32)

    @pl.when(at_top | at_bottom)
    def polar_part():
        offset = jnp.where(at_top, 0, rows - polar)
        for p in range(polar):
            whole = jnp.concatenate(
                [fields[offset + p], polar_left[p], polar_right[p]], axis=0
            )
            part = matmul(turned[p], whole).astype(BF16)
            for k in range(basis):
                cycle_rows[k, p * cols : (p + 1) * cols, :] = part[k * cols : (k + 1) * cols]
        for k in range(basis):
            part = matmul(cycle_rows[k], mix[k * chans : (k + 1) * chans, :]).astype(BF16)
            mixed_rows[k * polar : (k + 1) * polar] = part.reshape(polar, cols, chans)
        for b in range(cols // BLOCK):
            at = slice(BLOCK * b, BLOCK * (b + 1))
            cells = mixed_rows[:, at, :].reshape(-1, chans)
            acc[:, at, :] = acc[:, at, :] + matmul(polar_weights[...], cells).reshape(
                rows, BLOCK, chans
            )


def side_rows(
    side, halo, weights, acc, mix, ext, hidden, present, result, ready=lambda at: None
):
    half, cols, chans = result.shape
    basis = mix.shape[0] // chans
    rows = pl.ds(side * half, half)
    wide = cols // 2
    parts = [slice(n * wide, (n + 1) * wide) for n in range(2)]

    @pl.when(present)
    def arrived():
        for p in range(HALO):
            cells = halo(p)
            pad = jnp.zeros((ext.shape[1] - cells.shape[0], chans), BF16)
            ext[p] = jnp.concatenate([cells, pad], axis=0)
        groups = [(i, k) for k in range(basis) for i in range(half)]
        for n, part in enumerate(parts):
            for at in range(0, wide, BLOCK):
                cells = ext[:, part.start + at : part.start + at + SPAN, :]
                window_products(
                    weights.at[side], cells, hidden.at[n], groups, wide, at, chans
                )
        for n, part in enumerate(parts):
            total = matmul(hidden[n], mix[...]).reshape(half, wide, chans)
            result[:, part, :] = (total + acc[rows, part, :]).astype(BF16)
            ready(part)

    @pl.when(jnp.logical_not(present))
    def absent():
        for part in parts:
            result[:, part, :] = acc[rows, part, :].astype(BF16)
            ready(part)


def from_side(which):
    core = lax.axis_index("lon")
    side = 1 - core if which == 0 else core
    lat_pos = lax.axis_index("lat")
    last = lax.axis_size("lat") - 1
    present = jnp.where(side == 0, lat_pos != 0, lat_pos != last)
    return side, present


def early_kernel(halo, edges, weights, acc, mix, result, ext, hidden):
    side, present = from_side(0)
    reach = edges.shape[1] // 2

    def cells(p):
        edge = edges[p]
        return jnp.concatenate([edge[reach:], halo[p], edge[:reach]], axis=0)

    side_rows(side, cells, weights, acc, mix, ext, hidden, present, result)


def late_kernel(early, halo, weights, acc, mix, out, ext, hidden, result, sems):
    half, cols, _ = result.shape
    side, present = from_side(1)
    rows = pl.ds(side * half, half)
    other_rows = pl.ds((1 - side) * half, half)

    def copy_of(part):
        n = 0 if part.start == 0 else 1
        return pltpu.make_async_copy(
            result.at[:, part, :], out.at[rows, part, :], sems.at[n]
        )

    first = pltpu.make_async_copy(early, out.at[other_rows], sems.at[2])
    first.start()
    side_rows(
        side, lambda p: halo[p], weights, acc, mix, ext, hidden, present, result,
        lambda part: copy_of(part).start(),
    )
    first.wait()
    for n in range(2):
        copy_of(slice(n * cols // 2, (n + 1) * cols // 2)).wait()


def shards(fields, lon_taps, lat_taps, cycle_taps, band_start, band_width, mixing):
    rows, cols, chans = fields.shape
    row_total, basis, taps = lon_taps.shape
    band = lat_taps.shape[2]
    reach = (taps - 1) // 2
    polar = cycle_taps.shape[1] // 2
    cycle = cycle_taps.shape[2]
    lat_count = lax.axis_size("lat")
    core = lax.axis_index("lon")
    axes = ("lat", "lon")
    assert cycle == 2 * cols and rows == 2 * HALO and basis * polar * BLOCK == rows * SPAN
    assert reach == (SPAN - BLOCK) // 4 and polar == HALO
    ahead, back = ring(lat_count, 1), ring(lat_count, -1)
    head, tail = fields[:HALO], fields[rows - HALO :]
    going = jnp.where(core == 0, head, tail)
    staying = jnp.where(core == 0, tail, head)
    second = lax.ppermute(going, axes, back)
    going, staying, band_start = lax.optimization_barrier((going, staying, band_start))

    vmem = pl.BlockSpec(memory_space=pltpu.VMEM)
    hbm = pl.BlockSpec(memory_space=pltpu.HBM)
    sds = jax.ShapeDtypeStruct
    group = basis * rows * BLOCK
    ext_cols = cols + SPAN - BLOCK
    limit = pltpu.CompilerParams(vmem_limit_bytes=32 * 1024 * 1024)
    small = pl.CostEstimate(flops=100_000, bytes_accessed=1_000, transcendentals=0)
    large = pl.CostEstimate(flops=1_600_000_000, bytes_accessed=1_000, transcendentals=0)
    weight_shapes = (
        sds((2, group // 2, HALO * SPAN), BF16),
        sds((group, rows * SPAN), BF16),
        sds((rows * BLOCK, rows * SPAN), BF16),
        sds((basis, 2 * polar, cycle), BF16),
        sds((basis * chans, chans), BF16),
        sds((polar, basis * cols, cycle), BF16),
    )

    def weights(made):
        operands = [
            pltpu.with_memory_space_constraint(x, pltpu.HBM)
            for x in (
                band_start, band_width, jnp.transpose(lon_taps, (2, 1, 0)),
                jnp.transpose(lat_taps, (2, 1, 0)), cycle_taps,
                mixing.reshape(basis * chans, chans),
            )
        ]
        return pl.pallas_call(
            functools.partial(weight_kernel, bool(made)),
            out_shape=weight_shapes,
            in_specs=[hbm] * 6 + [vmem] * len(made),
            out_specs=[vmem] * 6,
            input_output_aliases={6 + n: n for n in range(len(made))},
            scratch_shapes=[
                pltpu.SMEM((rows,), jnp.int32),
                pltpu.SMEM((rows,), jnp.int32),
                pltpu.VMEM((taps, basis, row_total), F32),
                pltpu.VMEM((band, basis, rows), BF16),
                pltpu.VMEM((128, -(-row_total // 128) * 128), F32),
                pltpu.VMEM((128, 128), F32),
                pltpu.SemaphoreType.DMA((6,)),
            ],
            compiler_params=limit,
            cost_estimate=small,
            name="filter_weights" if made else "first_weights",
        )(*operands, *made)

    made = weights(())
    going, made = lax.optimization_barrier((going, made))
    whole, edges, polar_left, polar_right = pl.pallas_call(
        stage_kernel,
        out_shape=(
            sds((rows, cols, chans), BF16),
            sds((rows, 2 * reach, chans), BF16),
            sds((polar, cols // 2, chans), BF16),
            sds((polar, cols // 2, chans), BF16),
        ),
        in_specs=[vmem] * 2,
        out_specs=[vmem] * 4,
        compiler_params=limit,
        cost_estimate=small,
        name="stage_rows",
    )(going, staying)
    edges = lax.ppermute(edges, "lon", SWAP)
    polar_left = lax.ppermute(polar_left, "lon", SWAP)
    polar_right = lax.ppermute(polar_right, "lon", SWAP)
    message, corners = pl.pallas_call(
        pack_kernel,
        out_shape=(
            sds((HALO, cols + 2 * reach, chans), BF16),
            sds((HALO, 2 * reach, chans), BF16),
        ),
        in_specs=[vmem] * 2,
        out_specs=(vmem, vmem),
        compiler_params=limit,
        cost_estimate=small,
        name="pack_messages",
    )(whole, edges)
    first = lax.ppermute(message, axes, ahead)
    second_edges = lax.ppermute(corners, axes, back)
    corners, made = lax.optimization_barrier((corners, made))
    halo_weights, own_weights, polar_weights, turns, mix, turned = weights(made)
    acc, turned = pl.pallas_call(
        own_kernel,
        out_shape=(
            sds((rows, cols, chans), F32),
            sds((polar, basis * cols, cycle), BF16),
        ),
        in_specs=[vmem] * 5,
        out_specs=(vmem, vmem),
        input_output_aliases={0: 1},
        scratch_shapes=[
            pltpu.VMEM((rows, ext_cols, chans), BF16),
            pltpu.VMEM((rows * (cols - 2 * BLOCK), basis * chans), BF16),
        ],
        compiler_params=limit,
        cost_estimate=pl.CostEstimate(
            flops=100_000, bytes_accessed=1_000, transcendentals=0
        ),
        name="own_rows",
    )(turned, own_weights, turns, whole, mix)

    acc = pl.pallas_call(
        partner_kernel,
        out_shape=sds((rows, cols, chans), F32),
        in_specs=[vmem] * 9,
        out_specs=vmem,
        input_output_aliases={0: 0},
        scratch_shapes=[
            pltpu.VMEM((rows * 2 * BLOCK, basis * chans), BF16),
            pltpu.VMEM((basis, polar * cols, chans), BF16),
            pltpu.VMEM((basis * polar, cols, chans), BF16),
        ],
        compiler_params=limit,
        cost_estimate=pl.CostEstimate(
            flops=100_000, bytes_accessed=1_000, transcendentals=0
        ),
        name="partner_columns",
    )(acc, own_weights, polar_weights, turned, whole, mix, edges, polar_left, polar_right)

    half = rows // 2
    scratch = [
        pltpu.VMEM((HALO, ext_cols, chans), BF16),
        pltpu.VMEM((2, half * cols // 2, basis * chans), BF16),
    ]
    limit = pltpu.CompilerParams(vmem_limit_bytes=32 * 1024 * 1024)
    second, second_edges, acc = lax.optimization_barrier((second, second_edges, acc))
    early = pl.pallas_call(
        early_kernel,
        out_shape=sds((half, cols, chans), BF16),
        in_specs=[vmem] * 5,
        out_specs=vmem,
        scratch_shapes=scratch,
        compiler_params=limit,
        cost_estimate=large,
        name="early_side",
    )(second, second_edges, halo_weights, acc, mix)
    first, early = lax.optimization_barrier((first, early))
    return pl.pallas_call(
        late_kernel,
        out_shape=sds((rows, cols, chans), BF16),
        in_specs=[vmem] * 5,
        out_specs=hbm,
        scratch_shapes=[
            *scratch,
            pltpu.VMEM((half, cols, chans), BF16),
            pltpu.SemaphoreType.DMA((3,)),
        ],
        compiler_params=limit,
        name="late_side",
    )(early, first, halo_weights, acc, mix)


def solution(mesh):
    in_specs = (
        P(("ens", "lat"), "lon", None),
        P(),
        P("lat", None, None),
        P(),
        P("lat"),
        P("lat"),
        P(),
    )
    out_specs = P(("ens", "lat"), "lon", None)
    return jax.shard_map(shards, mesh=mesh, in_specs=in_specs, out_specs=out_specs, check_vma=False)
```

```python
import functools

import jax
import jax.numpy as jnp
from jax import lax
from jax.experimental import pallas as pl
from jax.experimental.pallas import tpu as pltpu
from jax.sharding import PartitionSpec as P

HALO = 4
BLOCK = 16
SPAN = 32
SWAP = [(0, 1), (1, 0)]
F32, BF16 = jnp.float32, jnp.bfloat16


def ring(lat_count, step):
    pairs = []
    for lat in range(lat_count):
        for core in range(2):
            to = lat + (step if core == 0 else -step)
            if 0 <= to < lat_count:
                pairs.append((lat * 2 + core, to * 2 + core))
            else:
                pairs.append((lat * 2 + core, lat * 2 + 1 - core))
    return pairs


def matmul(a, b):
    return jnp.dot(a, b, preferred_element_type=F32)


def staircase(line, steps):
    wide = jnp.broadcast_to(line, (steps, line.shape[1]))
    return pltpu.roll(wide, 0, 1, stride=1, stride_axis=0).astype(BF16)


def chosen(terms):
    total = None
    for mask, value in terms:
        term = jnp.where(mask, value, 0.0)
        total = term if total is None else total + term
    return total


def window_products(weights, cells, hidden, groups, width, offset, chans):
    part = matmul(weights[...], cells.reshape(-1, chans)).astype(BF16)
    for n, (i, k) in enumerate(groups):
        at = i * width + offset
        hidden[at : at + BLOCK, k * chans : (k + 1) * chans] = part[n * BLOCK : (n + 1) * BLOCK]


def polar_matrices(cycle_taps, turned, at_top):
    basis, twice, cycle = cycle_taps.shape
    polar = twice // 2
    cols = turned.shape[1] // basis
    total = lax.broadcasted_iota(jnp.int32, (cycle, cycle), 0) + lax.broadcasted_iota(
        jnp.int32, (cycle, cycle), 1
    )
    turn = jnp.where((total == 0) | (total == cycle), 1.0, 0.0).astype(BF16)
    negated = matmul(cycle_taps[...].reshape(-1, cycle), turn)
    for p in range(polar):
        for k in range(basis):
            n = k * twice + (p if at_top else p + polar)
            turned[p, k * cols : (k + 1) * cols, :] = staircase(negated[n : n + 1], cols)


def weight_kernel(
    late, start_in, width_in, lon_in, lat_in, cycle_in, mixing_in, *refs,
):
    if late:
        refs = refs[6:]
    halo_weights, own_weights, polar_weights, cycle_taps, mix, turned = refs[:6]
    start, width, lon, lat, lon_wide, lat_wide, sems = refs[6:]
    rows = halo_weights.shape[0] * HALO
    taps, basis, row_total = lon.shape
    band = lat.shape[0]
    polar = cycle_taps.shape[1] // 2
    lat_pos = lax.axis_index("lat")
    base = lat_pos * rows
    at_top = base == 0

    is_early = at_top & (lax.axis_index("lon") == 0) & (lax.axis_index("ens") == 0)

    @pl.when(jnp.logical_not(is_early) if late else is_early)
    def make():
        copies = []
        for n, (source, target) in enumerate(
            [
                (lon_in, lon), (lat_in, lat), (start_in, start), (width_in, width),
                (cycle_in, cycle_taps), (mixing_in, mix),
            ]
        ):
            copies.append(pltpu.make_async_copy(source, target, sems.at[n]))
            copies[-1].start()
        lon_wide[...] = jnp.zeros_like(lon_wide)
        lat_wide[...] = jnp.zeros_like(lat_wide)
        for n in range(4):
            copies[n].wait()

        for d in range(taps):
            for k in range(basis):
                lon_wide[k * 16 + d : k * 16 + d + 1, 0:row_total] = lon[d, k : k + 1, :]
        lanes = lon_wide.shape[1]
        slots = pltpu.roll(lon_wide[...], lax.rem(lanes + HALO - base, lanes), 1)[:, :128]
        slots = jnp.transpose(slots)[: rows + 2 * HALO]
        is_tap = lax.broadcasted_iota(jnp.int32, slots.shape, 1) < taps
        own_taps, halo_taps = [], []
        for k in range(basis):
            moved = slots if k == 0 else pltpu.roll(slots, 128 - 16 * k, 1)
            moved = jnp.where(is_tap, moved, 0.0)
            for _ in range(2):
                moved = pltpu.roll(moved, 0, 1, stride=SPAN // 2, stride_axis=0)
            quads = [jnp.sum(moved[4 * q : 4 * q + 4], axis=0, keepdims=True) for q in range(4)]
            own_taps.append(jnp.concatenate([quads[1], quads[2]], axis=1))
            halo_taps.append(jnp.concatenate([quads[0], quads[3]], axis=1))

        for t in range(band):
            lat_wide[t * basis : (t + 1) * basis, 0:rows] = lat[t].astype(F32)
        lat_cols = jnp.transpose(lat_wide[...])[:rows]
        shape = (rows, rows * SPAN)
        lane = lax.broadcasted_iota(jnp.int32, shape, 1)
        out_row = lax.broadcasted_iota(jnp.int32, shape, 0)
        first = jnp.zeros(shape, jnp.int32)
        count = jnp.zeros(shape, jnp.int32)
        for i in range(rows):
            first = jnp.where(out_row == i, start[i], first)
            count = jnp.where(out_row == i, width[i], count)
        spread = [
            [
                jnp.broadcast_to(lat_cols[:, t * basis + k : t * basis + k + 1], shape)
                for k in range(basis)
            ]
            for t in range(band)
        ]
        slot = lane // SPAN
        own_row = base + slot
        halo_row = jnp.where(slot < HALO, own_row - HALO, own_row + rows - HALO)
        is_polar = (own_row < polar) | (own_row >= row_total - polar)
        in_grid = (halo_row >= 0) & (halo_row < row_total)
        own_step, halo_step = own_row - first, halo_row - first
        own_used = [(own_step == t) & (count > t) & ~is_polar for t in range(band)]
        halo_used = [(halo_step == t) & (count > t) & in_grid for t in range(band)]
        for k in range(basis):
            own_line = own_taps[k] * chosen([(own_used[t], spread[t][k]) for t in range(band)])
            halo_line = halo_taps[k] * chosen([(halo_used[t], spread[t][k]) for t in range(band)])
            for i in range(rows):
                at = (k * rows + i) * BLOCK
                own_weights[at : at + BLOCK, :] = staircase(own_line[i : i + 1], BLOCK)
                side, at = i // HALO, (k * HALO + i % HALO) * BLOCK
                reached = halo_line[i : i + 1, side * HALO * SPAN : (side + 1) * HALO * SPAN]
                halo_weights[side, at : at + BLOCK, :] = staircase(reached, BLOCK)

        offset = jnp.where(at_top, 0, rows - polar)
        of_basis = lane // (polar * BLOCK)
        step = base + offset + lax.rem(lane // BLOCK, polar) - first
        at_start = lax.rem(lane, BLOCK) == 0
        terms = []
        for t in range(band):
            value = spread[t][0]
            for k in range(1, basis):
                value = jnp.where(of_basis == k, spread[t][k], value)
            terms.append(((step == t) & (count > t) & at_start, value))
        line = chosen(terms)
        for i in range(rows):
            polar_weights[i * BLOCK : (i + 1) * BLOCK, :] = staircase(line[i : i + 1], BLOCK)
        copies[4].wait()

        copies[5].wait()


def stage_kernel(
    start_in, width_in, lon_in, lat_in, cycle_in, mixing_in, going, staying,
    whole, edges, polar_left, polar_right, *refs,
):
    weight_kernel(False, start_in, width_in, lon_in, lat_in, cycle_in, mixing_in, *refs)
    cols = whole.shape[1]
    reach = edges.shape[1] // 2
    is_first = lax.axis_index("lon") == 0
    at_top = lax.axis_index("lat") == 0
    for p in range(HALO):
        upper = jnp.where(is_first, going[p], staying[p])
        lower = jnp.where(is_first, staying[p], going[p])
        polar = jnp.where(at_top, upper, lower)
        polar_left[p], polar_right[p] = polar[: cols // 2], polar[cols // 2 :]
        for r, row in ((p, upper), (HALO + p, lower)):
            whole[r] = row
            edges[r] = jnp.concatenate([row[:reach], row[cols - reach :]], axis=0)


def pack_kernel(whole, edges, message, corners):
    rows = whole.shape[0]
    reach = edges.shape[1] // 2
    start = jnp.where(lax.axis_index("lon") == 0, rows - HALO, 0)
    early = rows - HALO - start
    for p in range(HALO):
        near = edges[start + p]
        message[p] = jnp.concatenate([near[reach:], whole[start + p], near[:reach]], axis=0)
        corners[p] = edges[early + p]


def own_kernel(turned_in, own_weights, cycle_taps, fields, mix, acc, turned, ext, hidden):
    del turned_in
    rows, cols, chans = fields.shape
    basis = mix.shape[0] // chans
    near = (SPAN - BLOCK) // 4

    lat_pos = lax.axis_index("lat")

    @pl.when(lat_pos == 0)
    def top():
        polar_matrices(cycle_taps, turned, True)

    @pl.when(lat_pos == lax.axis_size("lat") - 1)
    def bottom():
        polar_matrices(cycle_taps, turned, False)

    blank = jnp.zeros((near, chans), BF16)
    pad = jnp.zeros((ext.shape[1] - cols - near, chans), BF16)
    for r in range(rows):
        ext[r] = jnp.concatenate([blank, fields[r], pad], axis=0)
    groups = [(i, k) for k in range(basis) for i in range(rows)]
    inner = cols - 2 * BLOCK
    for at in range(BLOCK, cols - BLOCK, BLOCK):
        window_products(
            own_weights, ext[:, at : at + SPAN, :], hidden, groups, inner, at - BLOCK, chans
        )
    half = rows // 2
    for n in range(2):
        at = slice(n * half, (n + 1) * half)
        total = matmul(hidden[n * half * inner : (n + 1) * half * inner], mix[...])
        acc[at, BLOCK : cols - BLOCK, :] = total.reshape(half, inner, chans) + fields[
            at, BLOCK : cols - BLOCK, :
        ].astype(F32)


def partner_kernel(
    acc_in, own_weights, polar_weights, turned, fields, mix, edges, polar_left, polar_right,
    acc, hidden, cycle_rows, mixed_rows,
):
    del acc_in
    rows, cols, chans = fields.shape
    polar = turned.shape[0]
    basis = mix.shape[0] // chans
    reach = (SPAN - BLOCK) // 4
    lat_pos = lax.axis_index("lat")
    at_top = lat_pos == 0
    at_bottom = lat_pos == lax.axis_size("lat") - 1
    groups = [(i, k) for k in range(basis) for i in range(rows)]
    left, right = [], []
    pad = jnp.zeros((SPAN - BLOCK - 2 * reach, chans), BF16)
    for r in range(rows):
        left.append(
            jnp.concatenate([edges[r, reach:], fields[r, : SPAN - reach]], axis=0)
        )
        right.append(
            jnp.concatenate(
                [fields[r, cols - BLOCK - reach :], edges[r, :reach], pad], axis=0
            )
        )
    for n, cells in enumerate((left, right)):
        window_products(
            own_weights, jnp.concatenate(cells, axis=0), hidden, groups, 2 * BLOCK, n * BLOCK,
            chans,
        )
    total = matmul(hidden[...], mix[...]).reshape(rows, 2 * BLOCK, chans)
    for n, at in enumerate((slice(0, BLOCK), slice(cols - BLOCK, cols))):
        acc[:, at, :] = total[:, n * BLOCK : (n + 1) * BLOCK] + fields[:, at, :].astype(F32)

    @pl.when(at_top | at_bottom)
    def polar_part():
        offset = jnp.where(at_top, 0, rows - polar)
        for p in range(polar):
            whole = jnp.concatenate(
                [fields[offset + p], polar_left[p], polar_right[p]], axis=0
            )
            part = matmul(turned[p], whole).astype(BF16)
            for k in range(basis):
                cycle_rows[k, p * cols : (p + 1) * cols, :] = part[k * cols : (k + 1) * cols]
        for k in range(basis):
            part = matmul(cycle_rows[k], mix[k * chans : (k + 1) * chans, :]).astype(BF16)
            mixed_rows[k * polar : (k + 1) * polar] = part.reshape(polar, cols, chans)
        for b in range(cols // BLOCK):
            at = slice(BLOCK * b, BLOCK * (b + 1))
            cells = mixed_rows[:, at, :].reshape(-1, chans)
            acc[:, at, :] = acc[:, at, :] + matmul(polar_weights[...], cells).reshape(
                rows, BLOCK, chans
            )


def side_rows(
    side, halo, weights, acc, mix, ext, hidden, present, result, ready=lambda at: None
):
    half, cols, chans = result.shape
    basis = mix.shape[0] // chans
    rows = pl.ds(side * half, half)
    wide = cols // 2
    parts = [slice(n * wide, (n + 1) * wide) for n in range(2)]

    @pl.when(present)
    def arrived():
        for p in range(HALO):
            cells = halo(p)
            pad = jnp.zeros((ext.shape[1] - cells.shape[0], chans), BF16)
            ext[p] = jnp.concatenate([cells, pad], axis=0)
        groups = [(i, k) for k in range(basis) for i in range(half)]
        for n, part in enumerate(parts):
            for at in range(0, wide, BLOCK):
                cells = ext[:, part.start + at : part.start + at + SPAN, :]
                window_products(
                    weights.at[side], cells, hidden.at[n], groups, wide, at, chans
                )
        for n, part in enumerate(parts):
            total = matmul(hidden[n], mix[...]).reshape(half, wide, chans)
            result[:, part, :] = (total + acc[rows, part, :]).astype(BF16)
            ready(part)

    @pl.when(jnp.logical_not(present))
    def absent():
        for part in parts:
            result[:, part, :] = acc[rows, part, :].astype(BF16)
            ready(part)


def from_side(which):
    core = lax.axis_index("lon")
    side = 1 - core if which == 0 else core
    lat_pos = lax.axis_index("lat")
    last = lax.axis_size("lat") - 1
    present = jnp.where(side == 0, lat_pos != 0, lat_pos != last)
    return side, present


def early_kernel(halo, edges, weights, acc, mix, result, ext, hidden):
    side, present = from_side(0)
    reach = edges.shape[1] // 2

    def cells(p):
        edge = edges[p]
        return jnp.concatenate([edge[reach:], halo[p], edge[:reach]], axis=0)

    side_rows(side, cells, weights, acc, mix, ext, hidden, present, result)


def late_kernel(early, halo, weights, acc, mix, out, ext, hidden, result, sems):
    half, cols, _ = result.shape
    side, present = from_side(1)
    rows = pl.ds(side * half, half)
    other_rows = pl.ds((1 - side) * half, half)

    def copy_of(part):
        n = 0 if part.start == 0 else 1
        return pltpu.make_async_copy(
            result.at[:, part, :], out.at[rows, part, :], sems.at[n]
        )

    first = pltpu.make_async_copy(early, out.at[other_rows], sems.at[2])
    first.start()
    side_rows(
        side, lambda p: halo[p], weights, acc, mix, ext, hidden, present, result,
        lambda part: copy_of(part).start(),
    )
    first.wait()
    for n in range(2):
        copy_of(slice(n * cols // 2, (n + 1) * cols // 2)).wait()


def shards(fields, lon_taps, lat_taps, cycle_taps, band_start, band_width, mixing):
    rows, cols, chans = fields.shape
    row_total, basis, taps = lon_taps.shape
    band = lat_taps.shape[2]
    reach = (taps - 1) // 2
    polar = cycle_taps.shape[1] // 2
    cycle = cycle_taps.shape[2]
    lat_count = lax.axis_size("lat")
    core = lax.axis_index("lon")
    axes = ("lat", "lon")
    assert cycle == 2 * cols and rows == 2 * HALO and basis * polar * BLOCK == rows * SPAN
    assert reach == (SPAN - BLOCK) // 4 and polar == HALO
    ahead, back = ring(lat_count, 1), ring(lat_count, -1)
    head, tail = fields[:HALO], fields[rows - HALO :]
    going = jnp.where(core == 0, head, tail)
    staying = jnp.where(core == 0, tail, head)
    second = lax.ppermute(going, axes, back)
    going, staying, band_start = lax.optimization_barrier((going, staying, band_start))

    vmem = pl.BlockSpec(memory_space=pltpu.VMEM)
    hbm = pl.BlockSpec(memory_space=pltpu.HBM)
    sds = jax.ShapeDtypeStruct
    group = basis * rows * BLOCK
    ext_cols = cols + SPAN - BLOCK
    limit = pltpu.CompilerParams(vmem_limit_bytes=32 * 1024 * 1024)
    small = pl.CostEstimate(flops=100_000, bytes_accessed=1_000, transcendentals=0)
    large = pl.CostEstimate(flops=1_600_000_000, bytes_accessed=1_000, transcendentals=0)
    weight_shapes = (
        sds((2, group // 2, HALO * SPAN), BF16),
        sds((group, rows * SPAN), BF16),
        sds((rows * BLOCK, rows * SPAN), BF16),
        sds((basis, 2 * polar, cycle), BF16),
        sds((basis * chans, chans), BF16),
        sds((polar, basis * cols, cycle), BF16),
    )

    operands = [
        pltpu.with_memory_space_constraint(x, pltpu.HBM)
        for x in (
            band_start, band_width, jnp.transpose(lon_taps, (2, 1, 0)),
            jnp.transpose(lat_taps, (2, 1, 0)), cycle_taps,
            mixing.reshape(basis * chans, chans),
        )
    ]
    weight_scratch = [
        pltpu.SMEM((rows,), jnp.int32),
        pltpu.SMEM((rows,), jnp.int32),
        pltpu.VMEM((taps, basis, row_total), F32),
        pltpu.VMEM((band, basis, rows), BF16),
        pltpu.VMEM((128, -(-row_total // 128) * 128), F32),
        pltpu.VMEM((128, 128), F32),
        pltpu.SemaphoreType.DMA((6,)),
    ]
    whole, edges, polar_left, polar_right, *made = pl.pallas_call(
        stage_kernel,
        out_shape=(
            sds((rows, cols, chans), BF16),
            sds((rows, 2 * reach, chans), BF16),
            sds((polar, cols // 2, chans), BF16),
            sds((polar, cols // 2, chans), BF16),
            *weight_shapes,
        ),
        in_specs=[hbm] * 6 + [vmem] * 2,
        out_specs=[vmem] * 10,
        scratch_shapes=weight_scratch,
        compiler_params=limit,
        cost_estimate=small,
        name="stage_rows",
    )(*operands, going, staying)
    edges = lax.ppermute(edges, "lon", SWAP)
    polar_left = lax.ppermute(polar_left, "lon", SWAP)
    polar_right = lax.ppermute(polar_right, "lon", SWAP)
    message, corners = pl.pallas_call(
        pack_kernel,
        out_shape=(
            sds((HALO, cols + 2 * reach, chans), BF16),
            sds((HALO, 2 * reach, chans), BF16),
        ),
        in_specs=[vmem] * 2,
        out_specs=(vmem, vmem),
        compiler_params=limit,
        cost_estimate=small,
        name="pack_messages",
    )(whole, edges)
    first = lax.ppermute(message, axes, ahead)
    second_edges = lax.ppermute(corners, axes, back)
    corners, made = lax.optimization_barrier((corners, made))
    halo_weights, own_weights, polar_weights, turns, mix, turned = pl.pallas_call(
        functools.partial(weight_kernel, True),
        out_shape=weight_shapes,
        in_specs=[hbm] * 6 + [vmem] * 6,
        out_specs=[vmem] * 6,
        input_output_aliases={6 + n: n for n in range(6)},
        scratch_shapes=weight_scratch,
        compiler_params=limit,
        cost_estimate=small,
        name="filter_weights",
    )(*operands, *made)
    acc, turned = pl.pallas_call(
        own_kernel,
        out_shape=(
            sds((rows, cols, chans), F32),
            sds((polar, basis * cols, cycle), BF16),
        ),
        in_specs=[vmem] * 5,
        out_specs=(vmem, vmem),
        input_output_aliases={0: 1},
        scratch_shapes=[
            pltpu.VMEM((rows, ext_cols, chans), BF16),
            pltpu.VMEM((rows * (cols - 2 * BLOCK), basis * chans), BF16),
        ],
        compiler_params=limit,
        cost_estimate=pl.CostEstimate(
            flops=100_000, bytes_accessed=1_000, transcendentals=0
        ),
        name="own_rows",
    )(turned, own_weights, turns, whole, mix)

    acc = pl.pallas_call(
        partner_kernel,
        out_shape=sds((rows, cols, chans), F32),
        in_specs=[vmem] * 9,
        out_specs=vmem,
        input_output_aliases={0: 0},
        scratch_shapes=[
            pltpu.VMEM((rows * 2 * BLOCK, basis * chans), BF16),
            pltpu.VMEM((basis, polar * cols, chans), BF16),
            pltpu.VMEM((basis * polar, cols, chans), BF16),
        ],
        compiler_params=limit,
        cost_estimate=pl.CostEstimate(
            flops=100_000, bytes_accessed=1_000, transcendentals=0
        ),
        name="partner_columns",
    )(acc, own_weights, polar_weights, turned, whole, mix, edges, polar_left, polar_right)

    half = rows // 2
    scratch = [
        pltpu.VMEM((HALO, ext_cols, chans), BF16),
        pltpu.VMEM((2, half * cols // 2, basis * chans), BF16),
    ]
    limit = pltpu.CompilerParams(vmem_limit_bytes=32 * 1024 * 1024)
    second, second_edges, acc = lax.optimization_barrier((second, second_edges, acc))
    early = pl.pallas_call(
        early_kernel,
        out_shape=sds((half, cols, chans), BF16),
        in_specs=[vmem] * 5,
        out_specs=vmem,
        scratch_shapes=scratch,
        compiler_params=limit,
        cost_estimate=large,
        name="early_side",
    )(second, second_edges, halo_weights, acc, mix)
    first, early = lax.optimization_barrier((first, early))
    return pl.pallas_call(
        late_kernel,
        out_shape=sds((rows, cols, chans), BF16),
        in_specs=[vmem] * 5,
        out_specs=hbm,
        scratch_shapes=[
            *scratch,
            pltpu.VMEM((half, cols, chans), BF16),
            pltpu.SemaphoreType.DMA((3,)),
        ],
        compiler_params=limit,
        name="late_side",
    )(early, first, halo_weights, acc, mix)


def solution(mesh):
    in_specs = (
        P(("ens", "lat"), "lon", None),
        P(),
        P("lat", None, None),
        P(),
        P("lat"),
        P("lat"),
        P(),
    )
    out_specs = P(("ens", "lat"), "lon", None)
    return jax.shard_map(shards, mesh=mesh, in_specs=in_specs, out_specs=out_specs, check_vma=False)
```

```python
import functools

import jax
import jax.numpy as jnp
from jax import lax
from jax.experimental import pallas as pl
from jax.experimental.pallas import tpu as pltpu
from jax.sharding import PartitionSpec as P

HALO = 4
BLOCK = 16
SPAN = 32
SWAP = [(0, 1), (1, 0)]
F32, BF16 = jnp.float32, jnp.bfloat16


def ring(lat_count, step):
    pairs = []
    for lat in range(lat_count):
        for core in range(2):
            to = lat + (step if core == 0 else -step)
            if 0 <= to < lat_count:
                pairs.append((lat * 2 + core, to * 2 + core))
            else:
                pairs.append((lat * 2 + core, lat * 2 + 1 - core))
    return pairs


def matmul(a, b):
    return jnp.dot(a, b, preferred_element_type=F32)


def staircase(line, steps):
    wide = jnp.broadcast_to(line, (steps, line.shape[1]))
    return pltpu.roll(wide, 0, 1, stride=1, stride_axis=0).astype(BF16)


def chosen(terms):
    total = None
    for mask, value in terms:
        term = jnp.where(mask, value, 0.0)
        total = term if total is None else total + term
    return total


def window_products(weights, cells, hidden, groups, width, offset, chans):
    part = matmul(weights[...], cells.reshape(-1, chans)).astype(BF16)
    for n, (i, k) in enumerate(groups):
        at = i * width + offset
        hidden[at : at + BLOCK, k * chans : (k + 1) * chans] = part[n * BLOCK : (n + 1) * BLOCK]


def polar_matrices(cycle_taps, turned, at_top):
    basis, twice, cycle = cycle_taps.shape
    polar = twice // 2
    cols = turned.shape[1] // basis
    total = lax.broadcasted_iota(jnp.int32, (cycle, cycle), 0) + lax.broadcasted_iota(
        jnp.int32, (cycle, cycle), 1
    )
    turn = jnp.where((total == 0) | (total == cycle), 1.0, 0.0).astype(BF16)
    negated = matmul(cycle_taps[...].reshape(-1, cycle), turn)
    for p in range(polar):
        for k in range(basis):
            n = k * twice + (p if at_top else p + polar)
            turned[p, k * cols : (k + 1) * cols, :] = staircase(negated[n : n + 1], cols)


def weight_kernel(
    late, start_in, width_in, lon_in, lat_in, cycle_in, mixing_in, *refs,
):
    if late:
        refs = refs[6:]
    halo_weights, own_weights, polar_weights, cycle_taps, mix, turned = refs[:6]
    start, width, lon, lat, lon_wide, lat_wide, sems = refs[6:]
    rows = halo_weights.shape[0] * HALO
    taps, basis, row_total = lon.shape
    band = lat.shape[0]
    polar = cycle_taps.shape[1] // 2
    lat_pos = lax.axis_index("lat")
    base = lat_pos * rows
    at_top = base == 0

    is_early = at_top & (lax.axis_index("lon") == 0) & (lax.axis_index("ens") == 0)

    @pl.when(jnp.logical_not(is_early) if late else is_early)
    def make():
        copies = []
        for n, (source, target) in enumerate(
            [
                (lon_in, lon), (lat_in, lat), (start_in, start), (width_in, width),
                (cycle_in, cycle_taps), (mixing_in, mix),
            ]
        ):
            copies.append(pltpu.make_async_copy(source, target, sems.at[n]))
            copies[-1].start()
        lon_wide[...] = jnp.zeros_like(lon_wide)
        lat_wide[...] = jnp.zeros_like(lat_wide)
        for n in range(4):
            copies[n].wait()

        for d in range(taps):
            for k in range(basis):
                lon_wide[k * 16 + d : k * 16 + d + 1, 0:row_total] = lon[d, k : k + 1, :]
        lanes = lon_wide.shape[1]
        slots = pltpu.roll(lon_wide[...], lax.rem(lanes + HALO - base, lanes), 1)[:, :128]
        slots = jnp.transpose(slots)[: rows + 2 * HALO]
        is_tap = lax.broadcasted_iota(jnp.int32, slots.shape, 1) < taps
        own_taps, halo_taps = [], []
        for k in range(basis):
            moved = slots if k == 0 else pltpu.roll(slots, 128 - 16 * k, 1)
            moved = jnp.where(is_tap, moved, 0.0)
            for _ in range(2):
                moved = pltpu.roll(moved, 0, 1, stride=SPAN // 2, stride_axis=0)
            quads = [jnp.sum(moved[4 * q : 4 * q + 4], axis=0, keepdims=True) for q in range(4)]
            own_taps.append(jnp.concatenate([quads[1], quads[2]], axis=1))
            halo_taps.append(jnp.concatenate([quads[0], quads[3]], axis=1))

        for t in range(band):
            lat_wide[t * basis : (t + 1) * basis, 0:rows] = lat[t].astype(F32)
        lat_cols = jnp.transpose(lat_wide[...])[:rows]
        shape = (rows, rows * SPAN)
        lane = lax.broadcasted_iota(jnp.int32, shape, 1)
        out_row = lax.broadcasted_iota(jnp.int32, shape, 0)
        first = jnp.zeros(shape, jnp.int32)
        count = jnp.zeros(shape, jnp.int32)
        for i in range(rows):
            first = jnp.where(out_row == i, start[i], first)
            count = jnp.where(out_row == i, width[i], count)
        spread = [
            [
                jnp.broadcast_to(lat_cols[:, t * basis + k : t * basis + k + 1], shape)
                for k in range(basis)
            ]
            for t in range(band)
        ]
        slot = lane // SPAN
        own_row = base + slot
        halo_row = jnp.where(slot < HALO, own_row - HALO, own_row + rows - HALO)
        is_polar = (own_row < polar) | (own_row >= row_total - polar)
        in_grid = (halo_row >= 0) & (halo_row < row_total)
        own_step, halo_step = own_row - first, halo_row - first
        own_used = [(own_step == t) & (count > t) & ~is_polar for t in range(band)]
        halo_used = [(halo_step == t) & (count > t) & in_grid for t in range(band)]
        for k in range(basis):
            own_line = own_taps[k] * chosen([(own_used[t], spread[t][k]) for t in range(band)])
            halo_line = halo_taps[k] * chosen([(halo_used[t], spread[t][k]) for t in range(band)])
            for i in range(rows):
                at = (k * rows + i) * BLOCK
                own_weights[at : at + BLOCK, :] = staircase(own_line[i : i + 1], BLOCK)
                side, at = i // HALO, (k * HALO + i % HALO) * BLOCK
                reached = halo_line[i : i + 1, side * HALO * SPAN : (side + 1) * HALO * SPAN]
                halo_weights[side, at : at + BLOCK, :] = staircase(reached, BLOCK)

        offset = jnp.where(at_top, 0, rows - polar)
        of_basis = lane // (polar * BLOCK)
        step = base + offset + lax.rem(lane // BLOCK, polar) - first
        at_start = lax.rem(lane, BLOCK) == 0
        terms = []
        for t in range(band):
            value = spread[t][0]
            for k in range(1, basis):
                value = jnp.where(of_basis == k, spread[t][k], value)
            terms.append(((step == t) & (count > t) & at_start, value))
        line = chosen(terms)
        for i in range(rows):
            polar_weights[i * BLOCK : (i + 1) * BLOCK, :] = staircase(line[i : i + 1], BLOCK)
        copies[4].wait()

        copies[5].wait()


def stage_kernel(
    start_in, width_in, lon_in, lat_in, cycle_in, mixing_in, going, staying,
    whole, edges, polar_left, polar_right, *refs,
):
    weight_kernel(False, start_in, width_in, lon_in, lat_in, cycle_in, mixing_in, *refs)
    cols = whole.shape[1]
    reach = edges.shape[1] // 2
    is_first = lax.axis_index("lon") == 0
    at_top = lax.axis_index("lat") == 0
    for p in range(HALO):
        upper = jnp.where(is_first, going[p], staying[p])
        lower = jnp.where(is_first, staying[p], going[p])
        polar = jnp.where(at_top, upper, lower)
        polar_left[p], polar_right[p] = polar[: cols // 2], polar[cols // 2 :]
        for r, row in ((p, upper), (HALO + p, lower)):
            whole[r] = row
            edges[r] = jnp.concatenate([row[:reach], row[cols - reach :]], axis=0)


def pack_kernel(whole, edges, message, corners):
    rows = whole.shape[0]
    reach = edges.shape[1] // 2
    start = jnp.where(lax.axis_index("lon") == 0, rows - HALO, 0)
    early = rows - HALO - start
    for p in range(HALO):
        near = edges[start + p]
        message[p] = jnp.concatenate([near[reach:], whole[start + p], near[:reach]], axis=0)
        corners[p] = edges[early + p]


def own_kernel(turned_in, own_weights, cycle_taps, fields, mix, acc, turned, ext, hidden):
    del turned_in
    rows, cols, chans = fields.shape
    basis = mix.shape[0] // chans
    near = (SPAN - BLOCK) // 4

    lat_pos = lax.axis_index("lat")

    @pl.when(lat_pos == 0)
    def top():
        polar_matrices(cycle_taps, turned, True)

    @pl.when(lat_pos == lax.axis_size("lat") - 1)
    def bottom():
        polar_matrices(cycle_taps, turned, False)

    blank = jnp.zeros((near, chans), BF16)
    pad = jnp.zeros((ext.shape[1] - cols - near, chans), BF16)
    for r in range(rows):
        ext[r] = jnp.concatenate([blank, fields[r], pad], axis=0)
    groups = [(i, k) for k in range(basis) for i in range(rows)]
    inner = cols - 2 * BLOCK
    for at in range(BLOCK, cols - BLOCK, BLOCK):
        window_products(
            own_weights, ext[:, at : at + SPAN, :], hidden, groups, inner, at - BLOCK, chans
        )
    half = rows // 2
    for n in range(2):
        at = slice(n * half, (n + 1) * half)
        total = matmul(hidden[n * half * inner : (n + 1) * half * inner], mix[...])
        acc[at, BLOCK : cols - BLOCK, :] = total.reshape(half, inner, chans) + fields[
            at, BLOCK : cols - BLOCK, :
        ].astype(F32)


def partner_kernel(
    acc_in, own_weights, polar_weights, turned, fields, mix, edges, polar_left, polar_right,
    acc, hidden, cycle_rows, mixed_rows,
):
    del acc_in
    rows, cols, chans = fields.shape
    polar = turned.shape[0]
    basis = mix.shape[0] // chans
    reach = (SPAN - BLOCK) // 4
    lat_pos = lax.axis_index("lat")
    at_top = lat_pos == 0
    at_bottom = lat_pos == lax.axis_size("lat") - 1
    groups = [(i, k) for k in range(basis) for i in range(rows)]
    left, right = [], []
    pad = jnp.zeros((SPAN - BLOCK - 2 * reach, chans), BF16)
    for r in range(rows):
        left.append(
            jnp.concatenate([edges[r, reach:], fields[r, : SPAN - reach]], axis=0)
        )
        right.append(
            jnp.concatenate(
                [fields[r, cols - BLOCK - reach :], edges[r, :reach], pad], axis=0
            )
        )
    for n, cells in enumerate((left, right)):
        window_products(
            own_weights, jnp.concatenate(cells, axis=0), hidden, groups, 2 * BLOCK, n * BLOCK,
            chans,
        )
    total = matmul(hidden[...], mix[...]).reshape(rows, 2 * BLOCK, chans)
    for n, at in enumerate((slice(0, BLOCK), slice(cols - BLOCK, cols))):
        acc[:, at, :] = total[:, n * BLOCK : (n + 1) * BLOCK] + fields[:, at, :].astype(F32)

    @pl.when(at_top | at_bottom)
    def polar_part():
        offset = jnp.where(at_top, 0, rows - polar)
        for p in range(polar):
            whole = jnp.concatenate(
                [fields[offset + p], polar_left[p], polar_right[p]], axis=0
            )
            part = matmul(turned[p], whole).astype(BF16)
            for k in range(basis):
                cycle_rows[k, p * cols : (p + 1) * cols, :] = part[k * cols : (k + 1) * cols]
        for k in range(basis):
            part = matmul(cycle_rows[k], mix[k * chans : (k + 1) * chans, :]).astype(BF16)
            mixed_rows[k * polar : (k + 1) * polar] = part.reshape(polar, cols, chans)
        for b in range(cols // BLOCK):
            at = slice(BLOCK * b, BLOCK * (b + 1))
            cells = mixed_rows[:, at, :].reshape(-1, chans)
            acc[:, at, :] = acc[:, at, :] + matmul(polar_weights[...], cells).reshape(
                rows, BLOCK, chans
            )


def side_rows(
    side, halo, weights, acc, mix, ext, hidden, present, result, ready=lambda at: None
):
    half, cols, chans = result.shape
    basis = mix.shape[0] // chans
    rows = pl.ds(side * half, half)
    wide = cols // 2
    parts = [slice(n * wide, (n + 1) * wide) for n in range(2)]

    @pl.when(present)
    def arrived():
        window = halo()
        groups = [(i, k) for k in range(basis) for i in range(half)]
        for n, part in enumerate(parts):
            for at in range(0, wide, BLOCK):
                cells = window(part.start + at)
                window_products(
                    weights.at[side], cells, hidden.at[n], groups, wide, at, chans
                )
        for n, part in enumerate(parts):
            total = matmul(hidden[n], mix[...]).reshape(half, wide, chans)
            result[:, part, :] = (total + acc[rows, part, :]).astype(BF16)
            ready(part)

    @pl.when(jnp.logical_not(present))
    def absent():
        for part in parts:
            result[:, part, :] = acc[rows, part, :].astype(BF16)
            ready(part)


def from_side(which):
    core = lax.axis_index("lon")
    side = 1 - core if which == 0 else core
    lat_pos = lax.axis_index("lat")
    last = lax.axis_size("lat") - 1
    present = jnp.where(side == 0, lat_pos != 0, lat_pos != last)
    return side, present


def early_kernel(halo, edges, weights, acc, mix, result, ext, hidden):
    side, present = from_side(0)
    reach = edges.shape[1] // 2

    def windows():
        cols, chans = halo.shape[1:]
        pad = jnp.zeros((ext.shape[1] - cols - 2 * reach, chans), BF16)
        for p in range(HALO):
            edge = edges[p]
            ext[p] = jnp.concatenate([edge[reach:], halo[p], edge[:reach], pad], axis=0)
        return lambda start: ext[:, start : start + SPAN, :]

    side_rows(side, windows, weights, acc, mix, ext, hidden, present, result)


def late_kernel(early, halo, weights, acc, mix, out, ext, hidden, result, sems):
    half, cols, _ = result.shape
    side, present = from_side(1)
    rows = pl.ds(side * half, half)
    other_rows = pl.ds((1 - side) * half, half)

    def windows():
        def window(start):
            here = min(SPAN, halo.shape[1] - start)
            cells = halo[:, start : start + here, :]
            if here == SPAN:
                return cells
            pad = jnp.zeros((HALO, SPAN - here, halo.shape[2]), BF16)
            return jnp.concatenate([cells, pad], axis=1)

        return window

    def copy_of(part):
        n = 0 if part.start == 0 else 1
        return pltpu.make_async_copy(
            result.at[:, part, :], out.at[rows, part, :], sems.at[n]
        )

    first = pltpu.make_async_copy(early, out.at[other_rows], sems.at[2])
    first.start()
    side_rows(
        side, windows, weights, acc, mix, ext, hidden, present, result,
        lambda part: copy_of(part).start(),
    )
    first.wait()
    for n in range(2):
        copy_of(slice(n * cols // 2, (n + 1) * cols // 2)).wait()


def shards(fields, lon_taps, lat_taps, cycle_taps, band_start, band_width, mixing):
    rows, cols, chans = fields.shape
    row_total, basis, taps = lon_taps.shape
    band = lat_taps.shape[2]
    reach = (taps - 1) // 2
    polar = cycle_taps.shape[1] // 2
    cycle = cycle_taps.shape[2]
    lat_count = lax.axis_size("lat")
    core = lax.axis_index("lon")
    axes = ("lat", "lon")
    assert cycle == 2 * cols and rows == 2 * HALO and basis * polar * BLOCK == rows * SPAN
    assert reach == (SPAN - BLOCK) // 4 and polar == HALO
    ahead, back = ring(lat_count, 1), ring(lat_count, -1)
    head, tail = fields[:HALO], fields[rows - HALO :]
    going = jnp.where(core == 0, head, tail)
    staying = jnp.where(core == 0, tail, head)
    second = lax.ppermute(going, axes, back)
    going, staying, band_start = lax.optimization_barrier((going, staying, band_start))

    vmem = pl.BlockSpec(memory_space=pltpu.VMEM)
    hbm = pl.BlockSpec(memory_space=pltpu.HBM)
    sds = jax.ShapeDtypeStruct
    group = basis * rows * BLOCK
    ext_cols = cols + SPAN - BLOCK
    limit = pltpu.CompilerParams(vmem_limit_bytes=32 * 1024 * 1024)
    small = pl.CostEstimate(flops=100_000, bytes_accessed=1_000, transcendentals=0)
    large = pl.CostEstimate(flops=1_600_000_000, bytes_accessed=1_000, transcendentals=0)
    weight_shapes = (
        sds((2, group // 2, HALO * SPAN), BF16),
        sds((group, rows * SPAN), BF16),
        sds((rows * BLOCK, rows * SPAN), BF16),
        sds((basis, 2 * polar, cycle), BF16),
        sds((basis * chans, chans), BF16),
        sds((polar, basis * cols, cycle), BF16),
    )

    operands = [
        pltpu.with_memory_space_constraint(x, pltpu.HBM)
        for x in (
            band_start, band_width, jnp.transpose(lon_taps, (2, 1, 0)),
            jnp.transpose(lat_taps, (2, 1, 0)), cycle_taps,
            mixing.reshape(basis * chans, chans),
        )
    ]
    weight_scratch = [
        pltpu.SMEM((rows,), jnp.int32),
        pltpu.SMEM((rows,), jnp.int32),
        pltpu.VMEM((taps, basis, row_total), F32),
        pltpu.VMEM((band, basis, rows), BF16),
        pltpu.VMEM((128, -(-row_total // 128) * 128), F32),
        pltpu.VMEM((128, 128), F32),
        pltpu.SemaphoreType.DMA((6,)),
    ]
    whole, edges, polar_left, polar_right, *made = pl.pallas_call(
        stage_kernel,
        out_shape=(
            sds((rows, cols, chans), BF16),
            sds((rows, 2 * reach, chans), BF16),
            sds((polar, cols // 2, chans), BF16),
            sds((polar, cols // 2, chans), BF16),
            *weight_shapes,
        ),
        in_specs=[hbm] * 6 + [vmem] * 2,
        out_specs=[vmem] * 10,
        scratch_shapes=weight_scratch,
        compiler_params=limit,
        cost_estimate=small,
        name="stage_rows",
    )(*operands, going, staying)
    edges = lax.ppermute(edges, "lon", SWAP)
    polar_left = lax.ppermute(polar_left, "lon", SWAP)
    polar_right = lax.ppermute(polar_right, "lon", SWAP)
    message, corners = pl.pallas_call(
        pack_kernel,
        out_shape=(
            sds((HALO, cols + 2 * reach, chans), BF16),
            sds((HALO, 2 * reach, chans), BF16),
        ),
        in_specs=[vmem] * 2,
        out_specs=(vmem, vmem),
        compiler_params=limit,
        cost_estimate=small,
        name="pack_messages",
    )(whole, edges)
    first = lax.ppermute(message, axes, ahead)
    second_edges = lax.ppermute(corners, axes, back)
    corners, made = lax.optimization_barrier((corners, made))
    halo_weights, own_weights, polar_weights, turns, mix, turned = pl.pallas_call(
        functools.partial(weight_kernel, True),
        out_shape=weight_shapes,
        in_specs=[hbm] * 6 + [vmem] * 6,
        out_specs=[vmem] * 6,
        input_output_aliases={6 + n: n for n in range(6)},
        scratch_shapes=weight_scratch,
        compiler_params=limit,
        cost_estimate=small,
        name="filter_weights",
    )(*operands, *made)
    acc, turned = pl.pallas_call(
        own_kernel,
        out_shape=(
            sds((rows, cols, chans), F32),
            sds((polar, basis * cols, cycle), BF16),
        ),
        in_specs=[vmem] * 5,
        out_specs=(vmem, vmem),
        input_output_aliases={0: 1},
        scratch_shapes=[
            pltpu.VMEM((rows, ext_cols, chans), BF16),
            pltpu.VMEM((rows * (cols - 2 * BLOCK), basis * chans), BF16),
        ],
        compiler_params=limit,
        cost_estimate=pl.CostEstimate(
            flops=100_000, bytes_accessed=1_000, transcendentals=0
        ),
        name="own_rows",
    )(turned, own_weights, turns, whole, mix)

    acc = pl.pallas_call(
        partner_kernel,
        out_shape=sds((rows, cols, chans), F32),
        in_specs=[vmem] * 9,
        out_specs=vmem,
        input_output_aliases={0: 0},
        scratch_shapes=[
            pltpu.VMEM((rows * 2 * BLOCK, basis * chans), BF16),
            pltpu.VMEM((basis, polar * cols, chans), BF16),
            pltpu.VMEM((basis * polar, cols, chans), BF16),
        ],
        compiler_params=limit,
        cost_estimate=pl.CostEstimate(
            flops=100_000, bytes_accessed=1_000, transcendentals=0
        ),
        name="partner_columns",
    )(acc, own_weights, polar_weights, turned, whole, mix, edges, polar_left, polar_right)

    half = rows // 2
    scratch = [
        pltpu.VMEM((HALO, ext_cols, chans), BF16),
        pltpu.VMEM((2, half * cols // 2, basis * chans), BF16),
    ]
    limit = pltpu.CompilerParams(vmem_limit_bytes=32 * 1024 * 1024)
    second, second_edges, acc = lax.optimization_barrier((second, second_edges, acc))
    early = pl.pallas_call(
        early_kernel,
        out_shape=sds((half, cols, chans), BF16),
        in_specs=[vmem] * 5,
        out_specs=vmem,
        scratch_shapes=scratch,
        compiler_params=limit,
        cost_estimate=large,
        name="early_side",
    )(second, second_edges, halo_weights, acc, mix)
    first, early = lax.optimization_barrier((first, early))
    return pl.pallas_call(
        late_kernel,
        out_shape=sds((rows, cols, chans), BF16),
        in_specs=[vmem] * 5,
        out_specs=hbm,
        scratch_shapes=[
            *scratch,
            pltpu.VMEM((half, cols, chans), BF16),
            pltpu.SemaphoreType.DMA((3,)),
        ],
        compiler_params=limit,
        name="late_side",
    )(early, first, halo_weights, acc, mix)


def solution(mesh):
    in_specs = (
        P(("ens", "lat"), "lon", None),
        P(),
        P("lat", None, None),
        P(),
        P("lat"),
        P("lat"),
        P(),
    )
    out_specs = P(("ens", "lat"), "lon", None)
    return jax.shard_map(shards, mesh=mesh, in_specs=in_specs, out_specs=out_specs, check_vma=False)
```

```python
import functools

import jax
import jax.numpy as jnp
from jax import lax
from jax.experimental import pallas as pl
from jax.experimental.pallas import tpu as pltpu
from jax.sharding import PartitionSpec as P

HALO = 4
BLOCK = 16
SPAN = 32
SWAP = [(0, 1), (1, 0)]
F32, BF16 = jnp.float32, jnp.bfloat16


def ring(lat_count, step):
    pairs = []
    for lat in range(lat_count):
        for core in range(2):
            to = lat + (step if core == 0 else -step)
            if 0 <= to < lat_count:
                pairs.append((lat * 2 + core, to * 2 + core))
            else:
                pairs.append((lat * 2 + core, lat * 2 + 1 - core))
    return pairs


def matmul(a, b):
    return jnp.dot(a, b, preferred_element_type=F32)


def staircase(line, steps):
    wide = jnp.broadcast_to(line, (steps, line.shape[1]))
    return pltpu.roll(wide, 0, 1, stride=1, stride_axis=0).astype(BF16)


def chosen(terms):
    total = None
    for mask, value in terms:
        term = jnp.where(mask, value, 0.0)
        total = term if total is None else total + term
    return total


def window_products(weights, cells, hidden, groups, width, offset, chans):
    part = matmul(weights[...], cells.reshape(-1, chans)).astype(BF16)
    for n, (i, k) in enumerate(groups):
        at = i * width + offset
        hidden[at : at + BLOCK, k * chans : (k + 1) * chans] = part[n * BLOCK : (n + 1) * BLOCK]


def polar_matrices(cycle_taps, turned, at_top):
    basis, twice, cycle = cycle_taps.shape
    polar = twice // 2
    cols = turned.shape[1] // basis
    total = lax.broadcasted_iota(jnp.int32, (cycle, cycle), 0) + lax.broadcasted_iota(
        jnp.int32, (cycle, cycle), 1
    )
    turn = jnp.where((total == 0) | (total == cycle), 1.0, 0.0).astype(BF16)
    negated = matmul(cycle_taps[...].reshape(-1, cycle), turn)
    for p in range(polar):
        for k in range(basis):
            n = k * twice + (p if at_top else p + polar)
            turned[p, k * cols : (k + 1) * cols, :] = staircase(negated[n : n + 1], cols)


def weight_kernel(
    late, start_in, width_in, lon_in, lat_in, cycle_in, mixing_in, *refs,
):
    if late:
        refs = refs[6:]
    halo_weights, own_weights, polar_weights, cycle_taps, mix, turned = refs[:6]
    start, width, lon, lat, lon_wide, lat_wide, sems = refs[6:]
    rows = halo_weights.shape[0] * HALO
    taps, basis, row_total = lon.shape
    band = lat.shape[0]
    polar = cycle_taps.shape[1] // 2
    lat_pos = lax.axis_index("lat")
    base = lat_pos * rows
    at_top = base == 0

    is_early = at_top & (lax.axis_index("lon") == 0) & (lax.axis_index("ens") == 0)

    @pl.when(jnp.logical_not(is_early) if late else is_early)
    def make():
        copies = []
        for n, (source, target) in enumerate(
            [
                (lon_in, lon), (lat_in, lat), (start_in, start), (width_in, width),
                (cycle_in, cycle_taps), (mixing_in, mix),
            ]
        ):
            copies.append(pltpu.make_async_copy(source, target, sems.at[n]))
            copies[-1].start()
        lon_wide[...] = jnp.zeros_like(lon_wide)
        lat_wide[...] = jnp.zeros_like(lat_wide)
        for n in range(4):
            copies[n].wait()

        for d in range(taps):
            for k in range(basis):
                lon_wide[k * 16 + d : k * 16 + d + 1, 0:row_total] = lon[d, k : k + 1, :]
        lanes = lon_wide.shape[1]
        slots = pltpu.roll(lon_wide[...], lax.rem(lanes + HALO - base, lanes), 1)[:, :128]
        slots = jnp.transpose(slots)[: rows + 2 * HALO]
        is_tap = lax.broadcasted_iota(jnp.int32, slots.shape, 1) < taps
        own_taps, halo_taps = [], []
        for k in range(basis):
            moved = slots if k == 0 else pltpu.roll(slots, 128 - 16 * k, 1)
            moved = jnp.where(is_tap, moved, 0.0)
            for _ in range(2):
                moved = pltpu.roll(moved, 0, 1, stride=SPAN // 2, stride_axis=0)
            quads = [jnp.sum(moved[4 * q : 4 * q + 4], axis=0, keepdims=True) for q in range(4)]
            own_taps.append(jnp.concatenate([quads[1], quads[2]], axis=1))
            halo_taps.append(jnp.concatenate([quads[0], quads[3]], axis=1))

        for t in range(band):
            lat_wide[t * basis : (t + 1) * basis, 0:rows] = lat[t].astype(F32)
        lat_cols = jnp.transpose(lat_wide[...])[:rows]
        shape = (rows, rows * SPAN)
        lane = lax.broadcasted_iota(jnp.int32, shape, 1)
        out_row = lax.broadcasted_iota(jnp.int32, shape, 0)
        first = jnp.zeros(shape, jnp.int32)
        count = jnp.zeros(shape, jnp.int32)
        for i in range(rows):
            first = jnp.where(out_row == i, start[i], first)
            count = jnp.where(out_row == i, width[i], count)
        spread = [
            [
                jnp.broadcast_to(lat_cols[:, t * basis + k : t * basis + k + 1], shape)
                for k in range(basis)
            ]
            for t in range(band)
        ]
        slot = lane // SPAN
        own_row = base + slot
        halo_row = jnp.where(slot < HALO, own_row - HALO, own_row + rows - HALO)
        is_polar = (own_row < polar) | (own_row >= row_total - polar)
        in_grid = (halo_row >= 0) & (halo_row < row_total)
        own_step, halo_step = own_row - first, halo_row - first
        own_used = [(own_step == t) & (count > t) & ~is_polar for t in range(band)]
        halo_used = [(halo_step == t) & (count > t) & in_grid for t in range(band)]
        for k in range(basis):
            own_line = own_taps[k] * chosen([(own_used[t], spread[t][k]) for t in range(band)])
            halo_line = halo_taps[k] * chosen([(halo_used[t], spread[t][k]) for t in range(band)])
            for i in range(rows):
                at = (k * rows + i) * BLOCK
                own_weights[at : at + BLOCK, :] = staircase(own_line[i : i + 1], BLOCK)
                side, at = i // HALO, (k * HALO + i % HALO) * BLOCK
                reached = halo_line[i : i + 1, side * HALO * SPAN : (side + 1) * HALO * SPAN]
                halo_weights[side, at : at + BLOCK, :] = staircase(reached, BLOCK)

        offset = jnp.where(at_top, 0, rows - polar)
        of_basis = lane // (polar * BLOCK)
        step = base + offset + lax.rem(lane // BLOCK, polar) - first
        at_start = lax.rem(lane, BLOCK) == 0
        terms = []
        for t in range(band):
            value = spread[t][0]
            for k in range(1, basis):
                value = jnp.where(of_basis == k, spread[t][k], value)
            terms.append(((step == t) & (count > t) & at_start, value))
        line = chosen(terms)
        for i in range(rows):
            polar_weights[i * BLOCK : (i + 1) * BLOCK, :] = staircase(line[i : i + 1], BLOCK)
        copies[4].wait()

        copies[5].wait()


def edge_kernel(
    start_in, width_in, lon_in, lat_in, cycle_in, mixing_in, going, staying, edges, *refs,
):
    weight_kernel(False, start_in, width_in, lon_in, lat_in, cycle_in, mixing_in, *refs)
    cols = going.shape[1]
    reach = edges.shape[1] // 2
    is_first = lax.axis_index("lon") == 0
    for p in range(HALO):
        for r, first, second in ((p, going, staying), (HALO + p, staying, going)):
            for n, at in enumerate((slice(0, reach), slice(cols - reach, cols))):
                edges[r, n * reach : (n + 1) * reach, :] = jnp.where(
                    is_first, first[p, at, :], second[p, at, :]
                )


def stage_kernel(going, staying, whole, polar_left, polar_right):
    cols = whole.shape[1]
    is_first = lax.axis_index("lon") == 0
    at_top = lax.axis_index("lat") == 0
    for p in range(HALO):
        upper = jnp.where(is_first, going[p], staying[p])
        lower = jnp.where(is_first, staying[p], going[p])
        polar = jnp.where(at_top, upper, lower)
        polar_left[p], polar_right[p] = polar[: cols // 2], polar[cols // 2 :]
        whole[p], whole[HALO + p] = upper, lower


def pack_kernel(whole, edges, message, corners):
    rows = whole.shape[0]
    reach = edges.shape[1] // 2
    start = jnp.where(lax.axis_index("lon") == 0, rows - HALO, 0)
    early = rows - HALO - start
    for p in range(HALO):
        near = edges[start + p]
        message[p] = jnp.concatenate([near[reach:], whole[start + p], near[:reach]], axis=0)
        corners[p] = edges[early + p]


def own_kernel(turned_in, own_weights, cycle_taps, fields, mix, acc, turned, ext, hidden):
    del turned_in
    rows, cols, chans = fields.shape
    basis = mix.shape[0] // chans
    near = (SPAN - BLOCK) // 4

    lat_pos = lax.axis_index("lat")

    @pl.when(lat_pos == 0)
    def top():
        polar_matrices(cycle_taps, turned, True)

    @pl.when(lat_pos == lax.axis_size("lat") - 1)
    def bottom():
        polar_matrices(cycle_taps, turned, False)

    blank = jnp.zeros((near, chans), BF16)
    pad = jnp.zeros((ext.shape[1] - cols - near, chans), BF16)
    for r in range(rows):
        ext[r] = jnp.concatenate([blank, fields[r], pad], axis=0)
    groups = [(i, k) for k in range(basis) for i in range(rows)]
    inner = cols - 2 * BLOCK
    for at in range(BLOCK, cols - BLOCK, BLOCK):
        window_products(
            own_weights, ext[:, at : at + SPAN, :], hidden, groups, inner, at - BLOCK, chans
        )
    half = rows // 2
    for n in range(2):
        at = slice(n * half, (n + 1) * half)
        total = matmul(hidden[n * half * inner : (n + 1) * half * inner], mix[...])
        acc[at, BLOCK : cols - BLOCK, :] = total.reshape(half, inner, chans) + fields[
            at, BLOCK : cols - BLOCK, :
        ].astype(F32)


def partner_kernel(
    acc_in, own_weights, polar_weights, turned, fields, mix, edges, polar_left, polar_right,
    acc, hidden, cycle_rows, mixed_rows,
):
    del acc_in
    rows, cols, chans = fields.shape
    polar = turned.shape[0]
    basis = mix.shape[0] // chans
    reach = (SPAN - BLOCK) // 4
    lat_pos = lax.axis_index("lat")
    at_top = lat_pos == 0
    at_bottom = lat_pos == lax.axis_size("lat") - 1
    groups = [(i, k) for k in range(basis) for i in range(rows)]
    left, right = [], []
    pad = jnp.zeros((SPAN - BLOCK - 2 * reach, chans), BF16)
    for r in range(rows):
        left.append(
            jnp.concatenate([edges[r, reach:], fields[r, : SPAN - reach]], axis=0)
        )
        right.append(
            jnp.concatenate(
                [fields[r, cols - BLOCK - reach :], edges[r, :reach], pad], axis=0
            )
        )
    for n, cells in enumerate((left, right)):
        window_products(
            own_weights, jnp.concatenate(cells, axis=0), hidden, groups, 2 * BLOCK, n * BLOCK,
            chans,
        )
    total = matmul(hidden[...], mix[...]).reshape(rows, 2 * BLOCK, chans)
    for n, at in enumerate((slice(0, BLOCK), slice(cols - BLOCK, cols))):
        acc[:, at, :] = total[:, n * BLOCK : (n + 1) * BLOCK] + fields[:, at, :].astype(F32)

    @pl.when(at_top | at_bottom)
    def polar_part():
        offset = jnp.where(at_top, 0, rows - polar)
        for p in range(polar):
            whole = jnp.concatenate(
                [fields[offset + p], polar_left[p], polar_right[p]], axis=0
            )
            part = matmul(turned[p], whole).astype(BF16)
            for k in range(basis):
                cycle_rows[k, p * cols : (p + 1) * cols, :] = part[k * cols : (k + 1) * cols]
        for k in range(basis):
            part = matmul(cycle_rows[k], mix[k * chans : (k + 1) * chans, :]).astype(BF16)
            mixed_rows[k * polar : (k + 1) * polar] = part.reshape(polar, cols, chans)
        for b in range(cols // BLOCK):
            at = slice(BLOCK * b, BLOCK * (b + 1))
            cells = mixed_rows[:, at, :].reshape(-1, chans)
            acc[:, at, :] = acc[:, at, :] + matmul(polar_weights[...], cells).reshape(
                rows, BLOCK, chans
            )


def side_rows(
    side, halo, weights, acc, mix, ext, hidden, present, result, ready=lambda at: None
):
    half, cols, chans = result.shape
    basis = mix.shape[0] // chans
    rows = pl.ds(side * half, half)
    wide = cols // 2
    parts = [slice(n * wide, (n + 1) * wide) for n in range(2)]

    @pl.when(present)
    def arrived():
        for p in range(HALO):
            cells = halo(p)
            pad = jnp.zeros((ext.shape[1] - cells.shape[0], chans), BF16)
            ext[p] = jnp.concatenate([cells, pad], axis=0)
        groups = [(i, k) for k in range(basis) for i in range(half)]
        for n, part in enumerate(parts):
            for at in range(0, wide, BLOCK):
                cells = ext[:, part.start + at : part.start + at + SPAN, :]
                window_products(
                    weights.at[side], cells, hidden.at[n], groups, wide, at, chans
                )
        for n, part in enumerate(parts):
            total = matmul(hidden[n], mix[...]).reshape(half, wide, chans)
            result[:, part, :] = (total + acc[rows, part, :]).astype(BF16)
            ready(part)

    @pl.when(jnp.logical_not(present))
    def absent():
        for part in parts:
            result[:, part, :] = acc[rows, part, :].astype(BF16)
            ready(part)


def from_side(which):
    core = lax.axis_index("lon")
    side = 1 - core if which == 0 else core
    lat_pos = lax.axis_index("lat")
    last = lax.axis_size("lat") - 1
    present = jnp.where(side == 0, lat_pos != 0, lat_pos != last)
    return side, present


def early_kernel(halo, edges, weights, acc, mix, result, ext, hidden):
    side, present = from_side(0)
    reach = edges.shape[1] // 2

    def cells(p):
        edge = edges[p]
        return jnp.concatenate([edge[reach:], halo[p], edge[:reach]], axis=0)

    side_rows(side, cells, weights, acc, mix, ext, hidden, present, result)


def late_kernel(early, halo, weights, acc, mix, out, ext, hidden, result, sems):
    half, cols, _ = result.shape
    side, present = from_side(1)
    rows = pl.ds(side * half, half)
    other_rows = pl.ds((1 - side) * half, half)

    def copy_of(part):
        n = 0 if part.start == 0 else 1
        return pltpu.make_async_copy(
            result.at[:, part, :], out.at[rows, part, :], sems.at[n]
        )

    first = pltpu.make_async_copy(early, out.at[other_rows], sems.at[2])
    first.start()
    side_rows(
        side, lambda p: halo[p], weights, acc, mix, ext, hidden, present, result,
        lambda part: copy_of(part).start(),
    )
    first.wait()
    for n in range(2):
        copy_of(slice(n * cols // 2, (n + 1) * cols // 2)).wait()


def shards(fields, lon_taps, lat_taps, cycle_taps, band_start, band_width, mixing):
    rows, cols, chans = fields.shape
    row_total, basis, taps = lon_taps.shape
    band = lat_taps.shape[2]
    reach = (taps - 1) // 2
    polar = cycle_taps.shape[1] // 2
    cycle = cycle_taps.shape[2]
    lat_count = lax.axis_size("lat")
    core = lax.axis_index("lon")
    axes = ("lat", "lon")
    assert cycle == 2 * cols and rows == 2 * HALO and basis * polar * BLOCK == rows * SPAN
    assert reach == (SPAN - BLOCK) // 4 and polar == HALO
    ahead, back = ring(lat_count, 1), ring(lat_count, -1)
    head, tail = fields[:HALO], fields[rows - HALO :]
    going = jnp.where(core == 0, head, tail)
    staying = jnp.where(core == 0, tail, head)
    second = lax.ppermute(going, axes, back)
    going, staying, band_start = lax.optimization_barrier((going, staying, band_start))

    vmem = pl.BlockSpec(memory_space=pltpu.VMEM)
    hbm = pl.BlockSpec(memory_space=pltpu.HBM)
    sds = jax.ShapeDtypeStruct
    group = basis * rows * BLOCK
    ext_cols = cols + SPAN - BLOCK
    limit = pltpu.CompilerParams(vmem_limit_bytes=32 * 1024 * 1024)
    small = pl.CostEstimate(flops=100_000, bytes_accessed=1_000, transcendentals=0)
    large = pl.CostEstimate(flops=1_600_000_000, bytes_accessed=1_000, transcendentals=0)
    weight_shapes = (
        sds((2, group // 2, HALO * SPAN), BF16),
        sds((group, rows * SPAN), BF16),
        sds((rows * BLOCK, rows * SPAN), BF16),
        sds((basis, 2 * polar, cycle), BF16),
        sds((basis * chans, chans), BF16),
        sds((polar, basis * cols, cycle), BF16),
    )

    operands = [
        pltpu.with_memory_space_constraint(x, pltpu.HBM)
        for x in (
            band_start, band_width, jnp.transpose(lon_taps, (2, 1, 0)),
            jnp.transpose(lat_taps, (2, 1, 0)), cycle_taps,
            mixing.reshape(basis * chans, chans),
        )
    ]
    weight_scratch = [
        pltpu.SMEM((rows,), jnp.int32),
        pltpu.SMEM((rows,), jnp.int32),
        pltpu.VMEM((taps, basis, row_total), F32),
        pltpu.VMEM((band, basis, rows), BF16),
        pltpu.VMEM((128, -(-row_total // 128) * 128), F32),
        pltpu.VMEM((128, 128), F32),
        pltpu.SemaphoreType.DMA((6,)),
    ]
    edges, *made = pl.pallas_call(
        edge_kernel,
        out_shape=(sds((rows, 2 * reach, chans), BF16), *weight_shapes),
        in_specs=[hbm] * 6 + [vmem] * 2,
        out_specs=[vmem] * 7,
        scratch_shapes=weight_scratch,
        compiler_params=limit,
        cost_estimate=small,
        name="stage_edges",
    )(*operands, going, staying)
    going, staying, edges = lax.optimization_barrier((going, staying, edges))
    whole, polar_left, polar_right = pl.pallas_call(
        stage_kernel,
        out_shape=(
            sds((rows, cols, chans), BF16),
            sds((polar, cols // 2, chans), BF16),
            sds((polar, cols // 2, chans), BF16),
        ),
        in_specs=[vmem] * 2,
        out_specs=[vmem] * 3,
        compiler_params=limit,
        cost_estimate=small,
        name="stage_rows",
    )(going, staying)
    edges = lax.ppermute(edges, "lon", SWAP)
    polar_left = lax.ppermute(polar_left, "lon", SWAP)
    polar_right = lax.ppermute(polar_right, "lon", SWAP)
    message, corners = pl.pallas_call(
        pack_kernel,
        out_shape=(
            sds((HALO, cols + 2 * reach, chans), BF16),
            sds((HALO, 2 * reach, chans), BF16),
        ),
        in_specs=[vmem] * 2,
        out_specs=(vmem, vmem),
        compiler_params=limit,
        cost_estimate=small,
        name="pack_messages",
    )(whole, edges)
    first = lax.ppermute(message, axes, ahead)
    second_edges = lax.ppermute(corners, axes, back)
    corners, made = lax.optimization_barrier((corners, made))
    halo_weights, own_weights, polar_weights, turns, mix, turned = pl.pallas_call(
        functools.partial(weight_kernel, True),
        out_shape=weight_shapes,
        in_specs=[hbm] * 6 + [vmem] * 6,
        out_specs=[vmem] * 6,
        input_output_aliases={6 + n: n for n in range(6)},
        scratch_shapes=weight_scratch,
        compiler_params=limit,
        cost_estimate=small,
        name="filter_weights",
    )(*operands, *made)
    acc, turned = pl.pallas_call(
        own_kernel,
        out_shape=(
            sds((rows, cols, chans), F32),
            sds((polar, basis * cols, cycle), BF16),
        ),
        in_specs=[vmem] * 5,
        out_specs=(vmem, vmem),
        input_output_aliases={0: 1},
        scratch_shapes=[
            pltpu.VMEM((rows, ext_cols, chans), BF16),
            pltpu.VMEM((rows * (cols - 2 * BLOCK), basis * chans), BF16),
        ],
        compiler_params=limit,
        cost_estimate=pl.CostEstimate(
            flops=100_000, bytes_accessed=1_000, transcendentals=0
        ),
        name="own_rows",
    )(turned, own_weights, turns, whole, mix)

    acc = pl.pallas_call(
        partner_kernel,
        out_shape=sds((rows, cols, chans), F32),
        in_specs=[vmem] * 9,
        out_specs=vmem,
        input_output_aliases={0: 0},
        scratch_shapes=[
            pltpu.VMEM((rows * 2 * BLOCK, basis * chans), BF16),
            pltpu.VMEM((basis, polar * cols, chans), BF16),
            pltpu.VMEM((basis * polar, cols, chans), BF16),
        ],
        compiler_params=limit,
        cost_estimate=pl.CostEstimate(
            flops=100_000, bytes_accessed=1_000, transcendentals=0
        ),
        name="partner_columns",
    )(acc, own_weights, polar_weights, turned, whole, mix, edges, polar_left, polar_right)

    half = rows // 2
    scratch = [
        pltpu.VMEM((HALO, ext_cols, chans), BF16),
        pltpu.VMEM((2, half * cols // 2, basis * chans), BF16),
    ]
    limit = pltpu.CompilerParams(vmem_limit_bytes=32 * 1024 * 1024)
    second, second_edges, acc = lax.optimization_barrier((second, second_edges, acc))
    early = pl.pallas_call(
        early_kernel,
        out_shape=sds((half, cols, chans), BF16),
        in_specs=[vmem] * 5,
        out_specs=vmem,
        scratch_shapes=scratch,
        compiler_params=limit,
        cost_estimate=large,
        name="early_side",
    )(second, second_edges, halo_weights, acc, mix)
    first, early = lax.optimization_barrier((first, early))
    return pl.pallas_call(
        late_kernel,
        out_shape=sds((rows, cols, chans), BF16),
        in_specs=[vmem] * 5,
        out_specs=hbm,
        scratch_shapes=[
            *scratch,
            pltpu.VMEM((half, cols, chans), BF16),
            pltpu.SemaphoreType.DMA((3,)),
        ],
        compiler_params=limit,
        name="late_side",
    )(early, first, halo_weights, acc, mix)


def solution(mesh):
    in_specs = (
        P(("ens", "lat"), "lon", None),
        P(),
        P("lat", None, None),
        P(),
        P("lat"),
        P("lat"),
        P(),
    )
    out_specs = P(("ens", "lat"), "lon", None)
    return jax.shard_map(shards, mesh=mesh, in_specs=in_specs, out_specs=out_specs, check_vma=False)
```
